32 devices in a mesh: dp: 8 (over z, x), fsdp: 4 (over y, core).
Axes of the slice: x: 2, y: 2, z: 4, core: 2. Of those that a mesh axis runs over, the one named last changes fastest.
Arguments:
- inputs: float32 [8192, 768], P(('dp', 'fsdp')), may hold values from -6 to 6
- lengths: int32 [32, 2], P(('dp', 'fsdp')), may hold values from 0 to 256, as said below
- in_projection: bfloat16 [2, 768, 2304], P(None, 'dp', 'fsdp'), may hold values from -0.21875 to 0.21875
- out_projection: bfloat16 [2, 768, 768], P(None, 'dp', 'fsdp'), may hold values from -0.21875 to 0.21875
- up_weight: bfloat16 [2, 768, 3072], P(None, 'dp', 'fsdp'), may hold values from -0.21875 to 0.21875
- down_weight: bfloat16 [2, 3072, 768], P(None, 'dp', 'fsdp'), may hold values from -0.109375 to 0.109375
- norm_gains: bfloat16 [2, 3, 768], P(None, None, 'dp'), may hold values from 0.5 to 1.5
- biases: bfloat16 [2, 7, 768], P(None, None, 'dp'), may hold values from -3 to 3
- hidden_gains: bfloat16 [2, 1, 3072], P(None, None, 'dp'), may hold values from 0.5 to 1.5
- hidden_biases: bfloat16 [2, 2, 3072], P(None, None, 'dp'), may hold values from -3 to 3
- cotangent: float32 [8192, 768], P(('dp', 'fsdp')), may hold values from -6 to 6
Outputs:
- outputs: float32 [8192, 768], P(('dp', 'fsdp'))
- input_gradient: float32 [8192, 768], P(('dp', 'fsdp'))
- in_projection_gradient: float32 [2, 768, 2304], P(None, 'dp', 'fsdp')
- out_projection_gradient: float32 [2, 768, 768], P(None, 'dp', 'fsdp')
- up_weight_gradient: float32 [2, 768, 3072], P(None, 'dp', 'fsdp')
- down_weight_gradient: float32 [2, 3072, 768], P(None, 'dp', 'fsdp')
- norm_gains_gradient: float32 [2, 3, 768], P(None, None, 'dp')
- biases_gradient: float32 [2, 7, 768], P(None, None, 'dp')
- hidden_gains_gradient: float32 [2, 1, 3072], P(None, None, 'dp')
- hidden_biases_gradient: float32 [2, 2, 3072], P(None, None, 'dp')
The draws below stay inside these ranges and needn't reach their ends.
Inputs may be any that keep to these rules, and one draw needn't show every extreme that they name: Row r lists the lengths of the 2 sequences packed in order from the first of device r's 256 token slots (devices in the order dp then fsdp); the slots after them are padding. A row sums to at most 256 and to at least 126. 0 marks an empty sequence slot; a nonempty sequence has 64 tokens or more; in every draw some device holds one sequence of 256 tokens.
All inputs are finite; a program needn't handle non-finite values.
Results may differ from the reference program's by a relative error of at most 0.018.
Values may be sent and summed in bfloat16 or wider, within the bound.
No kernel may reach another device: no remote copies, remote signals or barrier semaphores. Data moves between devices by JAX's collectives and lax.ppermute only.
A program may use at most 192 MiB of HBM per device.

```python
import math
import jax
import jax.numpy as jnp
from jax import lax

D = 768
HEADS = 12
HEAD_DIM = 64
FF = 3072
LAYERS = 2
TOK_DEV = 256
SEQS_DEV = 2
SHORTEST = 64
RANKS = 32
TOKENS = 8192


def draw_lengths(key, part):
    key = jax.random.fold_in(key, 11)
    key_weights, key_used, key_full = jax.random.split(key, 3)
    raw_draws = jax.random.randint(key_weights, (RANKS, SEQS_DEV), 1, 17)
    weights = raw_draws * raw_draws * raw_draws
    used_tokens = jax.random.randint(key_used, (RANKS, 1), TOK_DEV // 2, TOK_DEV + 1)
    spare_tokens = used_tokens - SHORTEST * SEQS_DEV
    shares = SHORTEST + spare_tokens * weights // jnp.sum(weights, axis=1, keepdims=True)
    chosen_rank = jax.random.randint(key_full, (), 0, RANKS)
    full_row = jnp.zeros((SEQS_DEV,), jnp.int32).at[0].set(TOK_DEV)
    rank_ids = jnp.arange(RANKS)
    return jnp.where((rank_ids == chosen_rank)[:, None], full_row[None, :], shares).astype(jnp.int32)


def strengthened(array, key, source, target, parts, factor):
    def block_of(dim):
        return (jnp.arange(array.shape[dim]) // (array.shape[dim] // parts)).reshape((-1,) + (1,) * (array.ndim - 1 - dim))

    near = jax.random.permutation(key, parts)[block_of(target)]
    other_side = (block_of(target) + parts // 2) % parts
    return jnp.where((block_of(source) == near) | (block_of(source) == other_side), factor * array, array)


def shard_levels(rng, shape, cuts, smallest, largest):
    def one(position, blocks):
        draws = jax.random.uniform(jax.random.fold_in(jax.random.fold_in(rng, 6), position), (blocks,), jnp.float32, smallest / len(cuts), largest / len(cuts))
        return jnp.repeat(jnp.exp(draws), shape[position] // blocks).reshape((-1,) + (1,) * (len(shape) - position - 1))

    factor_of = one(*cuts[0])
    for cut in cuts[1:]:
        factor_of = factor_of * one(*cut)
    return factor_of


def gaussian(rng, extent, deviation, bound, cuts=(), kind=jnp.bfloat16):
    entries = jax.random.normal(rng, extent, jnp.float32) * deviation
    if len(cuts) > 0:
        entries = shard_levels(rng, extent, cuts, -0.22, 0.18) * entries
    return jnp.clip(entries, min=-bound, max=bound).astype(kind)


def noise_with(own_key, extent, spread, reach, cuts, heavy, kind=jnp.bfloat16):
    entries = spread * jax.random.normal(own_key, extent, jnp.float32)
    if cuts:
        entries = entries * shard_levels(own_key, extent, cuts, -0.22, 0.18)
    return jnp.clip(strengthened(entries, jax.random.fold_in(own_key, 3), *heavy), -reach, reach).astype(kind)


def setup_inputs(seed: int = 0) -> dict:
    seeds = jax.random.split(jax.random.key(seed), 12)
    return {
        "inputs": gaussian(seeds[0], (TOKENS, D), 1.0, 6.0, ((0, 32),), jnp.float32),
        "lengths": draw_lengths(jax.random.fold_in(seeds[11], 71), 0),
        "in_projection": gaussian(seeds[2], (LAYERS, D, 3 * D), D ** -0.5, 0.21875, ((1, 8), (2, 4))),
        "out_projection": gaussian(seeds[3], (LAYERS, D, D), D ** -0.5, 0.21875, ((1, 8), (2, 4))),
        "up_weight": gaussian(seeds[4], (LAYERS, D, FF), D ** -0.5, 0.21875, ((1, 8), (2, 4))),
        "down_weight": gaussian(seeds[5], (LAYERS, FF, D), FF ** -0.5, 0.109375, ((1, 8), (2, 4))),
        "norm_gains": jnp.clip(0.5 + 1.0 * jax.random.uniform(seeds[6], (LAYERS, 3, D), jnp.float32) ** shard_levels(seeds[6], (LAYERS, 3, D), ((2, 8),), -0.2, 0.2), 0.5, 1.5).astype(jnp.bfloat16),
        "biases": gaussian(seeds[7], (LAYERS, 7, D), 0.5, 3.0, ((2, 8),)),
        "hidden_gains": jnp.clip(0.5 + 1.0 * jax.random.uniform(seeds[8], (LAYERS, 1, FF), jnp.float32) ** shard_levels(seeds[8], (LAYERS, 1, FF), ((2, 8),), -0.2, 0.2), 0.5, 1.5).astype(jnp.bfloat16),
        "hidden_biases": gaussian(seeds[9], (LAYERS, 2, FF), 0.5, 3.0, ((2, 8),)),
        "cotangent": noise_with(seeds[10], (TOKENS, D), 1.0, 6.0, ((0, 32),), (0, 1, 32, 2.75), jnp.float32),
    }


@jax.custom_vjp
def low(v):
    return lax.optimization_barrier(v.astype(jnp.bfloat16)).astype(jnp.float32)

@jax.custom_vjp
def low_back(v):
    return v

def low_keep(v):
    return (low(v), None)

def low_pass(kept, grad):
    return (grad,)

def back_keep(v):
    return (v, None)

def back_low(kept, grad):
    return (low(grad),)
low.defvjp(low_keep, low_pass)
low_back.defvjp(back_keep, back_low)
epsilon = 1e-05

def segments(lengths, count_rows):
    ends = jnp.cumsum(lengths, axis=-1)
    places = jnp.arange(count_rows, dtype=jnp.int32)
    return lax.optimization_barrier(jnp.sum((places[:, None] >= ends[0][None, :]).astype(jnp.int32), axis=1)).astype(jnp.int32)

def matmul(left, right):
    return jnp.dot(left, right, precision=lax.Precision.HIGHEST, preferred_element_type=jnp.float32)

def layer_norm(values, gain_row, shift_row):
    mean_value = lax.optimization_barrier(jnp.mean(values, axis=-1, keepdims=True))
    centred = values - mean_value
    variance = lax.optimization_barrier(jnp.mean(jnp.square(centred), axis=-1, keepdims=True))
    return centred * lax.rsqrt(variance + epsilon) * gain_row + shift_row

def gelu_value(values):
    return 0.5 * values * (1.0 + lax.erf(values * (1.0 / math.sqrt(2.0))))

def attend_device(operands):
    query_heads, key_heads, value_heads, segment_row = operands
    score_scale = 1.0 / math.sqrt(HEAD_DIM)
    scores = low_back(jnp.einsum('qhd,khd->hqk', query_heads, key_heads, precision=lax.Precision.HIGHEST) * score_scale)
    same_doc = segment_row[:, None] == segment_row[None, :]
    scores = jnp.where(same_doc[None], scores, -1e+30)
    row_max = lax.optimization_barrier(jnp.max(scores, axis=-1, keepdims=True))
    exponent = jnp.exp(scores - row_max)
    prob_rows = exponent / lax.optimization_barrier(jnp.sum(exponent, axis=-1, keepdims=True))
    return jnp.einsum('hqk,khd->qhd', low(prob_rows), value_heads, precision=lax.Precision.HIGHEST)

def attention(query_rows, key_rows, value_rows, segment_group):
    group_size = segment_group.shape[0]
    split_shape = (group_size, TOK_DEV, HEADS, HEAD_DIM)
    mixed_heads = lax.map(jax.checkpoint(attend_device), (query_rows.reshape(split_shape), key_rows.reshape(split_shape), value_rows.reshape(split_shape), segment_group))
    return mixed_heads.reshape(group_size * TOK_DEV, D)

def layer(stream, in_weight, out_weight, up_matrix, down_matrix, gain_rows, shift_rows, hidden_gain, hidden_shift, segment_group):
    attn_input = low(layer_norm(stream, gain_rows[0], shift_rows[0]))
    projected = matmul(attn_input, in_weight)
    query_rows = low_back(low(projected[:, 0:D] + shift_rows[1]))
    key_rows = low_back(low(projected[:, D:2 * D]))
    value_rows = low_back(low(projected[:, 2 * D:3 * D] + shift_rows[2]))
    attn_mixed = low_back(attention(query_rows, key_rows, value_rows, segment_group))
    mixed_input = low(layer_norm(attn_mixed, gain_rows[1], shift_rows[3]))
    middle = stream + low_back(matmul(mixed_input, out_weight) + shift_rows[4])
    ffn_input = low(layer_norm(middle, gain_rows[2], shift_rows[5]))
    hidden_pre = low_back(matmul(ffn_input, up_matrix) + hidden_shift[0])
    ffn_hidden = low(layer_norm(gelu_value(hidden_pre), hidden_gain[0], hidden_shift[1]))
    return middle + low_back(matmul(ffn_hidden, down_matrix) + shift_rows[6])

def forward(stream, weights, segment_group):
    for layer_index in range(LAYERS):
        stream = layer(stream, *[member[layer_index] for member in weights], segment_group)
    return stream

def reference(inputs, lengths, in_projection, out_projection, up_weight, down_weight, norm_gains, biases, hidden_gains, hidden_biases, cotangent):
    params = tuple((member.astype(jnp.float32) for member in (in_projection, out_projection, up_weight, down_weight, norm_gains, biases, hidden_gains, hidden_biases)))
    segment_ids = jax.vmap(lambda one_row: segments(one_row[None, :], TOK_DEV))(lengths)
    valid_rows = (segment_ids < SEQS_DEV).astype(jnp.float32)
    group_size = math.gcd(RANKS, max(1, 4096 // TOK_DEV))
    group_count = RANKS // group_size
    stream_groups = inputs.reshape(group_count, group_size * TOK_DEV, D)
    mask_groups = valid_rows.reshape(group_count, group_size * TOK_DEV, 1)
    cot_groups = cotangent.reshape(group_count, group_size * TOK_DEV, D) * mask_groups
    segment_groups = segment_ids.reshape(group_count, group_size, TOK_DEV)

    def group_step(totals, pieces):
        stream_group, cot_group, segment_group, mask_group = pieces

        def network(stream, *weights):
            return forward(stream, weights, segment_group)
        result, pullback = jax.vjp(network, stream_group, *params)
        gradients = pullback(cot_group)
        totals = jax.tree.map(jnp.add, totals, tuple(gradients[1:]))
        return (totals, (result * mask_group, gradients[0]))
    zero_grads = tuple((jnp.zeros(member.shape, jnp.float32) for member in params))
    totals, (outputs, input_gradient) = lax.scan(group_step, zero_grads, (stream_groups, cot_groups, segment_groups, mask_groups))
    return (outputs.reshape(TOKENS, D), input_gradient.reshape(TOKENS, D), totals[0], totals[1], totals[2], totals[3], totals[4], totals[5], totals[6], totals[7])
```

```python
import functools
import math

import jax
import jax.numpy as jnp
from jax import lax
from jax.experimental import pallas as pl
from jax.experimental.pallas import tpu as pltpu
from jax.sharding import PartitionSpec as P

HEADS = 12
HD = 64
LAYERS = 2
SEQS = 2
D = 768
FF = 3072
T = 256
EPS = 1e-05
BF = jnp.bfloat16
F32 = jnp.float32
MIB = 1 << 20

ANY = pl.BlockSpec(memory_space=pl.ANY)
SMEM = pl.BlockSpec(memory_space=pltpu.SMEM)
VMEM = pl.BlockSpec(memory_space=pltpu.VMEM)

G1, G2, G3, C1, BQ, BV, C2, BO, C3, B2 = range(10)
VROWS = 16
HROW = 10
G4, B1, C4 = 10, 11, 12

RB = 32


def dot(a, b):
    return jnp.dot(a, b, preferred_element_type=F32)


def dot_nt(a, b):
    return lax.dot_general(a, b, (((1,), (1,)), ((), ())), preferred_element_type=F32)


def unit_lane(u):
    f, j = divmod(u, 9)
    return 512 * f + 64 * j if j < 8 else 2048 + 128 * f


def ln_stats(v):
    m = jnp.mean(v, axis=-1, keepdims=True)
    cen = v - m
    inv = lax.rsqrt(jnp.mean(cen * cen, axis=-1, keepdims=True) + EPS)
    return cen * inv, inv


def ln_back(dn, g, n, inv):
    e = dn * g
    dv = inv * (e - jnp.mean(e, axis=-1, keepdims=True) - n * jnp.mean(e * n, axis=-1, keepdims=True))
    return dv, jnp.sum(dn * n, axis=0, keepdims=True), jnp.sum(dn, axis=0, keepdims=True)


def seg_of(scal, places):
    e0 = scal[0]
    e1 = scal[0] + scal[1]
    return (places >= e0).astype(jnp.int32) + (places >= e1).astype(jnp.int32)


class Plan:
    def __init__(self, fast):
        self.fast = fast

    def load_a(self, scal, pieces, m, dst):
        if not self.fast:
            return [(pieces[0], dst)]
        out = []
        for h, ri, x, f, ref in self._pieces(scal, pieces):
            src = ref.at[ri, :, pl.ds(m * 48, 48)]
            out.append((src.at[:, :, pl.ds(0, 512)], dst.at[:, x, h, :, pl.ds(pl.multiple_of(f * 512, 512), 512)]))
            out.append((src.at[:, :, pl.ds(512, 256)], dst.at[:, x, h, :, pl.ds(pl.multiple_of(2048 + f * 256, 256), 256)]))
        return out

    def load_b(self, scal, pieces, m, dst):
        if not self.fast:
            return [(pieces[1], dst)]
        return [
            (ref.at[ri, :, pl.ds(m * 48, 48)], dst.at[:, x, h, :, pl.ds(pl.multiple_of(f * 768, 768), 768)])
            for h, ri, x, f, ref in self._pieces(scal, pieces)
        ]

    def load_c(self, scal, pieces, m, dst):
        if not self.fast:
            return [(pieces[2], dst)]
        return [
            (
                ref.at[ri, :, pl.ds(m * 48, 48), pl.ds(j * 384, 384)],
                dst.at[:, f, j, h, :, pl.ds(pl.multiple_of(x * 384, 384), 384)],
            )
            for h, ri, x, f, ref in self._pieces(scal, pieces)
            for j in range(2)
        ]

    def _pieces(self, scal, pieces):
        mx, my, mc = scal[3], scal[4], scal[5]
        for h in range(2):
            for bi in range(4):
                ro, rc = bi % 2, bi // 2
                for ri in range(2):
                    rx, ry = (ri, ro) if h == 0 else (ro, ri)
                    x = lax.rem(mx + rx, 2)
                    y = lax.rem(my + ry, 2)
                    c = lax.rem(mc + rc, 2)
                    yield h, ri, x, y * 2 + c, pieces[h * 4 + bi]

    def blocks(self, scal):
        if not self.fast:
            return [(f, 0, 0) for f in range(4)]
        my, mc = scal[4], scal[5]
        return [(lax.rem(my + ry, 2) * 2 + lax.rem(mc + rc, 2), rc, ry) for rc in (1, 0) for ry in (1, 0)]

    def store_ab(self, scal, src, outs, m, f, rc, ry):
        if not self.fast:
            return [(src, outs[0].at[f])]
        res = []
        for rx in range(2):
            x = lax.rem(scal[3] + rx, 2)
            for h in range(2):
                first, second = (rx, ry) if h == 0 else (ry, rx)
                res.append((src.at[:, x, h], outs[rc * 2 + h].at[first, second, :, pl.ds(m * 48, 48)]))
        return res

    def store_c(self, scal, src, outs, m):
        if not self.fast:
            return [(src, outs[1])]
        res = []
        for f, rc, ry in self.blocks(scal):
            for rx in range(2):
                x = lax.rem(scal[3] + rx, 2)
                for h in range(2):
                    first, second = (rx, ry) if h == 0 else (ry, rx)
                    for j in range(2):
                        res.append(
                            (
                                src.at[:, f, j, h, :, pl.ds(pl.multiple_of(x * 384, 384), 384)],
                                outs[rc * 2 + h].at[first, second, :, pl.ds(m * 48, 48), pl.ds(j * 384, 384)],
                            )
                        )
        return res

    def store_vec(self, scal, src, outs):
        res = []
        for _, rc, ry in self.blocks(scal):
            for rx in range(2):
                x = lax.rem(scal[3] + rx, 2)
                res.append((src.at[:, x], outs[rc * 2].at[rx, ry, :, pl.ds(48, 16)]))
        return res


def start(copies, sems, base=0):
    made = [pltpu.make_async_copy(s, d, sems.at[base + i]) for i, (s, d) in enumerate(copies)]
    for c in made:
        c.start()
    return made


def wait(made):
    for c in made:
        c.wait()


def attn_fwd(plan, npieces, m, *refs):
    scal, x_ref, vec_ref, pb_ref = refs[:4]
    pieces = refs[4 : 4 + npieces]
    x1_ref, a1_ref, un_ref, p_ref, o_ref, a2_ref = refs[4 + npieces : 10 + npieces]
    wa, sems = refs[10 + npieces :]
    loads = start(plan.load_a(scal, pieces, m, wa), sems)
    n1, _ = ln_stats(x_ref[...])
    a1 = (n1 * vec_ref[G1 : G1 + 1] + vec_ref[C1 : C1 + 1]).astype(BF)
    a1_ref[...] = a1
    seg_row = seg_of(scal, lax.broadcasted_iota(jnp.int32, (T, T), 1))
    seg_col = seg_of(scal, lax.broadcasted_iota(jnp.int32, (T, T), 0))
    same = seg_row == seg_col
    wait(loads)
    for f in range(4):
        part = dot(a1, wa[:, :, :, :, 512 * f : 512 * f + 512].reshape(D, 512)) + pb_ref[0:1, 512 * f : 512 * f + 512]
        last = dot(a1, wa[:, :, :, :, 2048 + 256 * f : 2176 + 256 * f].reshape(D, 128)) + pb_ref[0:1, 2048 + 128 * f : 2176 + 128 * f]
        for j in range(9):
            u = 9 * f + j
            val = part[:, 64 * j : 64 * j + 64] if j < 8 else last[:, 0:64]
            val = val.astype(BF)
            if u < HEADS:
                val = val * BF(0.125)
            un_ref[u] = val
    for h in range(HEADS):
        s = jnp.where(same, dot_nt(un_ref[h], un_ref[HEADS + h]), -1e30)
        ex = jnp.exp(s - jnp.max(s, axis=-1, keepdims=True))
        p = ex * (1.0 / jnp.sum(ex, axis=-1, keepdims=True))
        p_ref[h] = p
        o_ref[:, 64 * h : 64 * h + 64] = dot(p.astype(BF), un_ref[2 * HEADS + h])
    n2, _ = ln_stats(o_ref[...])
    a2 = (n2 * vec_ref[G2 : G2 + 1] + vec_ref[C2 : C2 + 1]).astype(BF)
    a2_ref[...] = a2
    z = [dot(a2, wa[:, :, :, :, 2048 + 256 * f : 2304 + 256 * f].reshape(D, 256))[:, 64:] for f in range(4)]
    x1_ref[...] = x_ref[...] + (jnp.concatenate(z, axis=1) + vec_ref[BO : BO + 1])


def ff_fwd(plan, npieces, mb, mc, last, *refs):
    scal, x1_ref, vec_ref, hid_ref = refs[:4]
    pieces = refs[4 : 4 + npieces]
    x2_ref, a3_ref, sl_ref, n4_ref, a4_ref = refs[4 + npieces : 9 + npieces]
    wb, wc, sems = refs[9 + npieces :]
    load_b = start(plan.load_b(scal, pieces, mb, wb), sems)
    load_c = start(plan.load_c(scal, pieces, mc, wc), sems, len(load_b))
    n3, _ = ln_stats(x1_ref[...])
    a3 = (n3 * vec_ref[G3 : G3 + 1] + vec_ref[C3 : C3 + 1]).astype(BF)
    a3_ref[...] = a3
    wait(load_b)
    for f in range(4):
        cols = slice(768 * f, 768 * f + 768)
        n4_ref[:, cols] = dot(a3, wb[:, :, :, :, cols].reshape(D, 768)) + hid_ref[B1 : B1 + 1, cols]

    def rows_step(i, carry):
        rows = pl.ds(i * RB, RB)
        total = jnp.zeros((RB, 1), F32)
        for f in range(4):
            cols = slice(768 * f, 768 * f + 768)
            u = n4_ref[rows, cols]
            phi_c = 0.5 * (1.0 + lax.erf(u * (1.0 / math.sqrt(2.0))))
            r = u * phi_c
            sl_ref[rows, cols] = phi_c + u * (jnp.exp(-0.5 * u * u) * (1.0 / math.sqrt(2.0 * math.pi)))
            n4_ref[rows, cols] = r
            total += jnp.sum(r, axis=-1, keepdims=True)
        mean = total * (1.0 / FF)
        total = jnp.zeros((RB, 1), F32)
        for f in range(4):
            cols = slice(768 * f, 768 * f + 768)
            cen = n4_ref[rows, cols] - mean
            total += jnp.sum(cen * cen, axis=-1, keepdims=True)
        inv = lax.rsqrt(total * (1.0 / FF) + EPS)
        for f in range(4):
            cols = slice(768 * f, 768 * f + 768)
            n4 = (n4_ref[rows, cols] - mean) * inv
            n4_ref[rows, cols] = n4
            a4_ref[rows, cols] = (n4 * hid_ref[G4 : G4 + 1, cols] + hid_ref[C4 : C4 + 1, cols]).astype(BF)
            sl_ref[rows, cols] = sl_ref[rows, cols] * inv
        return carry

    lax.fori_loop(0, T // RB, rows_step, 0)
    wait(load_c)
    acc = dot_nt(a4_ref[:, 0:768], wc[0].reshape(D, 768))
    for z in range(1, 4):
        acc += dot_nt(a4_ref[:, 768 * z : 768 * z + 768], wc[z].reshape(D, 768))
    x2 = x1_ref[...] + (acc + vec_ref[B2 : B2 + 1])
    if last:
        seg = seg_of(scal, lax.broadcasted_iota(jnp.int32, (T, 1), 0))
        x2 = x2 * (seg < SEQS).astype(F32)
    x2_ref[...] = x2


def ff_bwd(plan, npieces, nouts, mb, mc, last, *refs):
    scal, dy_ref, x1_ref, a3_ref, sl_ref, n4_ref, a4_ref, vec_ref, hid_ref = refs[:9]
    pieces = refs[9 : 9 + npieces]
    dx1_ref, gv_ref, gh_ref = refs[9 + npieces : 12 + npieces]
    outs = refs[12 + npieces : 12 + npieces + nouts]
    wb, wc, gb, gc, da4, du_ref, sems = refs[12 + npieces + nouts :]
    load_c = start(plan.load_c(scal, pieces, mc, wc), sems)
    load_b = start(plan.load_b(scal, pieces, mb, wb), sems, len(load_c))
    base = len(load_c) + len(load_b)
    dy = dy_ref[...]
    if last:
        seg = seg_of(scal, lax.broadcasted_iota(jnp.int32, (T, 1), 0))
        dy = dy * (seg < SEQS).astype(F32)
    dz2 = dy.astype(BF)
    gv_ref[...] = jnp.zeros_like(gv_ref)
    gh_ref[...] = jnp.zeros_like(gh_ref)
    gv_ref[B2 : B2 + 1] = jnp.sum(dz2.astype(F32), axis=0, keepdims=True)
    dz2t = dz2.T
    wait(load_c)
    for z in range(4):
        cols = slice(768 * z, 768 * z + 768)
        da4[:, cols] = dot(dz2, wc[z].reshape(D, 768))
        gc[z] = dot(dz2t, a4_ref[:, cols]).astype(BF).reshape(4, 2, 2, 48, 768)
    saves = start(plan.store_c(scal, gc, outs, mc), sems, base)
    base += len(saves)

    def rows_step(i, carry):
        rows = pl.ds(i * RB, RB)
        s1 = jnp.zeros((RB, 1), F32)
        s2 = jnp.zeros((RB, 1), F32)
        for z in range(4):
            cols = slice(768 * z, 768 * z + 768)
            da = da4[rows, cols]
            n4 = n4_ref[rows, cols]
            dn = da * n4
            e = da * hid_ref[G4 : G4 + 1, cols]
            da4[rows, cols] = e
            s1 += jnp.sum(e, axis=-1, keepdims=True)
            s2 += jnp.sum(e * n4, axis=-1, keepdims=True)
            gh_ref[G4 : G4 + 1, cols] += jnp.sum(dn, axis=0, keepdims=True)
            gh_ref[C4 : C4 + 1, cols] += jnp.sum(da, axis=0, keepdims=True)
        s1 = s1 * (1.0 / FF)
        s2 = s2 * (1.0 / FF)
        for z in range(4):
            cols = slice(768 * z, 768 * z + 768)
            du = (sl_ref[rows, cols] * (da4[rows, cols] - s1 - n4_ref[rows, cols] * s2)).astype(BF)
            du_ref[rows, cols] = du
            gh_ref[B1 : B1 + 1, cols] += jnp.sum(du.astype(F32), axis=0, keepdims=True)
        return carry

    lax.fori_loop(0, T // RB, rows_step, 0)
    a3t = a3_ref[...].T
    wait(load_b)
    da3 = jnp.zeros((T, D), F32)
    for i, (f, rc, ry) in enumerate(plan.blocks(scal)):
        cols = pl.ds(pl.multiple_of(f * 768, 768), 768)
        du = du_ref[:, cols]
        gb[i] = dot(a3t, du).astype(BF).reshape(4, 2, 2, 48, 768)
        more = start(plan.store_ab(scal, gb.at[i], outs, mb, f, rc, ry), sems, base)
        base += len(more)
        saves += more
        da3 += dot_nt(du, wb[:, :, :, :, cols].reshape(D, 768))
    n3, inv3 = ln_stats(x1_ref[...])
    part, dg3, dc3 = ln_back(da3, vec_ref[G3 : G3 + 1], n3, inv3)
    gv_ref[G3 : G3 + 1] = dg3
    gv_ref[C3 : C3 + 1] = dc3
    dx1_ref[...] = dy + part
    wait(saves)


def attn_bwd(plan, npieces, nouts, m, fold, *refs):
    scal, dx1_ref, x_ref, a1_ref, un_ref, p_ref, o_ref, a2_ref, vec_ref = refs[:9]
    pos = 9
    others = refs[pos : pos + (5 if fold else 0)]
    pos += len(others)
    pieces = refs[pos : pos + npieces]
    pos += npieces
    dx_ref, gv_ref = refs[pos : pos + 2]
    outs = refs[pos + 2 : pos + 2 + nouts]
    scratch = refs[pos + 2 + nouts :]
    wa, ga, dpm, dzp, do_ref = scratch[:5]
    vblk = scratch[5] if fold else None
    sems = scratch[-1]
    loads = start(plan.load_a(scal, pieces, m, wa), sems)
    base = len(loads)
    dx1 = dx1_ref[...]
    dz = dx1.astype(BF)
    gv_ref[...] = jnp.zeros_like(gv_ref)
    gv_ref[BO : BO + 1] = jnp.sum(dz.astype(F32), axis=0, keepdims=True)
    dzp[...] = jnp.concatenate(
        [jnp.concatenate([jnp.zeros((T, 64), BF), dz[:, 192 * f : 192 * f + 192]], axis=1) for f in range(4)], axis=1
    )
    n2, inv2 = ln_stats(o_ref[...])
    wait(loads)
    da2 = dot_nt(dzp[...], wa[:, :, :, :, 2048:3072].reshape(D, 1024))
    do, dg2, dc2 = ln_back(da2, vec_ref[G2 : G2 + 1], n2, inv2)
    gv_ref[G2 : G2 + 1] = dg2
    gv_ref[C2 : C2 + 1] = dc2
    do = do.astype(BF)
    for f in range(4):
        dpm[:, 2048 + 256 * f : 2304 + 256 * f] = jnp.zeros((T, 256), BF)
    for h in range(HEADS):
        doh = do[:, 64 * h : 64 * h + 64]
        p = p_ref[h]
        q, k, v = un_ref[h], un_ref[HEADS + h], un_ref[2 * HEADS + h]
        dv = dot(p.astype(BF).T, doh)
        dp = dot_nt(doh, v)
        delta = jnp.sum(p * dp, axis=-1, keepdims=True)
        ds = (p * (dp - delta)).astype(BF)
        dq = dot(ds, k) * 0.125
        dk = dot(ds.T, q)
        for which, grad in ((0, dq), (1, dk), (2, dv)):
            u = which * HEADS + h
            f, j = divmod(u, 9)
            lane = 512 * f + 64 * j if j < 8 else 2048 + 256 * f
            grad = grad.astype(BF)
            dpm[:, lane : lane + 64] = grad
            if which != 1:
                row = BQ if which == 0 else BV
                gv_ref[row : row + 1, 64 * h : 64 * h + 64] = jnp.sum(grad.astype(F32), axis=0, keepdims=True)
    a1t = a1_ref[...].T
    a2t = a2_ref[...].T
    saves = []
    for i, (f, rc, ry) in enumerate(plan.blocks(scal)):
        main = dpm[:, pl.ds(pl.multiple_of(f * 512, 512), 512)]
        tail = dpm[:, pl.ds(pl.multiple_of(2048 + f * 256, 256), 256)]
        ga[i, :, :, :, :, 0:512] = dot(a1t, main).astype(BF).reshape(4, 2, 2, 48, 512)
        ga[i, :, :, :, :, 512:768] = (
            (dot(a1t, tail) + dot(a2t, dzp[:, pl.ds(pl.multiple_of(f * 256, 256), 256)])).astype(BF).reshape(4, 2, 2, 48, 256)
        )
        more = start(plan.store_ab(scal, ga.at[i], outs, m, f, rc, ry), sems, base)
        base += len(more)
        saves += more
    da1 = dot_nt(dpm[...], wa[...].reshape(D, FF))
    n1, inv1 = ln_stats(x_ref[...])
    part, dg1, dc1 = ln_back(da1, vec_ref[G1 : G1 + 1], n1, inv1)
    gv_ref[G1 : G1 + 1] = dg1
    gv_ref[C1 : C1 + 1] = dc1
    dx_ref[...] = dx1 + part
    if fold:
        va0, vb1, va1, gh0, gh1 = (r[...] for r in others)
        v0 = gv_ref[...] + va0
        v1 = vb1 + va1
        for d in range(8):
            c96 = slice(96 * d, 96 * d + 96)
            c384 = slice(384 * d, 384 * d + 384)
            low = jnp.concatenate([v0[:, c96], v1[:, c96], jnp.zeros((VROWS, 576), F32)], axis=1)
            vblk[d // 2, d % 2] = (low + jnp.concatenate([gh0[:, c384], gh1[:, c384]], axis=1)).astype(BF)
        more = start(plan.store_vec(scal, vblk, outs), sems, base)
        saves += more
    wait(saves)


def params(mib):
    return pltpu.CompilerParams(vmem_limit_bytes=mib * MIB)


def cost(flops, nbytes):
    return pl.CostEstimate(flops=int(flops), bytes_accessed=int(nbytes), transcendentals=0)


WA = pltpu.VMEM((4, 2, 2, 48, FF), BF)
WC = pltpu.VMEM((4, 4, 2, 2, 48, D), BF)
S = jax.ShapeDtypeStruct
WBYTES = D * FF * 2


def call_attn_fwd(plan, scal, x, vec, pbias, pieces, m):
    n = len(pieces)
    return pl.pallas_call(
        functools.partial(attn_fwd, plan, n, m),
        out_shape=(S((T, D), F32), S((T, D), BF), S((36, T, HD), BF), S((HEADS, T, T), F32), S((T, D), F32), S((T, D), BF)),
        in_specs=[SMEM, VMEM, VMEM, VMEM] + [ANY] * n,
        out_specs=[VMEM] * 6,
        scratch_shapes=[WA, pltpu.SemaphoreType.DMA((32,))],
        compiler_params=params(40),
        cost_estimate=cost(2 * T * D * FF * 6, WBYTES + 8e6),
        name="attn_fwd",
    )(scal, x, vec, pbias, *pieces)


def call_ff_fwd(plan, scal, x1, vec, hid, pieces, mb, mc, last):
    n = len(pieces)
    return pl.pallas_call(
        functools.partial(ff_fwd, plan, n, mb, mc, last),
        out_shape=(S((T, D), F32), S((T, D), BF), S((T, FF), F32), S((T, FF), F32), S((T, FF), BF)),
        in_specs=[SMEM, VMEM, VMEM, VMEM] + [ANY] * n,
        out_specs=[VMEM] * 5,
        scratch_shapes=[WA, WC, pltpu.SemaphoreType.DMA((48,))],
        compiler_params=params(40),
        cost_estimate=cost(2 * T * D * FF * 6, 2 * WBYTES + 8e6),
        name="ff_fwd",
    )(scal, x1, vec, hid, *pieces)


def grad_shapes(plan, n, extra=0):
    if not plan.fast:
        shapes = [S((4, 4, 2, 2, 48, D), BF)] * n
        return shapes
    return [S((2, 2, 4, n * 48 + e, D), BF) for e in (extra, 0, extra, 0)]


def call_ff_bwd(plan, scal, dy, x1, a3, sl, n4, a4, vec, hid, pieces, mb, mc, last):
    n = len(pieces)
    g = grad_shapes(plan, 2)
    res = pl.pallas_call(
        functools.partial(ff_bwd, plan, n, len(g), mb, mc, last),
        out_shape=(S((T, D), F32), S((VROWS, D), F32), S((VROWS, FF), F32), *g),
        in_specs=[SMEM] + [VMEM] * 8 + [ANY] * n,
        out_specs=[VMEM] * 3 + [ANY] * len(g),
        scratch_shapes=[
            WA,
            WC,
            WC,
            WC,
            pltpu.VMEM((T, FF), F32),
            pltpu.VMEM((T, FF), BF),
            pltpu.SemaphoreType.DMA((112,)),
        ],
        compiler_params=params(50),
        cost_estimate=cost(2 * T * D * FF * 8, 4 * WBYTES + 8e6),
        name="ff_bwd",
    )(scal, dy, x1, a3, sl, n4, a4, vec, hid, *pieces)
    return res[:3], res[3:]


def call_attn_bwd(plan, scal, dx1, x, a1, un, p, o, a2, vec, pieces, m, others):
    n = len(pieces)
    fold = len(others) > 0
    g = grad_shapes(plan, 1, 16 if fold else 0)
    vblk = [pltpu.VMEM((4, 2, VROWS, D), BF)] if fold else []
    res = pl.pallas_call(
        functools.partial(attn_bwd, plan, n, len(g), m, fold),
        out_shape=(S((T, D), F32), S((VROWS, D), F32), *g),
        in_specs=[SMEM] + [VMEM] * (8 + len(others)) + [ANY] * n,
        out_specs=[VMEM] * 2 + [ANY] * len(g),
        scratch_shapes=[
            WA,
            WC,
            pltpu.VMEM((T, FF), BF),
            pltpu.VMEM((T, 1024), BF),
            pltpu.VMEM((T, D), BF),
            *vblk,
            pltpu.SemaphoreType.DMA((64,)),
        ],
        compiler_params=params(40),
        cost_estimate=cost(2 * T * D * FF * 8, 2 * WBYTES + 8e6),
        name="attn_bwd",
    )(scal, dx1, x, a1, un, p, o, a2, vec, *others, *pieces)
    return res[:2], res[2:]


def shift(n, k):
    return [(i, (i + k) % n) for i in range(n)]


class Ring:
    def __init__(self, dp, fsdp):
        self.X = fsdp // 2
        self.Z = dp // self.X
        self.dp, self.fsdp = dp, fsdp

    def z(self, v, k):
        return lax.ppermute(v, "dp", [(z * self.X + x, (z + k) % self.Z * self.X + x) for z in range(self.Z) for x in range(self.X)])

    def x(self, v):
        return lax.ppermute(v, "dp", [(i, i ^ 1) for i in range(self.dp)])

    def y(self, v):
        return lax.ppermute(v, "fsdp", [(i, i ^ 2) for i in range(self.fsdp)])

    def c(self, v):
        return lax.ppermute(v, "fsdp", [(i, i ^ 1) for i in range(self.fsdp)])


def zcat_kernel(r1, r2, scal, p0, p1, p2, p3, o1, o2, sems):
    copies = []
    for k, ref in enumerate((p0, p1, p2, p3)):
        z = lax.rem(scal[2] + 4 - k, 4)
        copies.append((ref.at[pl.ds(0, r1)], o1.at[z]))
        copies.append((ref.at[pl.ds(r1, r2)], o2.at[z]))
    wait(start(copies, sems))


def zcat(scal, parts, r1, r2):
    return pl.pallas_call(
        functools.partial(zcat_kernel, r1, r2),
        out_shape=(S((4, r1, D), BF), S((4, r2, D), BF)),
        in_specs=[SMEM] + [ANY] * 4,
        out_specs=[ANY] * 2,
        scratch_shapes=[pltpu.SemaphoreType.DMA((8,))],
        cost_estimate=cost(0, 8 * (r1 + r2) * D * 4),
        name="zcat",
    )(scal, *parts)


def gather_chunk(ring, scal, pack, r1):
    r2 = pack.shape[0] - r1
    parts = [pack] + [ring.z(pack, k) for k in (1, 2, 3)]
    h1, h2 = zcat(scal, parts, r1, r2)
    x1 = ring.x(h1)
    y2 = ring.y(h2)
    h1 = jnp.stack([h1, x1])
    h2 = jnp.stack([h2, y2])
    y1 = ring.y(h1)
    x2 = ring.x(h2)
    return [h1, y1, ring.c(h1), ring.c(y1), h2, x2, ring.c(h2), ring.c(x2)]


def add(a, b):
    return (a.astype(F32) + b.astype(F32)).astype(BF)


def scatter_chunk(ring, zme, grads):
    k0, k1, s0, s1 = grads
    r0, r1 = ring.c(s0), ring.c(s1)
    x0 = ring.x(add(k0[1], r0[1]))
    y1 = ring.y(add(k1[1], r1[1]))
    a0 = add(k0[0], r0[0])
    a1 = add(k1[0], r1[0])
    y0 = ring.y(add(a0[1], x0[1]))
    x1 = ring.x(add(a1[1], y1[1]))
    b0 = add(a0[0], x0[0])
    b1 = add(a1[0], y1[0])

    def at(k):
        z = lax.rem(zme + k, 4)
        pick = lambda v: lax.dynamic_index_in_dim(v, z, 0, keepdims=False)
        return jnp.concatenate([add(pick(b0), pick(y0)), add(pick(b1), pick(x1))], axis=0)

    total = at(0).astype(F32)
    for k in (1, 2, 3):
        total = total + ring.z(at(k), k).astype(F32)
    return total


def unpack_vec(rows):
    rows = rows.astype(F32)
    vecs, hids = [], []
    for l in range(LAYERS):
        v = rows[:, :, 96 * l : 96 * l + 96].transpose(1, 0, 2).reshape(VROWS, D)
        h = rows[:, :, 384 * l : 384 * l + 384].transpose(1, 0, 2).reshape(VROWS, FF)
        vecs.append(v)
        hids.append(h)
    return vecs, hids


def proj_bias(vec):
    full = jnp.concatenate([vec[BQ], jnp.zeros((D,), F32), vec[BV]]).reshape(4, 9 * HD)
    return jnp.concatenate(
        [full[:, :512].reshape(2048), jnp.pad(full[:, 512:], ((0, 0), (0, 64))).reshape(512)]
    ).reshape(1, 2560)


def run_layers(plan, scal, inputs, cotangent, vecs, hids, pieces, after):
    pb = [proj_bias(v) for v in vecs]
    x = inputs
    kept = []
    for l in range(LAYERS):
        pa, ma, pbc, mb, mc = pieces[l]
        x1, a1, un, p, o, a2 = call_attn_fwd(plan, scal, x, vecs[l], pb[l], pa, ma)
        x2, a3, sl, n4, a4 = call_ff_fwd(plan, scal, x1, vecs[l], hids[l], pbc, mb, mc, l == LAYERS - 1)
        kept.append((x, x1, a1, un, p, o, a2, a3, sl, n4, a4))
        x = x2
    outputs = x
    dy = cotangent
    vec_grads = {}
    for l in reversed(range(LAYERS)):
        pa, ma, pbc, mb, mc = pieces[l]
        x, x1, a1, un, p, o, a2, a3, sl, n4, a4 = kept[l]
        (dx1, gva, gh), gbc = call_ff_bwd(plan, scal, dy, x1, a3, sl, n4, a4, vecs[l], hids[l], pbc, mb, mc, l == LAYERS - 1)
        after(l, "bc", gbc)
        others = (gva, *vec_grads[1][:2], gh, vec_grads[1][2]) if plan.fast and l == 0 else ()
        (dy, gvb), ga = call_attn_bwd(plan, scal, dx1, x, a1, un, p, o, a2, vecs[l], pa, ma, others)
        after(l, "a", ga)
        vec_grads[l] = (gva, gvb, gh)
    return outputs, dy, vec_grads


def fast_shards(ring, inputs, lengths, in_projection, out_projection, up_weight, down_weight, norm_gains, biases, hidden_gains, hidden_biases, cotangent):
    plan = Plan(True)
    dpi, fi = lax.axis_index("dp"), lax.axis_index("fsdp")
    zme = dpi // ring.X
    place = jnp.stack([zme, dpi % ring.X, fi // 2, fi % 2]).astype(jnp.int32)
    scal = jnp.concatenate([lengths[0], place, jnp.zeros((2,), jnp.int32)])

    own_vec = jnp.concatenate([norm_gains, biases], axis=1)
    own_hid = jnp.concatenate([hidden_gains, hidden_biases], axis=1)
    vec_rows = jnp.concatenate(
        [
            jnp.pad(jnp.concatenate([own_vec[0], own_vec[1]], axis=1), ((0, 0), (0, 576))),
            jnp.concatenate([own_hid[0], own_hid[1]], axis=1),
            jnp.zeros((3, D), BF),
        ],
        axis=0,
    )
    pack_a = [jnp.concatenate([in_projection[l], out_projection[l]], axis=1) for l in range(LAYERS)]
    pack_c = []
    for l in range(LAYERS):
        t = down_weight[l].T
        pack_c.append(jnp.concatenate([t[:96], t[96:]], axis=1))
    pack_bc = []
    for l in range(LAYERS):
        b, c = up_weight[l], pack_c[l]
        pack_bc.append(jnp.concatenate([b[:48], c[:48], b[48:], c[48:]], axis=0))
    first = jnp.concatenate([pack_a[0][:48], vec_rows, pack_a[0][48:]], axis=0)
    pieces = []
    for l in range(LAYERS):
        got_a = gather_chunk(ring, scal, first if l == 0 else pack_a[l], 64 if l == 0 else 48)
        got_bc = gather_chunk(ring, scal, pack_bc[l], 96)
        pieces.append((got_a, 0, got_bc, 0, 1))
        if l == 0:
            rows = got_a[0][:, :, 48:64]
            xme = dpi % ring.X
            rows = jnp.where(xme == 0, rows, rows[::-1]).transpose(1, 0, 2, 3).reshape(8, VROWS, D)
            vecs, hids = unpack_vec(rows)
    sums = {}

    def after(l, name, grads):
        sums[l, name] = scatter_chunk(ring, zme, grads)

    outputs, input_gradient, _ = run_layers(plan, scal, inputs, cotangent, vecs, hids, pieces, after)
    a = [sums[0, "a"], sums[1, "a"]]
    vrows = a[0][48:64]
    a[0] = jnp.concatenate([a[0][:48], a[0][64:]], axis=0)
    bc = [sums[l, "bc"] for l in range(LAYERS)]
    b = [jnp.concatenate([v[:48], v[96:144]], axis=0) for v in bc]
    c = [jnp.concatenate([v[48:96], v[144:]], axis=0) for v in bc]
    c = [jnp.concatenate([v[:, :384], v[:, 384:]], axis=0).T for v in c]
    gv = jnp.stack([vrows[:10, :96], vrows[:10, 96:192]])
    gh = jnp.stack([vrows[10:13, :384], vrows[10:13, 384:]])
    return (
        outputs,
        input_gradient,
        jnp.stack([v[:, :576] for v in a]),
        jnp.stack([v[:, 576:] for v in a]),
        jnp.stack(b),
        jnp.stack(c),
        gv[:, :3],
        gv[:, 3:],
        gh[:, :1],
        gh[:, 1:],
    )


def whole_shards(inputs, lengths, in_projection, out_projection, up_weight, down_weight, norm_gains, biases, hidden_gains, hidden_biases, cotangent):
    plan = Plan(False)
    scal = jnp.concatenate([lengths[0], jnp.zeros((6,), jnp.int32)])

    def full(w):
        return lax.all_gather(lax.all_gather(w, "fsdp", axis=1, tiled=True), "dp", axis=0, tiled=True)

    def rows(v, width):
        return jnp.pad(lax.all_gather(v, "dp", axis=1, tiled=True).astype(F32), ((0, VROWS - v.shape[0]), (0, 0)))

    vecs, hids, pieces = [], [], []
    for l in range(LAYERS):
        qkv = full(in_projection[l]).reshape(D, 4, 9 * HD)
        out = full(out_projection[l]).reshape(D, 4, 192)
        a = jnp.concatenate([qkv[:, :, :512].reshape(D, 2048), jnp.concatenate([qkv[:, :, 512:], out], axis=2).reshape(D, 1024)], axis=1)
        b = full(up_weight[l])
        c = full(down_weight[l]).reshape(4, D, D).transpose(0, 2, 1)
        shape = (4, 2, 2, 48, FF)
        got = [a.reshape(shape), b.reshape(shape), c.reshape(4, 4, 2, 2, 48, D)]
        pieces.append((got, 0, got, 0, 0))
        vecs.append(rows(jnp.concatenate([norm_gains[l], biases[l]], axis=0), D))
        hid = rows(jnp.concatenate([hidden_gains[l], hidden_biases[l]], axis=0), FF)
        hids.append(jnp.roll(hid, HROW, axis=0))
    grads = {}

    def after(l, name, got):
        grads[l, name] = got

    outputs, input_gradient, vec_grads = run_layers(plan, scal, inputs, cotangent, vecs, hids, pieces, after)

    def scatter(g):
        g = lax.psum_scatter(g.astype(BF), "dp", scatter_dimension=0, tiled=True)
        return lax.psum_scatter(g, "fsdp", scatter_dimension=1, tiled=True).astype(F32)

    def scatter_rows(v):
        v = lax.psum_scatter(v.astype(BF), "dp", scatter_dimension=1, tiled=True).astype(F32)
        return lax.psum(v, "fsdp")

    res = []
    for l in range(LAYERS):
        gb, gc = grads[l, "bc"]
        (ga,) = grads[l, "a"]
        ga = ga.reshape(4, D, D).transpose(1, 0, 2)
        gva, gvb, gh = vec_grads[l]
        gv = scatter_rows((gva + gvb)[:10])
        gh = scatter_rows(gh[HROW : HROW + 3])
        res.append(
            (
                scatter(ga[:, :, :576].reshape(D, 3 * D)),
                scatter(ga[:, :, 576:].reshape(D, D)),
                scatter(gb.reshape(4, D, D).transpose(1, 0, 2).reshape(D, FF)),
                scatter(gc.reshape(4, D, D).transpose(0, 2, 1).reshape(FF, D)),
                gv[:3],
                gv[3:],
                gh[:1],
                gh[1:],
            )
        )
    return (outputs, input_gradient, *(jnp.stack([r[i] for r in res]) for i in range(8)))


def solution(mesh):
    dp, fsdp = mesh.shape["dp"], mesh.shape["fsdp"]
    both = P(("dp", "fsdp"), None)
    mat = P(None, "dp", "fsdp")
    row = P(None, None, "dp")
    ring = Ring(dp, fsdp)
    shards = functools.partial(fast_shards, ring) if (dp, fsdp) == (8, 4) else whole_shards
    return jax.shard_map(
        shards,
        mesh=mesh,
        in_specs=(both, both, mat, mat, mat, mat, row, row, row, row, both),
        out_specs=(both, both, mat, mat, mat, mat, row, row, row, row),
        check_vma=False,
    )
```

```python
import functools
import math

import jax
import jax.numpy as jnp
from jax import lax
from jax.experimental import pallas as pl
from jax.experimental.pallas import tpu as pltpu
from jax.sharding import PartitionSpec as P

HEADS = 12
HD = 64
LAYERS = 2
SEQS = 2
D = 768
FF = 3072
T = 256
EPS = 1e-05
BF = jnp.bfloat16
F32 = jnp.float32
MIB = 1 << 20

ANY = pl.BlockSpec(memory_space=pltpu.HBM)
SMEM = pl.BlockSpec(memory_space=pltpu.SMEM)
VMEM = pl.BlockSpec(memory_space=pltpu.VMEM)

G1, G2, G3, C1, BQ, BV, C2, BO, C3, B2 = range(10)
VROWS = 16
HROW = 10
G4, B1, C4 = 10, 11, 12

RB = 32


def dot(a, b):
    return jnp.dot(a, b, preferred_element_type=F32)


def dot_nt(a, b):
    return lax.dot_general(a, b, (((1,), (1,)), ((), ())), preferred_element_type=F32)


def unit_lane(u):
    f, j = divmod(u, 9)
    return 512 * f + 64 * j if j < 8 else 2048 + 128 * f


def ln_stats(v):
    m = jnp.mean(v, axis=-1, keepdims=True)
    cen = v - m
    inv = lax.rsqrt(jnp.mean(cen * cen, axis=-1, keepdims=True) + EPS)
    return cen * inv, inv


def ln_back(dn, g, n, inv):
    e = dn * g
    dv = inv * (e - jnp.mean(e, axis=-1, keepdims=True) - n * jnp.mean(e * n, axis=-1, keepdims=True))
    return dv, jnp.sum(dn * n, axis=0, keepdims=True), jnp.sum(dn, axis=0, keepdims=True)


def seg_of(scal, places):
    e0 = scal[0]
    e1 = scal[0] + scal[1]
    return (places >= e0).astype(jnp.int32) + (places >= e1).astype(jnp.int32)


class Plan:
    def __init__(self, fast):
        self.fast = fast

    def load_a(self, scal, pieces, m, dst):
        if not self.fast:
            return [(pieces[0], dst)]
        out = []
        for h, ri, x, f, ref in self._pieces(scal, pieces):
            src = ref.at[ri, :, pl.ds(m * 48, 48)]
            out.append((src.at[:, :, pl.ds(0, 512)], dst.at[:, x, h, :, pl.ds(pl.multiple_of(f * 512, 512), 512)]))
            out.append((src.at[:, :, pl.ds(512, 256)], dst.at[:, x, h, :, pl.ds(pl.multiple_of(2048 + f * 256, 256), 256)]))
        return out

    def load_b(self, scal, pieces, m, dst):
        if not self.fast:
            return [(pieces[1], dst)]
        return [
            (ref.at[ri, :, pl.ds(m * 48, 48)], dst.at[:, x, h, :, pl.ds(pl.multiple_of(f * 768, 768), 768)])
            for h, ri, x, f, ref in self._pieces(scal, pieces)
        ]

    def load_c(self, scal, pieces, m, dst):
        if not self.fast:
            return [(pieces[2], dst)]
        pieces = pieces[-8:]
        return [
            (
                ref.at[ri, :, pl.ds(m * 48, 48), pl.ds(j * 384, 384)],
                dst.at[:, f, j, h, :, pl.ds(pl.multiple_of(x * 384, 384), 384)],
            )
            for h, ri, x, f, ref in self._pieces(scal, pieces)
            for j in range(2)
        ]

    def _pieces(self, scal, pieces):
        mx, my, mc = scal[3], scal[4], scal[5]
        for h in range(2):
            for bi in range(4):
                ro, rc = bi % 2, bi // 2
                for ri in range(2):
                    rx, ry = (ri, ro) if h == 0 else (ro, ri)
                    x = lax.rem(mx + rx, 2)
                    y = lax.rem(my + ry, 2)
                    c = lax.rem(mc + rc, 2)
                    yield h, ri, x, y * 2 + c, pieces[h * 4 + bi]


    def blocks(self, scal):
        if not self.fast:
            return [(f, 0, 0) for f in range(4)]
        my, mc = scal[4], scal[5]
        return [(lax.rem(my + ry, 2) * 2 + lax.rem(mc + rc, 2), rc, ry) for rc in (1, 0) for ry in (1, 0)]

    def store_ab(self, scal, src, outs, m, f, rc, ry):
        if not self.fast:
            return [(src, outs[0].at[f])]
        res = []
        for rx in range(2):
            x = lax.rem(scal[3] + rx, 2)
            for h in range(2):
                first, second = (rx, ry) if h == 0 else (ry, rx)
                res.append((src.at[:, x, h], outs[rc].at[h, first, second, :, pl.ds(m * 48, 48)]))
        return res

    def store_c(self, scal, src, outs, m):
        if not self.fast:
            return [(src, outs[1])]
        res = []
        for f, rc, ry in self.blocks(scal):
            for rx in range(2):
                x = lax.rem(scal[3] + rx, 2)
                for h in range(2):
                    first, second = (rx, ry) if h == 0 else (ry, rx)
                    for j in range(2):
                        res.append(
                            (
                                src.at[:, f, j, h, :, pl.ds(pl.multiple_of(x * 384, 384), 384)],
                                outs[rc].at[h, first, second, :, pl.ds(m * 48, 48), pl.ds(j * 384, 384)],
                            )
                        )
        return res

    def store_vec(self, scal, src, outs):
        res = []
        for _, rc, ry in self.blocks(scal):
            for rx in range(2):
                x = lax.rem(scal[3] + rx, 2)
                for h in range(2):
                    first, second = (rx, ry) if h == 0 else (ry, rx)
                    res.append((src.at[h, :, x], outs[rc].at[h, first, second, :, pl.ds(48, 16)]))
        return res


def flat(pieces):
    arrays, finds = [], []
    for piece in pieces:
        array, index = piece if isinstance(piece, tuple) else (piece, None)
        place = next((i for i, v in enumerate(arrays) if v is array), len(arrays))
        if place == len(arrays):
            arrays.append(array)
        finds.append((place, index))
    return arrays, lambda refs: [refs[i] if j is None else refs[i].at[j] for i, j in finds]


def start(copies, sems, base=0):
    made = [pltpu.make_async_copy(s, d, sems.at[base + i]) for i, (s, d) in enumerate(copies)]
    for c in made:
        c.start()
    return made


def wait(made):
    for c in made:
        c.wait()


def attn_fwd(plan, npieces, find, m, *refs):
    scal, x_ref, vec_ref, pb_ref = refs[:4]
    pieces = find(refs[4 : 4 + npieces])
    x1_ref, a1_ref, un_ref, p_ref, o_ref, a2_ref = refs[4 + npieces : 10 + npieces]
    wa, sems = refs[10 + npieces :]
    loads = start(plan.load_a(scal, pieces, m, wa), sems)
    n1, _ = ln_stats(x_ref[...])
    a1 = (n1 * vec_ref[G1 : G1 + 1] + vec_ref[C1 : C1 + 1]).astype(BF)
    a1_ref[...] = a1
    seg_row = seg_of(scal, lax.broadcasted_iota(jnp.int32, (T, T), 1))
    seg_col = seg_of(scal, lax.broadcasted_iota(jnp.int32, (T, T), 0))
    same = seg_row == seg_col
    wait(loads)
    for f in range(4):
        part = dot(a1, wa[:, :, :, :, 512 * f : 512 * f + 512].reshape(D, 512)) + pb_ref[0:1, 512 * f : 512 * f + 512]
        last = dot(a1, wa[:, :, :, :, 2048 + 256 * f : 2176 + 256 * f].reshape(D, 128)) + pb_ref[0:1, 2048 + 128 * f : 2176 + 128 * f]
        for j in range(9):
            u = 9 * f + j
            val = part[:, 64 * j : 64 * j + 64] if j < 8 else last[:, 0:64]
            val = val.astype(BF)
            if u < HEADS:
                val = val * BF(0.125)
            un_ref[u] = val
    for h in range(HEADS):
        s = jnp.where(same, dot_nt(un_ref[h], un_ref[HEADS + h]), -1e30)
        ex = jnp.exp(s - jnp.max(s, axis=-1, keepdims=True))
        p = ex * (1.0 / jnp.sum(ex, axis=-1, keepdims=True))
        p_ref[h] = p
        o_ref[:, 64 * h : 64 * h + 64] = dot(p.astype(BF), un_ref[2 * HEADS + h])
    n2, _ = ln_stats(o_ref[...])
    a2 = (n2 * vec_ref[G2 : G2 + 1] + vec_ref[C2 : C2 + 1]).astype(BF)
    a2_ref[...] = a2
    z = [dot(a2, wa[:, :, :, :, 2048 + 256 * f : 2304 + 256 * f].reshape(D, 256))[:, 64:] for f in range(4)]
    x1_ref[...] = x_ref[...] + (jnp.concatenate(z, axis=1) + vec_ref[BO : BO + 1])


def ff_fwd(plan, npieces, find, mb, mc, last, *refs):
    scal, x1_ref, vec_ref, hid_ref = refs[:4]
    pieces = find(refs[4 : 4 + npieces])
    x2_ref, a3_ref, sl_ref, n4_ref, a4_ref = refs[4 + npieces : 9 + npieces]
    wb, wc, sems = refs[9 + npieces :]
    load_b = start(plan.load_b(scal, pieces, mb, wb), sems)
    load_c = start(plan.load_c(scal, pieces, mc, wc), sems, len(load_b))
    n3, _ = ln_stats(x1_ref[...])
    a3 = (n3 * vec_ref[G3 : G3 + 1] + vec_ref[C3 : C3 + 1]).astype(BF)
    a3_ref[...] = a3
    wait(load_b)
    for f in range(4):
        cols = slice(768 * f, 768 * f + 768)
        n4_ref[:, cols] = dot(a3, wb[:, :, :, :, cols].reshape(D, 768)) + hid_ref[B1 : B1 + 1, cols]

    def rows_step(i, carry):
        rows = pl.ds(i * RB, RB)
        total = jnp.zeros((RB, 1), F32)
        for f in range(4):
            cols = slice(768 * f, 768 * f + 768)
            u = n4_ref[rows, cols]
            phi_c = 0.5 * (1.0 + lax.erf(u * (1.0 / math.sqrt(2.0))))
            r = u * phi_c
            sl_ref[rows, cols] = phi_c + u * (jnp.exp(-0.5 * u * u) * (1.0 / math.sqrt(2.0 * math.pi)))
            n4_ref[rows, cols] = r
            total += jnp.sum(r, axis=-1, keepdims=True)
        mean = total * (1.0 / FF)
        total = jnp.zeros((RB, 1), F32)
        for f in range(4):
            cols = slice(768 * f, 768 * f + 768)
            cen = n4_ref[rows, cols] - mean
            total += jnp.sum(cen * cen, axis=-1, keepdims=True)
        inv = lax.rsqrt(total * (1.0 / FF) + EPS)
        for f in range(4):
            cols = slice(768 * f, 768 * f + 768)
            n4 = (n4_ref[rows, cols] - mean) * inv
            n4_ref[rows, cols] = n4
            a4_ref[rows, cols] = (n4 * hid_ref[G4 : G4 + 1, cols] + hid_ref[C4 : C4 + 1, cols]).astype(BF)
            sl_ref[rows, cols] = sl_ref[rows, cols] * inv
        return carry

    lax.fori_loop(0, T // RB, rows_step, 0)
    wait(load_c)
    acc = dot_nt(a4_ref[:, 0:768], wc[0].reshape(D, 768))
    for z in range(1, 4):
        acc += dot_nt(a4_ref[:, 768 * z : 768 * z + 768], wc[z].reshape(D, 768))
    x2 = x1_ref[...] + (acc + vec_ref[B2 : B2 + 1])
    if last:
        seg = seg_of(scal, lax.broadcasted_iota(jnp.int32, (T, 1), 0))
        x2 = x2 * (seg < SEQS).astype(F32)
    x2_ref[...] = x2


def ff_bwd(plan, npieces, find, nouts, mb, mc, last, *refs):
    scal, dy_ref, x1_ref, a3_ref, sl_ref, n4_ref, a4_ref, vec_ref, hid_ref = refs[:9]
    pieces = find(refs[9 : 9 + npieces])
    dx1_ref, gv_ref, gh_ref = refs[9 + npieces : 12 + npieces]
    outs = refs[12 + npieces : 12 + npieces + nouts]
    wb, wc, gb, gc, da4, du_ref, sems = refs[12 + npieces + nouts :]
    load_c = start(plan.load_c(scal, pieces, mc, wc), sems)
    load_b = start(plan.load_b(scal, pieces, mb, wb), sems, len(load_c))
    base = len(load_c) + len(load_b)
    dy = dy_ref[...]
    if last:
        seg = seg_of(scal, lax.broadcasted_iota(jnp.int32, (T, 1), 0))
        dy = dy * (seg < SEQS).astype(F32)
    dz2 = dy.astype(BF)
    gv_ref[...] = jnp.zeros_like(gv_ref)
    gh_ref[...] = jnp.zeros_like(gh_ref)
    gv_ref[B2 : B2 + 1] = jnp.sum(dz2.astype(F32), axis=0, keepdims=True)
    dz2t = dz2.T
    wait(load_c)
    for z in range(4):
        cols = slice(768 * z, 768 * z + 768)
        da4[:, cols] = dot(dz2, wc[z].reshape(D, 768))
        gc[z] = dot(dz2t, a4_ref[:, cols]).astype(BF).reshape(4, 2, 2, 48, 768)
    saves = start(plan.store_c(scal, gc, outs, 1), sems, base)
    base += len(saves)

    def rows_step(i, carry):
        rows = pl.ds(i * RB, RB)
        s1 = jnp.zeros((RB, 1), F32)
        s2 = jnp.zeros((RB, 1), F32)
        for z in range(4):
            cols = slice(768 * z, 768 * z + 768)
            da = da4[rows, cols]
            n4 = n4_ref[rows, cols]
            dn = da * n4
            e = da * hid_ref[G4 : G4 + 1, cols]
            da4[rows, cols] = e
            s1 += jnp.sum(e, axis=-1, keepdims=True)
            s2 += jnp.sum(e * n4, axis=-1, keepdims=True)
            gh_ref[G4 : G4 + 1, cols] += jnp.sum(dn, axis=0, keepdims=True)
            gh_ref[C4 : C4 + 1, cols] += jnp.sum(da, axis=0, keepdims=True)
        s1 = s1 * (1.0 / FF)
        s2 = s2 * (1.0 / FF)
        for z in range(4):
            cols = slice(768 * z, 768 * z + 768)
            du = (sl_ref[rows, cols] * (da4[rows, cols] - s1 - n4_ref[rows, cols] * s2)).astype(BF)
            du_ref[rows, cols] = du
            gh_ref[B1 : B1 + 1, cols] += jnp.sum(du.astype(F32), axis=0, keepdims=True)
        return carry

    lax.fori_loop(0, T // RB, rows_step, 0)
    a3t = a3_ref[...].T
    wait(load_b)
    da3 = jnp.zeros((T, D), F32)
    for i, (f, rc, ry) in enumerate(plan.blocks(scal)):
        cols = pl.ds(pl.multiple_of(f * 768, 768), 768)
        du = du_ref[:, cols]
        gb[i] = dot(a3t, du).astype(BF).reshape(4, 2, 2, 48, 768)
        more = start(plan.store_ab(scal, gb.at[i], outs, 0, f, rc, ry), sems, base)
        base += len(more)
        saves += more
        da3 += dot_nt(du, wb[:, :, :, :, cols].reshape(D, 768))
    n3, inv3 = ln_stats(x1_ref[...])
    part, dg3, dc3 = ln_back(da3, vec_ref[G3 : G3 + 1], n3, inv3)
    gv_ref[G3 : G3 + 1] = dg3
    gv_ref[C3 : C3 + 1] = dc3
    dx1_ref[...] = dy + part
    wait(saves)


def attn_bwd(plan, npieces, find, nouts, m, fold, *refs):
    scal, dx1_ref, x_ref, a1_ref, un_ref, p_ref, o_ref, a2_ref, vec_ref = refs[:9]
    pos = 9
    others = refs[pos : pos + (5 if fold else 0)]
    pos += len(others)
    pieces = find(refs[pos : pos + npieces])
    pos += npieces
    dx_ref, gv_ref = refs[pos : pos + 2]
    outs = refs[pos + 2 : pos + 2 + nouts]
    scratch = refs[pos + 2 + nouts :]
    wa, ga, dpm, dzp, do_ref = scratch[:5]
    vblk = scratch[5] if fold else None
    sems = scratch[-1]
    loads = start(plan.load_a(scal, pieces, m, wa), sems)
    base = len(loads)
    dx1 = dx1_ref[...]
    dz = dx1.astype(BF)
    gv_ref[...] = jnp.zeros_like(gv_ref)
    gv_ref[BO : BO + 1] = jnp.sum(dz.astype(F32), axis=0, keepdims=True)
    dzp[...] = jnp.concatenate(
        [jnp.concatenate([jnp.zeros((T, 64), BF), dz[:, 192 * f : 192 * f + 192]], axis=1) for f in range(4)], axis=1
    )
    n2, inv2 = ln_stats(o_ref[...])
    wait(loads)
    da2 = dot_nt(dzp[...], wa[:, :, :, :, 2048:3072].reshape(D, 1024))
    do, dg2, dc2 = ln_back(da2, vec_ref[G2 : G2 + 1], n2, inv2)
    gv_ref[G2 : G2 + 1] = dg2
    gv_ref[C2 : C2 + 1] = dc2
    do = do.astype(BF)
    for f in range(4):
        dpm[:, 2048 + 256 * f : 2304 + 256 * f] = jnp.zeros((T, 256), BF)
    for h in range(HEADS):
        doh = do[:, 64 * h : 64 * h + 64]
        p = p_ref[h]
        q, k, v = un_ref[h], un_ref[HEADS + h], un_ref[2 * HEADS + h]
        dv = dot(p.astype(BF).T, doh)
        dp = dot_nt(doh, v)
        delta = jnp.sum(p * dp, axis=-1, keepdims=True)
        ds = (p * (dp - delta)).astype(BF)
        dq = dot(ds, k) * 0.125
        dk = dot(ds.T, q)
        for which, grad in ((0, dq), (1, dk), (2, dv)):
            u = which * HEADS + h
            f, j = divmod(u, 9)
            lane = 512 * f + 64 * j if j < 8 else 2048 + 256 * f
            grad = grad.astype(BF)
            dpm[:, lane : lane + 64] = grad
            if which != 1:
                row = BQ if which == 0 else BV
                gv_ref[row : row + 1, 64 * h : 64 * h + 64] = jnp.sum(grad.astype(F32), axis=0, keepdims=True)
    a1t = a1_ref[...].T
    a2t = a2_ref[...].T
    saves = []
    for i, (f, rc, ry) in enumerate(plan.blocks(scal)):
        main = dpm[:, pl.ds(pl.multiple_of(f * 512, 512), 512)]
        tail = dpm[:, pl.ds(pl.multiple_of(2048 + f * 256, 256), 256)]
        ga[i, :, :, :, :, 0:512] = dot(a1t, main).astype(BF).reshape(4, 2, 2, 48, 512)
        ga[i, :, :, :, :, 512:768] = (
            (dot(a1t, tail) + dot(a2t, dzp[:, pl.ds(pl.multiple_of(f * 256, 256), 256)])).astype(BF).reshape(4, 2, 2, 48, 256)
        )
        more = start(plan.store_ab(scal, ga.at[i], outs, m, f, rc, ry), sems, base)
        base += len(more)
        saves += more
    da1 = dot_nt(dpm[...], wa[...].reshape(D, FF))
    n1, inv1 = ln_stats(x_ref[...])
    part, dg1, dc1 = ln_back(da1, vec_ref[G1 : G1 + 1], n1, inv1)
    gv_ref[G1 : G1 + 1] = dg1
    gv_ref[C1 : C1 + 1] = dc1
    dx_ref[...] = dx1 + part
    if fold:
        va0, vb1, va1, gh0, gh1 = (r[...] for r in others)
        v0 = gv_ref[...] + va0
        v1 = vb1 + va1
        for d in range(8):
            c96 = slice(96 * d, 96 * d + 96)
            c384 = slice(384 * d, 384 * d + 384)
            low = jnp.concatenate([v0[:, c96], v1[:, c96], jnp.zeros((VROWS, 576), F32)], axis=1)
            vblk[0, d // 2, d % 2] = low.astype(BF)
            vblk[1, d // 2, d % 2] = jnp.concatenate([gh0[:, c384], gh1[:, c384]], axis=1).astype(BF)
        more = start(plan.store_vec(scal, vblk, outs), sems, base)
        saves += more
    wait(saves)


def cost(flops, nbytes):
    return pl.CostEstimate(flops=int(flops), bytes_accessed=int(nbytes), transcendentals=0)


class Seq:
    def __init__(self, chained):
        self.chained = chained
        self.token = None
        self.held = []
        self.carried = []

    def hold(self, *arrays):
        self.held += arrays

    def carry(self, *arrays):
        self.carried = list(arrays)

    def __call__(self, kernel, out_shape, in_specs, out_specs, args, scratch=(), mib=24, **options):
        deps = [self.token] if self.chained and self.token is not None else []
        deps += self.held
        carried = self.carried
        self.held, self.carried = [], []
        n, k, m, q = len(args), len(deps), len(carried), len(out_shape)

        def body(*refs):
            first = n + k + m
            kernel(*refs[:n], *refs[first : first + q], *refs[first + q + m :])

        res = pl.pallas_call(
            body,
            out_shape=tuple(out_shape) + tuple(S(v.shape, v.dtype) for v in carried),
            in_specs=list(in_specs) + [ANY] * (k + m),
            out_specs=tuple(out_specs) + (ANY,) * m,
            scratch_shapes=list(scratch),
            input_output_aliases={n + k + i: q + i for i in range(m)},
            compiler_params=pltpu.CompilerParams(vmem_limit_bytes=mib * MIB),
            **options,
        )(*args, *deps, *carried)
        self.token = res[0]
        self.carried = list(res[q:])
        return res[:q]


WA = pltpu.VMEM((4, 2, 2, 48, FF), BF)
WC = pltpu.VMEM((4, 4, 2, 2, 48, D), BF)
S = jax.ShapeDtypeStruct
WBYTES = D * FF * 2


def call_attn_fwd(seq, plan, scal, x, vec, pbias, pieces, m):
    pieces, find = flat(pieces)
    n = len(pieces)
    return seq(
        functools.partial(attn_fwd, plan, n, find, m),
        (S((T, D), F32), S((T, D), BF), S((36, T, HD), BF), S((HEADS, T, T), F32), S((T, D), F32), S((T, D), BF)),
        [SMEM, VMEM, VMEM, VMEM] + [ANY] * n,
        [VMEM] * 6,
        (scal, x, vec, pbias, *pieces),
        [WA, pltpu.SemaphoreType.DMA((32,))],
        cost_estimate=cost(2 * T * D * FF * 6, WBYTES + 8e6),
        name="attn_fwd",
        mib=64,
    )


def call_ff_fwd(seq, plan, scal, x1, vec, hid, pieces, mb, mc, last):
    pieces, find = flat(pieces)
    n = len(pieces)
    return seq(
        functools.partial(ff_fwd, plan, n, find, mb, mc, last),
        (S((T, D), F32), S((T, D), BF), S((T, FF), F32), S((T, FF), F32), S((T, FF), BF)),
        [SMEM, VMEM, VMEM, VMEM] + [ANY] * n,
        [VMEM] * 5,
        (scal, x1, vec, hid, *pieces),
        [WA, WC, pltpu.SemaphoreType.DMA((48,))],
        cost_estimate=cost(2 * T * D * FF * 6, 2 * WBYTES + 8e6),
        name="ff_fwd",
        mib=64,
    )


def grad_shapes(plan, n, extra=0):
    if not plan.fast:
        return [S((4, 4, 2, 2, 48, D), BF)] * n
    return [S((2, 2, 2, 4, n * 48 + extra, D), BF)] * 2


def call_ff_bwd(seq, plan, scal, dy, x1, a3, sl, n4, a4, vec, hid, pieces, mb, mc, last):
    pieces, find = flat(pieces)
    n = len(pieces)
    g = grad_shapes(plan, 2)
    res = seq(
        functools.partial(ff_bwd, plan, n, find, len(g), mb, mc, last),
        (S((T, D), F32), S((VROWS, D), F32), S((VROWS, FF), F32), *g),
        [SMEM] + [VMEM] * 8 + [ANY] * n,
        [VMEM] * 3 + [ANY] * len(g),
        (scal, dy, x1, a3, sl, n4, a4, vec, hid, *pieces),
        [WA, WC, WC, WC, pltpu.VMEM((T, FF), F32), pltpu.VMEM((T, FF), BF), pltpu.SemaphoreType.DMA((112,))],
        cost_estimate=cost(2 * T * D * FF * 8, 4 * WBYTES + 8e6),
        name="ff_bwd",
        mib=64,
    )
    return res[:3], res[3:]


def call_attn_bwd(seq, plan, scal, dx1, x, a1, un, p, o, a2, vec, pieces, m, others):
    pieces, find = flat(pieces)
    n = len(pieces)
    fold = len(others) > 0
    g = grad_shapes(plan, 1, 16 if fold else 0)
    vblk = [pltpu.VMEM((2, 4, 2, VROWS, D), BF)] if fold else []
    res = seq(
        functools.partial(attn_bwd, plan, n, find, len(g), m, fold),
        (S((T, D), F32), S((VROWS, D), F32), *g),
        [SMEM] + [VMEM] * (8 + len(others)) + [ANY] * n,
        [VMEM] * 2 + [ANY] * len(g),
        (scal, dx1, x, a1, un, p, o, a2, vec, *others, *pieces),
        [WA, WC, pltpu.VMEM((T, FF), BF), pltpu.VMEM((T, 1024), BF), pltpu.VMEM((T, D), BF), *vblk, pltpu.SemaphoreType.DMA((64,))],
        cost_estimate=cost(2 * T * D * FF * 8, 2 * WBYTES + 8e6),
        name="attn_bwd",
        mib=64,
    )
    return res[:2], res[2:]


def shift(n, k):
    return [(i, (i + k) % n) for i in range(n)]


class Ring:
    def __init__(self, dp, fsdp):
        self.X = fsdp // 2
        self.Z = dp // self.X
        self.dp, self.fsdp = dp, fsdp

    def z(self, v, k):
        return lax.ppermute(v, "dp", [(z * self.X + x, (z + k) % self.Z * self.X + x) for z in range(self.Z) for x in range(self.X)])

    def z_xor(self, v, k):
        return lax.ppermute(v, "dp", [(i, i ^ (k * self.X)) for i in range(self.dp)])

    def x(self, v):
        return lax.ppermute(v, "dp", [(i, i ^ 1) for i in range(self.dp)])

    def y(self, v):
        return lax.ppermute(v, "fsdp", [(i, i ^ 2) for i in range(self.fsdp)])

    def c(self, v):
        return lax.ppermute(v, "fsdp", [(i, i ^ 1) for i in range(self.fsdp)])


def pack_a_kernel(l, wqkv, wo, out):
    out[...] = jnp.concatenate([wqkv[l], wo[l]], axis=1)


def pack_a(seq, l, wqkv, wo):
    return seq(
        functools.partial(pack_a_kernel, l),
        [S((96, D), BF)],
        [VMEM] * 2,
        [VMEM],
        (wqkv, wo),
        cost_estimate=cost(0, 4 * 96 * D),
        name="pack_a",
    )[0]


def pack_bc_rows(l, w1, w2, out, first, second):
    t = w2[l].T
    for i, at in enumerate((first, second)):
        out[at : at + 48] = w1[l, 48 * i : 48 * i + 48]
        for j in range(2):
            out[at + 48 : at + 96, 384 * j : 384 * j + 384] = t[96 * j + 48 * i : 96 * j + 48 * i + 48]


def pack_vec_kernel(w1, w2, ng, bi, hg, hb, out):
    def column(v, u, w, first):
        v = jnp.concatenate([v.astype(F32), u.astype(F32)], axis=0)
        parts = [jnp.zeros((first, w), F32)] if first else []
        return jnp.concatenate(parts + [v, jnp.zeros((VROWS - first - v.shape[0], w), F32)], axis=0)

    pack_bc_rows(0, w1, w2, out, 0, 112)
    low = [column(ng[i], bi[i], 96, 0) for i in range(LAYERS)]
    hid = [column(hg[i], hb[i], 384, HROW) for i in range(LAYERS)]
    low = jnp.concatenate(low + [jnp.zeros((VROWS, 576), F32)], axis=1)
    out[96:112] = (low + jnp.concatenate(hid, axis=1)).astype(BF)
    out[208:224] = jnp.zeros((VROWS, D), BF)


def pack_vec(seq, w1, w2, vectors):
    return seq(
        pack_vec_kernel,
        [S((224, D), BF)],
        [VMEM] * 6,
        [VMEM],
        (w1, w2, *vectors),
        cost_estimate=cost(0, 4 * 224 * D),
        name="pack_vec",
    )[0]


def pack_all_kernel(l, wqkv, wo, w1, w2, out):
    a = jnp.concatenate([wqkv[l], wo[l]], axis=1)
    out[0:48] = a[0:48]
    out[144:192] = a[48:96]
    pack_bc_rows(l, w1, w2, out, 48, 192)


def pack_all(seq, l, weights):
    return seq(
        functools.partial(pack_all_kernel, l),
        [S((288, D), BF)],
        [VMEM] * 4,
        [VMEM],
        weights,
        cost_estimate=cost(0, 4 * 288 * D),
        name="pack_all",
    )[0]


def zcat_kernel(r1, scal, p0, p1, p2, p3, o1, o2):
    for k, ref in enumerate((p0, p1, p2, p3)):
        z = lax.rem(scal[2] + 4 - k, 4)
        o1[z] = ref[0:r1]
        o2[z] = ref[r1:]


def zcat(seq, scal, parts, r1):
    r2 = parts[0].shape[0] - r1
    return seq(
        functools.partial(zcat_kernel, r1),
        (S((4, r1, D), BF), S((4, r2, D), BF)),
        [SMEM] + [VMEM] * 4,
        [VMEM] * 2,
        (scal, *parts),
        cost_estimate=cost(0, 8 * (r1 + r2) * D * 2),
        name="zcat",
    )


def pile_kernel(first, rows, h1, x1, h2, y2, o1, o2):
    mine = pl.ds(first, rows)
    o1[0] = h1[:, mine]
    o1[1] = x1[:, mine]
    o2[0] = h2[:, mine]
    o2[1] = y2[:, mine]


def pile(seq, first, rows, parts):
    return seq(
        functools.partial(pile_kernel, first, rows),
        [S((2, 4, rows, D), BF)] * 2,
        [VMEM] * 4,
        [VMEM] * 2,
        parts,
        cost_estimate=cost(0, 64 * rows * D),
        name="pile",
    )


def merge_kernel(*refs):
    for i, ref in enumerate(refs[:-1]):
        refs[-1][i] = ref[...]


def merge(seq, *parts):
    shape = (len(parts), *parts[0].shape)
    return seq(merge_kernel, [S(shape, BF)], [VMEM] * len(parts), [VMEM], parts, cost_estimate=cost(0, 4 * math.prod(shape)), name="merge")[0]


def total(refs):
    out = refs[0].astype(F32)
    for r in refs[1:]:
        out = out + r.astype(F32)
    return out


class Sums:
    def __init__(self, scal):
        self.scal = scal
        self.arrays = []
        self.outs = []
        self.sums = []

    def source(self, array):
        for i, v in enumerate(self.arrays):
            if v is array:
                return i
        self.arrays.append(array)
        return len(self.arrays) - 1

    def out(self, *shape):
        self.outs.append(shape)
        return len(self.outs) - 1

    def add(self, out, where, sources, rows):
        self.sums.append((out, where, [(self.source(v), at, deep) for v, at, deep in sources], rows))

    def run(self, seq, name):
        n, q = len(self.arrays), len(self.outs)
        copies = sum(len(v[2]) for v in self.sums)
        sums = self.sums

        def kernel(scal, *refs):
            arrays, outs = refs[:n], refs[n : n + q]
            ins, made, sems = refs[n + q : n + q + copies], refs[n + q + copies : -1], refs[-1]
            pairs = [(arrays[i].at[at(scal)], ins[j]) for j, (i, at, _) in enumerate(v for t in sums for v in t[2])]
            loads = start(pairs, sems)
            saves, first = [], 0
            for t, (out, where, sources, rows) in enumerate(sums):
                mine = range(first, first + len(sources))
                first += len(sources)
                wait([loads[j] for j in mine])
                made[t][...] = total([ins[j][...].reshape(rows, D) for j in mine]).astype(BF)
                saves += start([(made[t], outs[out].at[where(scal)])], sems, copies + t)
            wait(saves)

        scratch = [pltpu.VMEM((4, t[3] // 4, D) if deep else (t[3], D), BF) for t in sums for _, _, deep in t[2]]
        scratch += [pltpu.VMEM((t[3], D), BF) for t in sums]
        return seq(
            kernel,
            [S((*v, D), BF) for v in self.outs],
            [SMEM] + [ANY] * n,
            [ANY] * q,
            (self.scal, *self.arrays),
            scratch + [pltpu.SemaphoreType.DMA((copies + len(sums),))],
            cost_estimate=cost(0, 2 * D * sum(t[3] * (1 + len(t[2])) for t in sums)),
            name=name,
            mib=64,
        )


def finish_kernel(scal, *refs):
    keep_bc, got_bc, keep_a, got_a, last = refs[:5]
    in_out, out_out, up_out, down_out, vec_out = refs[13:]
    i = lax.rem(scal[2], 2)
    upper = total([keep_bc[i], got_bc[i], last[0:192]])
    a1 = total([keep_a[i], got_a[i], last[192:]])
    lower = total([r[...] for r in refs[5:9]])
    rows_a = total([r[...] for r in refs[9:13]])
    vec_out[0:VROWS] = rows_a[48:64]
    vec_out[VROWS:] = rows_a[112:128]
    a0 = jnp.concatenate([rows_a[:48], rows_a[64:112]], axis=0)
    for l, a, bc in ((0, a0, lower), (1, a1, upper)):
        in_out[l] = a[:, :576]
        out_out[l] = a[:, 576:]
        up_out[l, 0:48] = bc[0:48]
        up_out[l, 48:96] = bc[96:144]
        c = jnp.concatenate([bc[48:96], bc[144:192]], axis=0)
        for j in range(2):
            down_out[l, :, 96 * j : 96 * j + 96] = c[:, 384 * j : 384 * j + 384].T


def finish(seq, scal, parts):
    return seq(
        finish_kernel,
        [S((2, 96, 576), F32), S((2, 96, 192), F32), S((2, 96, D), F32), S((2, 384, 192), F32), S((2 * VROWS, D), F32)],
        [SMEM] + [VMEM] * len(parts),
        [VMEM] * 5,
        (scal, *parts),
        cost_estimate=cost(0, 8e6),
        name="finish",
    )


class Gather:
    def __init__(self, seq, ring, scal):
        self.seq, self.ring, self.scal = seq, ring, scal

    def z_all(self, pack):
        self.parts = [pack] + [self.ring.z(pack, k) for k in (1, 2, 3)]

    def xy_first(self):
        h1, h2 = zcat(self.seq, self.scal, self.parts, self.parts[0].shape[0] // 2)
        self.both = h1, self.ring.x(h1), h2, self.ring.y(h2)

    def xy_second(self, both, first, rows):
        self.h1, self.h2 = pile(self.seq, first, rows, both)
        self.y1, self.x2 = self.ring.y(self.h1), self.ring.x(self.h2)

    def core(self):
        both = self.ring.c(merge(self.seq, self.h1, self.y1, self.h2, self.x2))
        self.other = [(both, i) for i in range(4)]
        return both

    def core_own(self):
        self.own = self.ring.c(self.h1), self.ring.c(self.h2)
        return self.own

    def core_got(self):
        both = self.ring.c(merge(self.seq, self.y1, self.x2))
        self.other = [self.own[0], (both, 0), self.own[1], (both, 1)]
        return both

    def pieces(self):
        return [self.h1, self.y1, *self.other[:2], self.h2, self.x2, *self.other[2:]]


def rows_at(first, rows):
    return lambda scal: (pl.ds(first, rows),)


class Scatter:
    def __init__(self, ring, grads):
        self.ring = ring
        self.keep, self.send = grads
        self.rows = self.keep.shape[4]

    def core(self, send):
        self.got = self.ring.c(send)
        return self.got

    def both(self, *index):
        return [(v, lambda scal: index, True) for v in (self.keep, self.got)]

    def first(self, sums, x, y, at=0):
        self.at1 = at
        r = 4 * self.rows
        for h, out in ((0, x), (1, y)):
            for s in range(2):
                sums.add(out, rows_at(at + s * r, r), self.both(h, 1, s), r)

    def second(self, sums, x, y, at=0):
        self.at2 = at
        r = 4 * self.rows
        for h, got, out in ((0, self.x1st, y), (1, self.y1st, x)):
            sums.add(out, rows_at(at, r), self.both(h, 0, 1) + [(got, rows_at(self.at1 + r, r), False)], r)

    def block(self, sums, out, where, z):
        n = self.rows
        for h, a, b in ((0, self.x1st, self.y2nd), (1, self.y1st, self.x2nd)):

            def local(scal, h=h):
                return (h, 0, 0, z(scal))

            def sent(first):
                return lambda scal: (pl.ds(pl.multiple_of(first + z(scal) * n, 16), n),)

            sources = [(v, local, False) for v in (self.keep, self.got)]
            sources += [(a, sent(self.at1), False), (b, sent(self.at2), False)]
            sums.add(out, where(h * n, n), sources, n)

    def third_pair(self, sums):
        outs = [sums.out(2, 2 * self.rows) for _ in range(2)]
        for k in (1, 0):
            for i in range(2):

                def z(scal, k=k, i=i):
                    high = scal[2] // 2
                    return 2 * (1 - high if k else high) + i

                self.block(sums, outs[k], lambda first, n, i=i: lambda scal: (i, pl.ds(first, n)), z)
        return outs

    def third_direct(self, sums):
        outs = [sums.out(2 * self.rows) for _ in range(4)]
        for k in (1, 2, 3, 0):
            self.block(sums, outs[k], rows_at, lambda scal, k=k: lax.rem(scal[2] + k, 4))
        return outs


def fourth(sums, out, at, keep, got):
    rows = keep.shape[1]
    where = lambda scal: (1 - lax.rem(scal[2], 2),)
    sums.add(out, rows_at(at, rows), [(keep, where, False), (got, where, False)], rows)


def unpack_vec(rows):
    rows = rows.astype(F32)
    vecs, hids = [], []
    for l in range(LAYERS):
        v = rows[:, :, 96 * l : 96 * l + 96].transpose(1, 0, 2).reshape(VROWS, D)
        h = rows[:, :, 384 * l : 384 * l + 384].transpose(1, 0, 2).reshape(VROWS, FF)
        vecs.append(v)
        hids.append(h)
    return vecs, hids


def proj_bias(vec):
    full = jnp.concatenate([vec[BQ], jnp.zeros((D,), F32), vec[BV]]).reshape(4, 9 * HD)
    return jnp.concatenate(
        [full[:, :512].reshape(2048), jnp.pad(full[:, 512:], ((0, 0), (0, 64))).reshape(512)]
    ).reshape(1, 2560)


def fast_shards(ring, inputs, lengths, in_projection, out_projection, up_weight, down_weight, norm_gains, biases, hidden_gains, hidden_biases, cotangent):
    plan = Plan(True)
    seq = Seq(True)
    dpi, fi = lax.axis_index("dp"), lax.axis_index("fsdp")
    xme = dpi % ring.X
    place = jnp.stack([dpi // ring.X, xme, fi // 2, fi % 2]).astype(jnp.int32)
    scal = jnp.concatenate([lengths[0], place, jnp.zeros((2,), jnp.int32)])

    a, b, c, d, e = (Gather(seq, ring, scal) for _ in range(5))
    a.z_all(pack_a(seq, 0, in_projection, out_projection))
    cd = pack_all(seq, 1, (in_projection, out_projection, up_weight, down_weight))
    a.xy_first()
    b.z_all(pack_vec(seq, up_weight, down_weight, (norm_gains, biases, hidden_gains, hidden_biases)))
    seq.hold(b.parts[1])
    a.xy_second(a.both, 0, 48)
    seq.hold(a.y1, a.x2)
    b.xy_first()
    c.z_all(cd)
    seq.hold(a.core(), c.parts[3])
    b.xy_second(b.both, 0, 112)
    rows = b.h1[:, :, 96:112]
    rows = jnp.where(xme == 0, rows, rows[::-1]).transpose(1, 0, 2, 3).reshape(8, VROWS, D)
    vecs, hids = unpack_vec(rows)
    pb = [proj_bias(v) for v in vecs]
    kept = [None, None]
    x = inputs
    x1, a1, un, p, o, a2 = call_attn_fwd(seq, plan, scal, x, vecs[0], pb[0], a.pieces(), 0)
    seq.hold(b.y1, b.x2, *b.core_own())
    c.xy_first()
    c.xy_second(c.both, 0, 48)
    d.xy_second(c.both, 48, 48)
    e.xy_second(c.both, 96, 48)
    b.core_got()
    x2, a3, sl, n4, a4 = call_ff_fwd(seq, plan, scal, x1, vecs[0], hids[0], b.pieces(), 0, 1, False)
    kept[0] = (x, x1, a1, un, p, o, a2, a3, sl, n4, a4)
    x = x2
    seq.hold(d.y1, d.x2)
    c.core()
    d.core()
    x1, a1, un, p, o, a2 = call_attn_fwd(seq, plan, scal, x, vecs[1], pb[1], c.pieces(), 0)
    e.core_own()
    e.core_got()
    outputs, a3, sl, n4, a4 = call_ff_fwd(seq, plan, scal, x1, vecs[1], hids[1], d.pieces() + e.pieces(), 0, 0, True)

    (dx1, gva1, gh1), grads = call_ff_bwd(seq, plan, scal, cotangent, x1, a3, sl, n4, a4, vecs[1], hids[1], d.pieces() + e.pieces(), 0, 0, True)
    s1 = Scatter(ring, grads)
    s1.core(s1.send)
    (dy, gvb1), grads = call_attn_bwd(seq, plan, scal, dx1, x, a1, un, p, o, a2, vecs[1], c.pieces(), 0, ())
    s2 = Scatter(ring, grads)

    sums = Sums(scal)
    outs = sums.out(768), sums.out(768)
    s1.first(sums, *outs)
    seq.carry(s2.send)
    u, v = sums.run(seq, "sums_1")
    s2.core(*seq.carried)
    s1.x1st, s1.y1st = ring.x(u), ring.y(v)

    x, x1, a1, un, p, o, a2, a3, sl, n4, a4 = kept[0]
    (dx1, gva0, gh0), grads = call_ff_bwd(seq, plan, scal, dy, x1, a3, sl, n4, a4, vecs[0], hids[0], b.pieces(), 0, 1, False)
    s3 = Scatter(ring, grads)

    sums = Sums(scal)
    outs = sums.out(768), sums.out(768)
    s2.first(sums, *outs)
    s1.second(sums, *outs, 384)
    seq.carry(s3.send)
    u, v = sums.run(seq, "sums_2")
    s3.core(*seq.carried)
    s2.x1st, s2.y1st = s1.x2nd, s1.y2nd = ring.x(u), ring.y(v)

    others = (gva0, gva1, gvb1, gh0, gh1)
    (input_gradient, _), grads = call_attn_bwd(seq, plan, scal, dx1, x, a1, un, p, o, a2, vecs[0], a.pieces(), 0, others)
    s4 = Scatter(ring, grads)

    sums = Sums(scal)
    outs = sums.out(960), sums.out(960)
    s2.second(sums, *outs)
    s3.first(sums, *outs, 192)
    s1.third_pair(sums)
    seq.carry(s4.send)
    u, v, keep1, send1 = sums.run(seq, "sums_3")
    s4.core(*seq.carried)
    s3.x1st, s3.y1st = s2.x2nd, s2.y2nd = ring.x(u), ring.y(v)
    got1 = ring.z_xor(send1, 2)

    sums = Sums(scal)
    outs = sums.out(384), sums.out(384)
    s3.second(sums, *outs)
    s2.third_pair(sums)
    seq.hold(got1)
    u, v, keep2, send2 = sums.run(seq, "sums_4")
    s3.x2nd, s3.y2nd = ring.x(u), ring.y(v)
    got2 = ring.z_xor(send2, 2)

    sums = Sums(scal)
    s3.third_direct(sums)
    outs = sums.out(512), sums.out(512)
    s4.first(sums, *outs)
    seq.hold(got2)
    *parts3, u, v = sums.run(seq, "sums_5")
    parts3 = parts3[:1] + [ring.z(parts3[k], k) for k in (1, 2, 3)]
    s4.x1st, s4.y1st = ring.x(u), ring.y(v)

    sums = Sums(scal)
    outs = sums.out(256), sums.out(256)
    s4.second(sums, *outs)
    seq.hold(*parts3[1:3])
    u, v = sums.run(seq, "sums_6")
    s4.x2nd, s4.y2nd = ring.x(u), ring.y(v)

    sums = Sums(scal)
    s4.third_direct(sums)
    out = sums.out(288)
    fourth(sums, out, 0, keep1, got1)
    fourth(sums, out, 192, keep2, got2)
    seq.hold(parts3[3])
    res = sums.run(seq, "sums_7")
    parts4 = [res[0]] + [ring.z(res[k], k) for k in (1, 2, 3)]
    last = ring.z_xor(res[4], 1)
    g_in, g_out, g_up, g_down, vrows = finish(seq, scal, [keep1, got1, keep2, got2, last, *parts3, *parts4])
    gv = jnp.stack([vrows[:10, :96], vrows[:10, 96:192]])
    gh = jnp.stack([vrows[26:29, :384], vrows[26:29, 384:]])
    return outputs, input_gradient, g_in, g_out, g_up, g_down, gv[:, :3], gv[:, 3:], gh[:, :1], gh[:, 1:]


def whole_shards(inputs, lengths, in_projection, out_projection, up_weight, down_weight, norm_gains, biases, hidden_gains, hidden_biases, cotangent):
    plan = Plan(False)
    seq = Seq(False)
    scal = jnp.concatenate([lengths[0], jnp.zeros((6,), jnp.int32)])

    def full(w):
        return lax.all_gather(lax.all_gather(w, "fsdp", axis=1, tiled=True), "dp", axis=0, tiled=True)

    def rows(v, width):
        return jnp.pad(lax.all_gather(v, "dp", axis=1, tiled=True).astype(F32), ((0, VROWS - v.shape[0]), (0, 0)))

    vecs, hids, pieces = [], [], []
    for l in range(LAYERS):
        qkv = full(in_projection[l]).reshape(D, 4, 9 * HD)
        out = full(out_projection[l]).reshape(D, 4, 192)
        a = jnp.concatenate([qkv[:, :, :512].reshape(D, 2048), jnp.concatenate([qkv[:, :, 512:], out], axis=2).reshape(D, 1024)], axis=1)
        b = full(up_weight[l])
        c = full(down_weight[l]).reshape(4, D, D).transpose(0, 2, 1)
        shape = (4, 2, 2, 48, FF)
        got = [a.reshape(shape), b.reshape(shape), c.reshape(4, 4, 2, 2, 48, D)]
        pieces.append(got)
        vecs.append(rows(jnp.concatenate([norm_gains[l], biases[l]], axis=0), D))
        hid = rows(jnp.concatenate([hidden_gains[l], hidden_biases[l]], axis=0), FF)
        hids.append(jnp.roll(hid, HROW, axis=0))
    pb = [proj_bias(v) for v in vecs]
    x = inputs
    kept = []
    for l in range(LAYERS):
        x1, a1, un, p, o, a2 = call_attn_fwd(seq, plan, scal, x, vecs[l], pb[l], pieces[l], 0)
        x2, a3, sl, n4, a4 = call_ff_fwd(seq, plan, scal, x1, vecs[l], hids[l], pieces[l], 0, 0, l == LAYERS - 1)
        kept.append((x, x1, a1, un, p, o, a2, a3, sl, n4, a4))
        x = x2
    outputs = x
    dy = cotangent
    layer_grads = [None] * LAYERS
    for l in reversed(range(LAYERS)):
        x, x1, a1, un, p, o, a2, a3, sl, n4, a4 = kept[l]
        last = l == LAYERS - 1
        (dx1, gva, gh), (gb, gc) = call_ff_bwd(seq, plan, scal, dy, x1, a3, sl, n4, a4, vecs[l], hids[l], pieces[l], 0, 0, last)
        (dy, gvb), (ga,) = call_attn_bwd(seq, plan, scal, dx1, x, a1, un, p, o, a2, vecs[l], pieces[l], 0, ())
        layer_grads[l] = (ga, gb, gc, gva + gvb, gh)

    def scatter(g):
        g = lax.psum_scatter(g.astype(BF), "dp", scatter_dimension=0, tiled=True)
        return lax.psum_scatter(g, "fsdp", scatter_dimension=1, tiled=True).astype(F32)

    def scatter_rows(v):
        v = lax.psum_scatter(v.astype(BF), "dp", scatter_dimension=1, tiled=True).astype(F32)
        return lax.psum(v, "fsdp")

    res = []
    for l in range(LAYERS):
        ga, gb, gc, gv, gh = layer_grads[l]
        ga = ga.reshape(4, D, D).transpose(1, 0, 2)
        gv = scatter_rows(gv[:10])
        gh = scatter_rows(gh[HROW : HROW + 3])
        res.append(
            (
                scatter(ga[:, :, :576].reshape(D, 3 * D)),
                scatter(ga[:, :, 576:].reshape(D, D)),
                scatter(gb.reshape(4, D, D).transpose(1, 0, 2).reshape(D, FF)),
                scatter(gc.reshape(4, D, D).transpose(0, 2, 1).reshape(FF, D)),
                gv[:3],
                gv[3:],
                gh[:1],
                gh[1:],
            )
        )
    return (outputs, dy, *(jnp.stack([r[i] for r in res]) for i in range(8)))


def solution(mesh):
    dp, fsdp = mesh.shape["dp"], mesh.shape["fsdp"]
    both = P(("dp", "fsdp"), None)
    mat = P(None, "dp", "fsdp")
    row = P(None, None, "dp")
    ring = Ring(dp, fsdp)
    shards = functools.partial(fast_shards, ring) if (dp, fsdp) == (8, 4) else whole_shards
    return jax.shard_map(
        shards,
        mesh=mesh,
        in_specs=(both, both, mat, mat, mat, mat, row, row, row, row, both),
        out_specs=(both, both, mat, mat, mat, mat, row, row, row, row),
        check_vma=False,
    )
```

```python
import functools
import math

import jax
import jax.numpy as jnp
from jax import lax
from jax.experimental import pallas as pl
from jax.experimental.pallas import tpu as pltpu
from jax.sharding import PartitionSpec as P

HEADS = 12
HD = 64
LAYERS = 2
SEQS = 2
D = 768
FF = 3072
T = 256
EPS = 1e-05
BF = jnp.bfloat16
F32 = jnp.float32
MIB = 1 << 20

ANY = pl.BlockSpec(memory_space=pltpu.HBM)
SMEM = pl.BlockSpec(memory_space=pltpu.SMEM)
VMEM = pl.BlockSpec(memory_space=pltpu.VMEM)
LAZY = object()


class Lazy:
    def __init__(self, far, near, sem, out):
        self.near = near
        self.copy = pltpu.make_async_copy(near, far, sem) if out else pltpu.make_async_copy(far, near, sem)
        self.flying = False

    def begin(self):
        self.copy.start()
        self.flying = True

    def ready(self):
        if self.flying:
            self.copy.wait()
            self.flying = False
        return self.near


def begin(*operands):
    for v in operands:
        v.begin()

G1, G2, G3, C1, BQ, BV, C2, BO, C3, B2 = range(10)
VROWS = 16
HROW = 10
G4, B1, C4 = 10, 11, 12

RB = 32


def dot(a, b):
    return jnp.dot(a, b, preferred_element_type=F32)


def dot_nt(a, b):
    return lax.dot_general(a, b, (((1,), (1,)), ((), ())), preferred_element_type=F32)


def unit_lane(u):
    f, j = divmod(u, 9)
    return 512 * f + 64 * j if j < 8 else 2048 + 128 * f


def ln_stats(v):
    m = jnp.mean(v, axis=-1, keepdims=True)
    cen = v - m
    inv = lax.rsqrt(jnp.mean(cen * cen, axis=-1, keepdims=True) + EPS)
    return cen * inv, inv


def ln_back(dn, g, n, inv):
    e = dn * g
    dv = inv * (e - jnp.mean(e, axis=-1, keepdims=True) - n * jnp.mean(e * n, axis=-1, keepdims=True))
    return dv, jnp.sum(dn * n, axis=0, keepdims=True), jnp.sum(dn, axis=0, keepdims=True)


def seg_of(scal, places):
    e0 = scal[0]
    e1 = scal[0] + scal[1]
    return (places >= e0).astype(jnp.int32) + (places >= e1).astype(jnp.int32)


class Plan:
    def __init__(self, fast):
        self.fast = fast

    def load_a(self, scal, pieces, m, dst):
        if not self.fast:
            return [(pieces[0], dst)]
        out = []
        for h, ri, x, f, ref in self._pieces(scal, pieces):
            src = ref.at[ri, :, pl.ds(m * 48, 48)]
            out.append((src.at[:, :, pl.ds(0, 512)], dst.at[:, x, h, :, pl.ds(pl.multiple_of(f * 512, 512), 512)]))
            out.append((src.at[:, :, pl.ds(512, 256)], dst.at[:, x, h, :, pl.ds(pl.multiple_of(2048 + f * 256, 256), 256)]))
        return out

    def load_b(self, scal, pieces, m, dst):
        if not self.fast:
            return [(pieces[1], dst)]
        return [
            (ref.at[ri, :, pl.ds(m * 48, 48)], dst.at[:, x, h, :, pl.ds(pl.multiple_of(f * 768, 768), 768)])
            for h, ri, x, f, ref in self._pieces(scal, pieces)
        ]

    def load_c(self, scal, pieces, m, dst):
        if not self.fast:
            return [(pieces[2], dst)]
        pieces = pieces[-8:]
        return [
            (
                ref.at[ri, :, pl.ds(m * 48, 48), pl.ds(j * 384, 384)],
                dst.at[:, f, j, h, :, pl.ds(pl.multiple_of(x * 384, 384), 384)],
            )
            for h, ri, x, f, ref in self._pieces(scal, pieces)
            for j in range(2)
        ]

    def _pieces(self, scal, pieces):
        mx, my, mc = scal[3], scal[4], scal[5]
        for h in range(2):
            for bi in range(4):
                ro, rc = bi % 2, bi // 2
                for ri in range(2):
                    rx, ry = (ri, ro) if h == 0 else (ro, ri)
                    x = lax.rem(mx + rx, 2)
                    y = lax.rem(my + ry, 2)
                    c = lax.rem(mc + rc, 2)
                    yield h, ri, x, y * 2 + c, pieces[h * 4 + bi]


    def blocks(self, scal):
        if not self.fast:
            return [(f, 0, 0) for f in range(4)]
        my, mc = scal[4], scal[5]
        return [(lax.rem(my + ry, 2) * 2 + lax.rem(mc + rc, 2), rc, ry) for rc in (1, 0) for ry in (1, 0)]

    def store_ab(self, scal, src, outs, m, f, rc, ry):
        if not self.fast:
            return [(src, outs[0].at[f])]
        res = []
        for rx in range(2):
            x = lax.rem(scal[3] + rx, 2)
            for h in range(2):
                first, second = (rx, ry) if h == 0 else (ry, rx)
                res.append((src.at[:, x, h], outs[rc].at[h, first, second, :, pl.ds(m * 48, 48)]))
        return res

    def store_c(self, scal, src, outs, m):
        if not self.fast:
            return [(src, outs[1])]
        res = []
        for f, rc, ry in self.blocks(scal):
            for rx in range(2):
                x = lax.rem(scal[3] + rx, 2)
                for h in range(2):
                    first, second = (rx, ry) if h == 0 else (ry, rx)
                    for j in range(2):
                        res.append(
                            (
                                src.at[:, f, j, h, :, pl.ds(pl.multiple_of(x * 384, 384), 384)],
                                outs[rc].at[h, first, second, :, pl.ds(m * 48, 48), pl.ds(j * 384, 384)],
                            )
                        )
        return res

    def store_vec(self, scal, src, outs):
        res = []
        for _, rc, ry in self.blocks(scal):
            for rx in range(2):
                x = lax.rem(scal[3] + rx, 2)
                for h in range(2):
                    first, second = (rx, ry) if h == 0 else (ry, rx)
                    res.append((src.at[h, :, x], outs[rc].at[h, first, second, :, pl.ds(48, 16)]))
        return res


def flat(pieces):
    arrays, finds = [], []
    for piece in pieces:
        array, index = piece if isinstance(piece, tuple) else (piece, None)
        place = next((i for i, v in enumerate(arrays) if v is array), len(arrays))
        if place == len(arrays):
            arrays.append(array)
        finds.append((place, index))
    return arrays, lambda refs: [refs[i] if j is None else refs[i].at[j] for i, j in finds]


def start(copies, sems, base=0):
    made = [pltpu.make_async_copy(s, d, sems.at[base + i]) for i, (s, d) in enumerate(copies)]
    for c in made:
        c.start()
    return made


def wait(made):
    for c in made:
        c.wait()


def attn_fwd(plan, npieces, find, m, *refs):
    scal, x_in, vec_in, pb_in = refs[:4]
    pieces = find(refs[4 : 4 + npieces])
    x1_out, a1_out, un_out, p_out, o_out, a2_out = refs[4 + npieces : 10 + npieces]
    wa, sems = refs[10 + npieces :]
    begin(x_in, vec_in)
    loads = start(plan.load_a(scal, pieces, m, wa), sems)
    begin(pb_in)
    x_ref, vec_ref = x_in.ready(), vec_in.ready()
    n1, _ = ln_stats(x_ref[...])
    a1 = (n1 * vec_ref[G1 : G1 + 1] + vec_ref[C1 : C1 + 1]).astype(BF)
    a1_out.near[...] = a1
    a1_out.begin()
    seg_row = seg_of(scal, lax.broadcasted_iota(jnp.int32, (T, T), 1))
    seg_col = seg_of(scal, lax.broadcasted_iota(jnp.int32, (T, T), 0))
    same = seg_row == seg_col
    pb_ref, un_ref = pb_in.ready(), un_out.near
    wait(loads)
    for f in range(4):
        part = dot(a1, wa[:, :, :, :, 512 * f : 512 * f + 512].reshape(D, 512)) + pb_ref[0:1, 512 * f : 512 * f + 512]
        last = dot(a1, wa[:, :, :, :, 2048 + 256 * f : 2176 + 256 * f].reshape(D, 128)) + pb_ref[0:1, 2048 + 128 * f : 2176 + 128 * f]
        for j in range(9):
            u = 9 * f + j
            val = part[:, 64 * j : 64 * j + 64] if j < 8 else last[:, 0:64]
            val = val.astype(BF)
            if u < HEADS:
                val = val * BF(0.125)
            un_ref[u] = val
    un_out.begin()
    o_ref = o_out.near
    for h in range(HEADS):
        s = jnp.where(same, dot_nt(un_ref[h], un_ref[HEADS + h]), -1e30)
        ex = jnp.exp(s - jnp.max(s, axis=-1, keepdims=True))
        p = ex * (1.0 / jnp.sum(ex, axis=-1, keepdims=True))
        p_out.near[h] = p
        o_ref[:, 64 * h : 64 * h + 64] = dot(p.astype(BF), un_ref[2 * HEADS + h])
    p_out.begin()
    o_out.begin()
    n2, _ = ln_stats(o_ref[...])
    a2 = (n2 * vec_ref[G2 : G2 + 1] + vec_ref[C2 : C2 + 1]).astype(BF)
    a2_out.near[...] = a2
    a2_out.begin()
    z = [dot(a2, wa[:, :, :, :, 2048 + 256 * f : 2304 + 256 * f].reshape(D, 256))[:, 64:] for f in range(4)]
    x1_out.near[...] = x_ref[...] + (jnp.concatenate(z, axis=1) + vec_ref[BO : BO + 1])
    x1_out.begin()


def hidden_rows(hid_ref, sl_ref, n4_ref, a4_ref):
    def rows_step(i, carry):
        rows = pl.ds(i * RB, RB)
        total = jnp.zeros((RB, 1), F32)
        for f in range(4):
            cols = slice(768 * f, 768 * f + 768)
            u = n4_ref[rows, cols]
            phi_c = 0.5 * (1.0 + lax.erf(u * (1.0 / math.sqrt(2.0))))
            r = u * phi_c
            sl_ref[rows, cols] = phi_c + u * (jnp.exp(-0.5 * u * u) * (1.0 / math.sqrt(2.0 * math.pi)))
            n4_ref[rows, cols] = r
            total += jnp.sum(r, axis=-1, keepdims=True)
        mean = total * (1.0 / FF)
        total = jnp.zeros((RB, 1), F32)
        for f in range(4):
            cols = slice(768 * f, 768 * f + 768)
            cen = n4_ref[rows, cols] - mean
            total += jnp.sum(cen * cen, axis=-1, keepdims=True)
        inv = lax.rsqrt(total * (1.0 / FF) + EPS)
        for f in range(4):
            cols = slice(768 * f, 768 * f + 768)
            n4 = (n4_ref[rows, cols] - mean) * inv
            n4_ref[rows, cols] = n4
            a4_ref[rows, cols] = (n4 * hid_ref[G4 : G4 + 1, cols] + hid_ref[C4 : C4 + 1, cols]).astype(BF)
            sl_ref[rows, cols] = sl_ref[rows, cols] * inv
        return carry

    lax.fori_loop(0, T // RB, rows_step, 0)


def hidden(x1_in, vec_in, hid_in, wb, load_b, a3_out, sl_out, n4_out, a4_out):
    x1_ref, vec_ref = x1_in.ready(), vec_in.ready()
    n3, _ = ln_stats(x1_ref[...])
    a3 = (n3 * vec_ref[G3 : G3 + 1] + vec_ref[C3 : C3 + 1]).astype(BF)
    a3_out.near[...] = a3
    a3_out.begin()
    hid_ref = hid_in.ready()
    n4_ref = n4_out.near
    wait(load_b)
    for f in range(4):
        cols = slice(768 * f, 768 * f + 768)
        n4_ref[:, cols] = dot(a3, wb[:, :, :, :, cols].reshape(D, 768)) + hid_ref[B1 : B1 + 1, cols]
    hidden_rows(hid_ref, sl_out.near, n4_ref, a4_out.near)
    begin(a4_out, n4_out, sl_out)


def down(x1_in, vec_in, a4_ref, wc):
    x1_ref, vec_ref = x1_in.ready(), vec_in.ready()
    acc = dot_nt(a4_ref[:, 0:768], wc[0].reshape(D, 768))
    for z in range(1, 4):
        acc += dot_nt(a4_ref[:, 768 * z : 768 * z + 768], wc[z].reshape(D, 768))
    return x1_ref[...] + (acc + vec_ref[B2 : B2 + 1])


def valid_rows(scal):
    seg = seg_of(scal, lax.broadcasted_iota(jnp.int32, (T, 1), 0))
    return (seg < SEQS).astype(F32)


def ff_fwd(plan, npieces, find, mb, mc, *refs):
    scal, x1_in, vec_in, hid_in = refs[:4]
    pieces = find(refs[4 : 4 + npieces])
    x2_out, a3_out, sl_out, n4_out, a4_out = refs[4 + npieces : 9 + npieces]
    wb, wc, sems = refs[9 + npieces :]
    begin(x1_in, vec_in)
    load_b = start(plan.load_b(scal, pieces, mb, wb), sems)
    begin(hid_in)
    load_c = start(plan.load_c(scal, pieces, mc, wc), sems, len(load_b))
    hidden(x1_in, vec_in, hid_in, wb, load_b, a3_out, sl_out, n4_out, a4_out)
    wait(load_c)
    x2_out.near[...] = down(x1_in, vec_in, a4_out.near, wc)
    x2_out.begin()


def ff_mid(plan, npieces, find, nouts, mb, *refs):
    scal, x1_in, dy_in, vec_in, hid_in = refs[:5]
    pieces = find(refs[5 : 5 + npieces])
    a3_out, sl_out, n4_out, a4_out = refs[5 + npieces : 9 + npieces]
    outs = refs[9 + npieces : 9 + npieces + nouts]
    wb, gc, sems = refs[9 + npieces + nouts :]
    begin(x1_in, vec_in)
    load_b = start(plan.load_b(scal, pieces, mb, wb), sems)
    begin(hid_in, dy_in)
    hidden(x1_in, vec_in, hid_in, wb, load_b, a3_out, sl_out, n4_out, a4_out)
    dz2t = (dy_in.ready()[...] * valid_rows(scal)).astype(BF).T
    for z in range(4):
        gc[z] = dot(dz2t, a4_out.near[:, 768 * z : 768 * z + 768]).astype(BF).reshape(4, 2, 2, 48, 768)
    wait(start(plan.store_c(scal, gc, outs, 0), sems, len(load_b)))


def down_grad(plan, nouts, *refs):
    scal, dy_in, a4_in = refs[:3]
    outs = refs[3 : 3 + nouts]
    gc, sems = refs[3 + nouts :]
    begin(dy_in, a4_in)
    dz2t = dy_in.ready()[...].astype(BF).T
    a4_ref = a4_in.ready()
    for z in range(4):
        gc[z] = dot(dz2t, a4_ref[:, 768 * z : 768 * z + 768]).astype(BF).reshape(4, 2, 2, 48, 768)
    wait(start(plan.store_c(scal, gc, outs, 0), sems))


def ff_out(plan, npieces, find, mc, *refs):
    scal, x1_in, a4_in, vec_in = refs[:4]
    pieces = find(refs[4 : 4 + npieces])
    out, wc, sems = refs[4 + npieces :]
    load_c = start(plan.load_c(scal, pieces, mc, wc), sems)
    begin(a4_in, x1_in, vec_in)
    wait(load_c)
    out.near[...] = down(x1_in, vec_in, a4_in.ready(), wc) * valid_rows(scal)
    out.begin()


def ff_bwd(plan, npieces, find, nouts, mb, mc, last, with_c, *refs):
    scal, dy_in, x1_in, a3_in, sl_in, n4_in, a4_in, vec_in, hid_in = refs[:9]
    pieces = find(refs[9 : 9 + npieces])
    dx1_out, gv_out, gh_out = refs[9 + npieces : 12 + npieces]
    outs = refs[12 + npieces : 12 + npieces + nouts]
    wb, wc, gb, da4, du_ref, sems = refs[12 + npieces + nouts : 18 + npieces + nouts]
    gc = refs[18 + npieces + nouts] if with_c else None
    begin(dy_in)
    load_c = start(plan.load_c(scal, pieces, mc, wc), sems)
    if with_c:
        begin(a4_in)
    begin(n4_in, hid_in, sl_in)
    load_b = start(plan.load_b(scal, pieces, mb, wb), sems, len(load_c))
    begin(a3_in, x1_in, vec_in)
    base = len(load_c) + len(load_b)
    gv_ref, gh_ref = gv_out.near, gh_out.near
    dy = dy_in.ready()[...]
    if last:
        dy = dy * valid_rows(scal)
    dz2 = dy.astype(BF)
    gv_ref[...] = jnp.zeros_like(gv_ref)
    gh_ref[...] = jnp.zeros_like(gh_ref)
    gv_ref[B2 : B2 + 1] = jnp.sum(dz2.astype(F32), axis=0, keepdims=True)
    dz2t = dz2.T if with_c else None
    wait(load_c)
    for z in range(4):
        cols = slice(768 * z, 768 * z + 768)
        da4[:, cols] = dot(dz2, wc[z].reshape(D, 768))
        if with_c:
            gc[z] = dot(dz2t, a4_in.ready()[:, cols]).astype(BF).reshape(4, 2, 2, 48, 768)
    saves = start(plan.store_c(scal, gc, outs, 1), sems, base) if with_c else []
    base += len(saves)
    n4_ref, hid_ref, sl_ref = n4_in.ready(), hid_in.ready(), sl_in.ready()

    def rows_step(i, carry):
        rows = pl.ds(i * RB, RB)
        s1 = jnp.zeros((RB, 1), F32)
        s2 = jnp.zeros((RB, 1), F32)
        for z in range(4):
            cols = slice(768 * z, 768 * z + 768)
            da = da4[rows, cols]
            n4 = n4_ref[rows, cols]
            dn = da * n4
            e = da * hid_ref[G4 : G4 + 1, cols]
            da4[rows, cols] = e
            s1 += jnp.sum(e, axis=-1, keepdims=True)
            s2 += jnp.sum(e * n4, axis=-1, keepdims=True)
            gh_ref[G4 : G4 + 1, cols] += jnp.sum(dn, axis=0, keepdims=True)
            gh_ref[C4 : C4 + 1, cols] += jnp.sum(da, axis=0, keepdims=True)
        s1 = s1 * (1.0 / FF)
        s2 = s2 * (1.0 / FF)
        for z in range(4):
            cols = slice(768 * z, 768 * z + 768)
            du = (sl_ref[rows, cols] * (da4[rows, cols] - s1 - n4_ref[rows, cols] * s2)).astype(BF)
            du_ref[rows, cols] = du
            gh_ref[B1 : B1 + 1, cols] += jnp.sum(du.astype(F32), axis=0, keepdims=True)
        return carry

    lax.fori_loop(0, T // RB, rows_step, 0)
    gh_out.begin()
    a3t = a3_in.ready()[...].T
    wait(load_b)
    da3 = jnp.zeros((T, D), F32)
    for i, (f, rc, ry) in enumerate(plan.blocks(scal)):
        cols = pl.ds(pl.multiple_of(f * 768, 768), 768)
        du = du_ref[:, cols]
        gb[i] = dot(a3t, du).astype(BF).reshape(4, 2, 2, 48, 768)
        more = start(plan.store_ab(scal, gb.at[i], outs, 0, f, rc, ry), sems, base)
        base += len(more)
        saves += more
        da3 += dot_nt(du, wb[:, :, :, :, cols].reshape(D, 768))
    n3, inv3 = ln_stats(x1_in.ready()[...])
    vec_ref = vec_in.ready()
    part, dg3, dc3 = ln_back(da3, vec_ref[G3 : G3 + 1], n3, inv3)
    gv_ref[G3 : G3 + 1] = dg3
    gv_ref[C3 : C3 + 1] = dc3
    dx1_out.near[...] = dy + part
    begin(dx1_out, gv_out)
    wait(saves)


def attn_bwd(plan, npieces, find, nouts, m, fold, *refs):
    scal, dx1_in, x_in, a1_in, un_in, p_in, o_in, a2_in, vec_in = refs[:9]
    pos = 9
    others = refs[pos : pos + (5 if fold else 0)]
    pos += len(others)
    pieces = find(refs[pos : pos + npieces])
    pos += npieces
    dx_out, gv_out = refs[pos : pos + 2]
    outs = refs[pos + 2 : pos + 2 + nouts]
    scratch = refs[pos + 2 + nouts :]
    wa, ga, dpm, dzp, do_ref = scratch[:5]
    vblk = scratch[5] if fold else None
    sems = scratch[-1]
    begin(dx1_in)
    loads = start(plan.load_a(scal, pieces, m, wa), sems)
    begin(o_in, vec_in, un_in, p_in, a1_in, a2_in, x_in, *others)
    base = len(loads)
    gv_ref = gv_out.near
    dx1 = dx1_in.ready()[...]
    dz = dx1.astype(BF)
    gv_ref[...] = jnp.zeros_like(gv_ref)
    gv_ref[BO : BO + 1] = jnp.sum(dz.astype(F32), axis=0, keepdims=True)
    dzp[...] = jnp.concatenate(
        [jnp.concatenate([jnp.zeros((T, 64), BF), dz[:, 192 * f : 192 * f + 192]], axis=1) for f in range(4)], axis=1
    )
    n2, inv2 = ln_stats(o_in.ready()[...])
    vec_ref = vec_in.ready()
    wait(loads)
    da2 = dot_nt(dzp[...], wa[:, :, :, :, 2048:3072].reshape(D, 1024))
    do, dg2, dc2 = ln_back(da2, vec_ref[G2 : G2 + 1], n2, inv2)
    gv_ref[G2 : G2 + 1] = dg2
    gv_ref[C2 : C2 + 1] = dc2
    do = do.astype(BF)
    for f in range(4):
        dpm[:, 2048 + 256 * f : 2304 + 256 * f] = jnp.zeros((T, 256), BF)
    un_ref, p_ref = un_in.ready(), p_in.ready()
    for h in range(HEADS):
        doh = do[:, 64 * h : 64 * h + 64]
        p = p_ref[h]
        q, k, v = un_ref[h], un_ref[HEADS + h], un_ref[2 * HEADS + h]
        dv = dot(p.astype(BF).T, doh)
        dp = dot_nt(doh, v)
        delta = jnp.sum(p * dp, axis=-1, keepdims=True)
        ds = (p * (dp - delta)).astype(BF)
        dq = dot(ds, k) * 0.125
        dk = dot(ds.T, q)
        for which, grad in ((0, dq), (1, dk), (2, dv)):
            u = which * HEADS + h
            f, j = divmod(u, 9)
            lane = 512 * f + 64 * j if j < 8 else 2048 + 256 * f
            grad = grad.astype(BF)
            dpm[:, lane : lane + 64] = grad
            if which != 1:
                row = BQ if which == 0 else BV
                gv_ref[row : row + 1, 64 * h : 64 * h + 64] = jnp.sum(grad.astype(F32), axis=0, keepdims=True)
    a1t = a1_in.ready()[...].T
    a2t = a2_in.ready()[...].T
    saves = []
    for i, (f, rc, ry) in enumerate(plan.blocks(scal)):
        main = dpm[:, pl.ds(pl.multiple_of(f * 512, 512), 512)]
        tail = dpm[:, pl.ds(pl.multiple_of(2048 + f * 256, 256), 256)]
        ga[i, :, :, :, :, 0:512] = dot(a1t, main).astype(BF).reshape(4, 2, 2, 48, 512)
        ga[i, :, :, :, :, 512:768] = (
            (dot(a1t, tail) + dot(a2t, dzp[:, pl.ds(pl.multiple_of(f * 256, 256), 256)])).astype(BF).reshape(4, 2, 2, 48, 256)
        )
        more = start(plan.store_ab(scal, ga.at[i], outs, m, f, rc, ry), sems, base)
        base += len(more)
        saves += more
    da1 = dot_nt(dpm[...], wa[...].reshape(D, FF))
    n1, inv1 = ln_stats(x_in.ready()[...])
    part, dg1, dc1 = ln_back(da1, vec_ref[G1 : G1 + 1], n1, inv1)
    gv_ref[G1 : G1 + 1] = dg1
    gv_ref[C1 : C1 + 1] = dc1
    dx_out.near[...] = dx1 + part
    begin(dx_out, gv_out)
    if fold:
        va0, vb1, va1, gh0, gh1 = (r.ready()[...] for r in others)
        v0 = gv_ref[...] + va0
        v1 = vb1 + va1
        for d in range(8):
            c96 = slice(96 * d, 96 * d + 96)
            c384 = slice(384 * d, 384 * d + 384)
            low = jnp.concatenate([v0[:, c96], v1[:, c96], jnp.zeros((VROWS, 576), F32)], axis=1)
            vblk[0, d // 2, d % 2] = low.astype(BF)
            vblk[1, d // 2, d % 2] = jnp.concatenate([gh0[:, c384], gh1[:, c384]], axis=1).astype(BF)
        more = start(plan.store_vec(scal, vblk, outs), sems, base)
        saves += more
    wait(saves)


def cost(flops, nbytes):
    return pl.CostEstimate(flops=int(flops), bytes_accessed=int(nbytes), transcendentals=0)


class Seq:
    def __init__(self, chained):
        self.chained = chained
        self.token = None
        self.held = []
        self.carrying = []
        self.carried = []

    def hold(self, *arrays):
        self.held += arrays

    def carry(self, *arrays):
        self.carrying = list(arrays)

    def __call__(self, kernel, out_shape, in_specs, out_specs, args, scratch=(), mib=24, **options):
        deps = [self.token] if self.chained and self.token is not None else []
        deps += self.held
        carried = self.carrying
        self.held, self.carrying = [], []
        n, k, m, q = len(args), len(deps), len(carried), len(out_shape)
        lazy_in = [i for i, v in enumerate(in_specs) if v is LAZY]
        lazy_out = [i for i, v in enumerate(out_specs) if v is LAZY]
        lazy_scratch = [pltpu.VMEM(args[i].shape, args[i].dtype) for i in lazy_in]
        lazy_scratch += [pltpu.VMEM(out_shape[i].shape, out_shape[i].dtype) for i in lazy_out]
        if lazy_scratch:
            lazy_scratch.append(pltpu.SemaphoreType.DMA((len(lazy_scratch),)))

        def body(*refs):
            first = n + k + m
            ins, outs = list(refs[:n]), list(refs[first : first + q])
            rest = list(refs[first + q + m :])
            near = rest[len(scratch) :]
            made = []
            for j, (group, i) in enumerate([(ins, i) for i in lazy_in] + [(outs, i) for i in lazy_out]):
                made.append(Lazy(group[i], near[j], near[-1].at[j], group is outs))
                group[i] = made[-1]
            kernel(*ins, *outs, *rest[: len(scratch)])
            for v in made:
                v.ready()

        res = pl.pallas_call(
            body,
            out_shape=tuple(out_shape) + tuple(S(v.shape, v.dtype) for v in carried),
            in_specs=[ANY if v is LAZY else v for v in in_specs] + [ANY] * (k + m),
            out_specs=tuple(ANY if v is LAZY else v for v in out_specs) + (ANY,) * m,
            scratch_shapes=list(scratch) + lazy_scratch,
            input_output_aliases={n + k + i: q + i for i in range(m)},
            compiler_params=pltpu.CompilerParams(vmem_limit_bytes=mib * MIB),
            **options,
        )(*args, *deps, *carried)
        self.token = res[0]
        self.carried = list(res[q:])
        return res[:q]


WA = pltpu.VMEM((4, 2, 2, 48, FF), BF)
WC = pltpu.VMEM((4, 4, 2, 2, 48, D), BF)
S = jax.ShapeDtypeStruct
WBYTES = D * FF * 2


def call_attn_fwd(seq, plan, scal, x, vec, pbias, pieces, m):
    pieces, find = flat(pieces)
    n = len(pieces)
    return seq(
        functools.partial(attn_fwd, plan, n, find, m),
        (S((T, D), F32), S((T, D), BF), S((36, T, HD), BF), S((HEADS, T, T), F32), S((T, D), F32), S((T, D), BF)),
        [SMEM, LAZY, LAZY, LAZY] + [ANY] * n,
        [LAZY] * 6,
        (scal, x, vec, pbias, *pieces),
        [WA, pltpu.SemaphoreType.DMA((32,))],
        cost_estimate=cost(2 * T * D * FF * 6, WBYTES + 8e6),
        name="attn_fwd",
        mib=64,
    )


def call_ff_fwd(seq, plan, scal, x1, vec, hid, pieces, mb, mc):
    pieces, find = flat(pieces)
    n = len(pieces)
    return seq(
        functools.partial(ff_fwd, plan, n, find, mb, mc),
        (S((T, D), F32), S((T, D), BF), S((T, FF), F32), S((T, FF), F32), S((T, FF), BF)),
        [SMEM, LAZY, LAZY, LAZY] + [ANY] * n,
        [LAZY] * 5,
        (scal, x1, vec, hid, *pieces),
        [WA, WC, pltpu.SemaphoreType.DMA((48,))],
        cost_estimate=cost(2 * T * D * FF * 6, 2 * WBYTES + 8e6),
        name="ff_fwd",
        mib=64,
    )


def call_ff_mid(seq, plan, scal, x1, dy, vec, hid, pieces, mb):
    pieces, find = flat(pieces)
    n = len(pieces)
    g = grad_shapes(plan, 1)
    res = seq(
        functools.partial(ff_mid, plan, n, find, len(g), mb),
        (S((T, D), BF), S((T, FF), F32), S((T, FF), F32), S((T, FF), BF), *g),
        [SMEM] + [LAZY] * 4 + [ANY] * n,
        [LAZY] * 4 + [ANY] * len(g),
        (scal, x1, dy, vec, hid, *pieces),
        [WA, WC, pltpu.SemaphoreType.DMA((48,))],
        cost_estimate=cost(2 * T * D * FF * 6, 2 * WBYTES + 8e6),
        name="ff_mid",
        mib=64,
    )
    return res[:4], res[4:]


def call_down_grad(seq, plan, scal, dy, a4):
    g = grad_shapes(plan, 1)
    return seq(
        functools.partial(down_grad, plan, len(g)),
        g,
        [SMEM, LAZY, LAZY],
        [ANY] * len(g),
        (scal, dy, a4),
        [WC, pltpu.SemaphoreType.DMA((32,))],
        cost_estimate=cost(2 * T * D * FF, WBYTES + 3e6),
        name="ff_down_grad",
        mib=64,
    )


def call_ff_out(seq, plan, scal, x1, a4, vec, pieces, mc):
    pieces, find = flat(pieces)
    n = len(pieces)
    return seq(
        functools.partial(ff_out, plan, n, find, mc),
        [S((T, D), F32)],
        [SMEM, LAZY, LAZY, LAZY] + [ANY] * n,
        [LAZY],
        (scal, x1, a4, vec, *pieces),
        [WC, pltpu.SemaphoreType.DMA((32,))],
        cost_estimate=cost(2 * T * D * FF * 3, WBYTES + 3e6),
        name="ff_out",
        mib=64,
    )[0]


def grad_shapes(plan, n, extra=0):
    if not plan.fast:
        return [S((4, 4, 2, 2, 48, D), BF)] * n
    return [S((2, 2, 2, 4, n * 48 + extra, D), BF)] * 2


def call_ff_bwd(seq, plan, scal, dy, x1, a3, sl, n4, a4, vec, hid, pieces, mb, mc, last, with_c):
    pieces, find = flat(pieces)
    n = len(pieces)
    g = grad_shapes(plan, 2 if with_c else 1)
    res = seq(
        functools.partial(ff_bwd, plan, n, find, len(g), mb, mc, last, with_c),
        (S((T, D), F32), S((VROWS, D), F32), S((VROWS, FF), F32), *g),
        [SMEM] + [LAZY] * 8 + [ANY] * n,
        [LAZY] * 3 + [ANY] * len(g),
        (scal, dy, x1, a3, sl, n4, a4, vec, hid, *pieces),
        [WA, WC, WC, pltpu.VMEM((T, FF), F32), pltpu.VMEM((T, FF), BF), pltpu.SemaphoreType.DMA((112,))] + [WC] * with_c,
        cost_estimate=cost(2 * T * D * FF * 8, 4 * WBYTES + 8e6),
        name="ff_bwd",
        mib=64,
    )
    return res[:3], res[3:]


def call_attn_bwd(seq, plan, scal, dx1, x, a1, un, p, o, a2, vec, pieces, m, others):
    pieces, find = flat(pieces)
    n = len(pieces)
    fold = len(others) > 0
    g = grad_shapes(plan, 1, 16 if fold else 0)
    vblk = [pltpu.VMEM((2, 4, 2, VROWS, D), BF)] if fold else []
    res = seq(
        functools.partial(attn_bwd, plan, n, find, len(g), m, fold),
        (S((T, D), F32), S((VROWS, D), F32), *g),
        [SMEM] + [LAZY] * (8 + len(others)) + [ANY] * n,
        [LAZY] * 2 + [ANY] * len(g),
        (scal, dx1, x, a1, un, p, o, a2, vec, *others, *pieces),
        [WA, WC, pltpu.VMEM((T, FF), BF), pltpu.VMEM((T, 1024), BF), pltpu.VMEM((T, D), BF), *vblk, pltpu.SemaphoreType.DMA((64,))],
        cost_estimate=cost(2 * T * D * FF * 8, 2 * WBYTES + 8e6),
        name="attn_bwd",
        mib=64,
    )
    return res[:2], res[2:]


def shift(n, k):
    return [(i, (i + k) % n) for i in range(n)]


class Ring:
    def __init__(self, dp, fsdp):
        self.X = fsdp // 2
        self.Z = dp // self.X
        self.dp, self.fsdp = dp, fsdp

    def z(self, v, k):
        return lax.ppermute(v, "dp", [(z * self.X + x, (z + k) % self.Z * self.X + x) for z in range(self.Z) for x in range(self.X)])

    def z_xor(self, v, k):
        return lax.ppermute(v, "dp", [(i, i ^ (k * self.X)) for i in range(self.dp)])

    def x(self, v):
        return lax.ppermute(v, "dp", [(i, i ^ 1) for i in range(self.dp)])

    def y(self, v):
        return lax.ppermute(v, "fsdp", [(i, i ^ 2) for i in range(self.fsdp)])

    def c(self, v):
        return lax.ppermute(v, "fsdp", [(i, i ^ 1) for i in range(self.fsdp)])


def pack_a_kernel(l, wqkv, wo, out):
    out[...] = jnp.concatenate([wqkv[l], wo[l]], axis=1)


def pack_a(seq, l, wqkv, wo):
    return seq(
        functools.partial(pack_a_kernel, l),
        [S((96, D), BF)],
        [VMEM] * 2,
        [VMEM],
        (wqkv, wo),
        cost_estimate=cost(0, 4 * 96 * D),
        name="pack_a",
    )[0]


def pack_bc_rows(l, w1, w2, out, first, second):
    t = w2[l].T
    for i, at in enumerate((first, second)):
        out[at : at + 48] = w1[l, 48 * i : 48 * i + 48]
        for j in range(2):
            out[at + 48 : at + 96, 384 * j : 384 * j + 384] = t[96 * j + 48 * i : 96 * j + 48 * i + 48]


def pack_vec_kernel(w1, w2, ng, bi, hg, hb, out):
    def column(v, u, w, first):
        v = jnp.concatenate([v.astype(F32), u.astype(F32)], axis=0)
        parts = [jnp.zeros((first, w), F32)] if first else []
        return jnp.concatenate(parts + [v, jnp.zeros((VROWS - first - v.shape[0], w), F32)], axis=0)

    pack_bc_rows(0, w1, w2, out, 0, 112)
    low = [column(ng[i], bi[i], 96, 0) for i in range(LAYERS)]
    hid = [column(hg[i], hb[i], 384, HROW) for i in range(LAYERS)]
    low = jnp.concatenate(low + [jnp.zeros((VROWS, 576), F32)], axis=1)
    out[96:112] = (low + jnp.concatenate(hid, axis=1)).astype(BF)
    out[208:224] = jnp.zeros((VROWS, D), BF)


def pack_vec(seq, w1, w2, vectors):
    return seq(
        pack_vec_kernel,
        [S((224, D), BF)],
        [VMEM] * 6,
        [VMEM],
        (w1, w2, *vectors),
        cost_estimate=cost(0, 4 * 224 * D),
        name="pack_vec",
    )[0]


def pack_ab_kernel(l, wqkv, wo, w1, out):
    a = jnp.concatenate([wqkv[l], wo[l]], axis=1)
    for i in range(2):
        out[96 * i : 96 * i + 48] = a[48 * i : 48 * i + 48]
        out[96 * i + 48 : 96 * i + 96] = w1[l, 48 * i : 48 * i + 48]


def pack_ab(seq, l, weights):
    return seq(
        functools.partial(pack_ab_kernel, l),
        [S((192, D), BF)],
        [VMEM] * 3,
        [VMEM],
        weights,
        cost_estimate=cost(0, 4 * 192 * D),
        name="pack_ab",
    )[0]


def pack_c_kernel(l, w2, o1, o2):
    t = w2[l].T
    for i, out in enumerate((o1, o2)):
        for j in range(2):
            out[:, 384 * j : 384 * j + 384] = t[96 * j + 48 * i : 96 * j + 48 * i + 48]


def pack_c(seq, l, w2):
    return seq(
        functools.partial(pack_c_kernel, l),
        [S((48, D), BF)] * 2,
        [VMEM],
        [VMEM] * 2,
        (w2,),
        cost_estimate=cost(0, 4 * 96 * D),
        name="pack_c",
    )


def join_kernel(a, b, c, d, o1, o2):
    o1[0] = a[...]
    o1[1] = b[...]
    o2[0] = c[...]
    o2[1] = d[...]


def join(seq, *parts):
    shape = S((2, *parts[0].shape), BF)
    return seq(join_kernel, [shape] * 2, [VMEM] * 4, [VMEM] * 2, parts, cost_estimate=cost(0, 16 * parts[0].size), name="join")


Q_CUTS = ((0, 2), (2, 1), (3, 1))


def zquad_kernel(scal, *refs):
    high = scal[2] // 2
    out = refs[-1]
    first = 0
    for k in range(0, len(refs) - 1, 2):
        rows = refs[k].shape[1]
        for part, pos in ((refs[k], high), (refs[k + 1], 1 - high)):
            for i in range(2):
                for r in range(rows):
                    for ri in range(2):
                        out[first + r, ri, 2 * pos + i] = part[i, r, ri]
        first += rows


def zquad(seq, scal, *parts):
    return seq(
        zquad_kernel,
        [S((2, 2, 4, 48, D), BF)],
        [SMEM] + [VMEM] * len(parts),
        [VMEM],
        (scal, *parts),
        cost_estimate=cost(0, 64 * 48 * D),
        name="zquad",
        mib=64,
    )[0]


def pile_vec_kernel(scal, h1, x1, h2, y2, o1, o2, own, *outs):
    for i, (out, parts) in enumerate(((o1, (h1, x1)), (o2, (h2, y2)))):
        for k, part in enumerate(parts):
            out[k] = part[...]
            own[i, k] = part[...]
    for l in range(LAYERS):
        low, high = [], []
        for z in range(4):
            for x in range(2):
                rows = o1[lax.rem(scal[3] + x, 2), z, 96:112].astype(F32)
                low.append(rows[:, 96 * l : 96 * l + 96])
                high.append(rows[:, 384 * l : 384 * l + 384])
        vec = jnp.concatenate(low, axis=1)
        outs[3 * l][...] = vec
        outs[3 * l + 1][...] = jnp.concatenate(high, axis=1)
        bias = jnp.concatenate([vec[BQ : BQ + 1], jnp.zeros((1, D), F32), vec[BV : BV + 1]], axis=1)
        parts = [bias[:, 576 * f : 576 * f + 512] for f in range(4)]
        for f in range(4):
            parts += [bias[:, 576 * f + 512 : 576 * f + 576], jnp.zeros((1, 64), F32)]
        outs[3 * l + 2][...] = jnp.concatenate(parts, axis=1)


def pile_vec(seq, scal, parts):
    rows = parts[0].shape[1]
    outs = [S((2, 4, rows, D), BF)] * 2 + [S((2, 2, 4, rows, D), BF)]
    outs += [S((VROWS, D), F32), S((VROWS, FF), F32), S((1, 2560), F32)] * LAYERS
    res = seq(
        pile_vec_kernel,
        outs,
        [SMEM] + [VMEM] * 4,
        [VMEM] * len(outs),
        (scal, *parts),
        cost_estimate=cost(0, 120 * rows * D),
        name="pile_vec",
        mib=64,
    )
    return res[:2], res[2], res[3::3], res[4::3], res[5::3]


def zcat_kernel(r1, scal, *refs):
    n = (len(refs) - 2) if len(refs) == 6 else (len(refs) - 3)
    o1, o2 = refs[n : n + 2]
    for k, ref in enumerate(refs[:4]):
        z = lax.rem(scal[2] + 4 - k, 4)
        o1[z] = ref[0:r1]
        o2[z] = ref[r1:]
    for i, ref in enumerate(refs[4:n]):
        refs[-1][i] = ref[...]


def zcat(seq, scal, parts, r1, *riders):
    r2 = parts[0].shape[0] - r1
    outs = [S((4, r1, D), BF), S((4, r2, D), BF)]
    if riders:
        outs.append(S((len(riders), *riders[0].shape), BF))
    return seq(
        functools.partial(zcat_kernel, r1),
        outs,
        [SMEM] + [VMEM] * (4 + len(riders)),
        [VMEM] * len(outs),
        (scal, *parts, *riders),
        cost_estimate=cost(0, 8 * (r1 + r2) * D * 2),
        name="zcat",
    )


def pile_kernel(cuts, scal, h1, x1, h2, y2, *refs):
    outs = refs[-2 * len(cuts) :] if len(refs) == 2 * len(cuts) else refs[2 : 2 + 2 * len(cuts)]
    for i, (first, rows) in enumerate(cuts):
        mine = pl.ds(first, rows)
        for j, parts in enumerate(((h1, x1), (h2, y2))):
            for k, part in enumerate(parts):
                outs[2 * i + j][k] = part[:, mine]
    if len(refs) > 2 * len(cuts):
        low = lax.rem(scal[2], 2)
        for (first, rows), out in zip(Q_CUTS, refs[2 + 2 * len(cuts) :]):
            out[low] = refs[0][first : first + rows]
            out[1 - low] = refs[1][first : first + rows]


def pile(seq, scal, parts, cuts, pair=()):
    outs = [S((2, 4, rows, D), BF) for _, rows in cuts for _ in range(2)]
    if pair:
        outs += [S((2, rows, *pair[0].shape[1:]), BF) for _, rows in Q_CUTS]
    return seq(
        functools.partial(pile_kernel, cuts),
        outs,
        [SMEM] + [VMEM] * (4 + len(pair)),
        [VMEM] * len(outs),
        (scal, *parts, *pair),
        cost_estimate=cost(0, 64 * sum(rows for _, rows in cuts) * D),
        name="pile",
    )


def merge_kernel(*refs):
    for i, ref in enumerate(refs[:-1]):
        refs[-1][i] = ref[...]


def merge(seq, *parts):
    shape = (len(parts), *parts[0].shape)
    return seq(merge_kernel, [S(shape, BF)], [VMEM] * len(parts), [VMEM], parts, cost_estimate=cost(0, 4 * math.prod(shape)), name="merge")[0]


def total(refs):
    out = refs[0].astype(F32)
    for r in refs[1:]:
        out = out + r.astype(F32)
    return out


class Sums:
    def __init__(self, scal):
        self.scal = scal
        self.arrays = []
        self.outs = []
        self.sums = []

    def source(self, array):
        for i, v in enumerate(self.arrays):
            if v is array:
                return i
        self.arrays.append(array)
        return len(self.arrays) - 1

    def out(self, *shape):
        self.outs.append(shape)
        return len(self.outs) - 1

    def add(self, out, where, sources, rows):
        self.sums.append((out, where, [(self.source(v), at, deep) for v, at, deep in sources], rows))

    def run(self, seq, name):
        n, q = len(self.arrays), len(self.outs)
        copies = sum(len(v[2]) for v in self.sums)
        sums = self.sums

        def kernel(scal, *refs):
            arrays, outs = refs[:n], refs[n : n + q]
            ins, made, sems = refs[n + q : n + q + copies], refs[n + q + copies : -1], refs[-1]
            pairs = [(arrays[i].at[at(scal)], ins[j]) for j, (i, at, _) in enumerate(v for t in sums for v in t[2])]
            loads = start(pairs, sems)
            saves, first = [], 0
            for t, (out, where, sources, rows) in enumerate(sums):
                mine = range(first, first + len(sources))
                first += len(sources)
                wait([loads[j] for j in mine])
                made[t][...] = total([ins[j][...].reshape(rows, D) for j in mine]).astype(BF)
                saves += start([(made[t], outs[out].at[where(scal)])], sems, copies + t)
            wait(saves)

        scratch = [pltpu.VMEM((4, t[3] // 4, D) if deep else (t[3], D), BF) for t in sums for _, _, deep in t[2]]
        scratch += [pltpu.VMEM((t[3], D), BF) for t in sums]
        return seq(
            kernel,
            [S((*v, D), BF) for v in self.outs],
            [SMEM] + [ANY] * n,
            [ANY] * q,
            (self.scal, *self.arrays),
            scratch + [pltpu.SemaphoreType.DMA((copies + len(sums),))],
            cost_estimate=cost(0, 2 * D * sum(t[3] * (1 + len(t[2])) for t in sums)),
            name=name,
            mib=64,
        )


def finish_kernel(scal, *refs):
    last = refs[4]
    in_out, out_out, up_out, down_out, vec_out = refs[17:]
    i = lax.rem(scal[2], 2)
    b1, c1 = (total([refs[2 * k][i], refs[2 * k + 1][i], last[96 * k : 96 * k + 96]]) for k in range(2))
    both = total([r[...] for r in refs[5:9]])
    b0 = total([r[...] for r in refs[9:13]])
    rows_a = total([r[...] for r in refs[13:17]])
    vec_out[0:VROWS] = rows_a[48:64]
    vec_out[VROWS:] = rows_a[112:128]
    a0 = jnp.concatenate([rows_a[:48], rows_a[64:112]], axis=0)
    for l, a, b, c in ((0, a0, b0, both[96:]), (1, both[:96], b1, c1)):
        in_out[l] = a[:, :576]
        out_out[l] = a[:, 576:]
        up_out[l] = b
        for j in range(2):
            down_out[l, :, 96 * j : 96 * j + 96] = c[:, 384 * j : 384 * j + 384].T


def finish(seq, scal, parts):
    return seq(
        finish_kernel,
        [S((2, 96, 576), F32), S((2, 96, 192), F32), S((2, 96, D), F32), S((2, 384, 192), F32), S((2 * VROWS, D), F32)],
        [SMEM] + [VMEM] * len(parts),
        [VMEM] * 5,
        (scal, *parts),
        cost_estimate=cost(0, 8e6),
        name="finish",
        mib=64,
    )


class Gather:
    def __init__(self, seq, ring, scal):
        self.seq, self.ring, self.scal = seq, ring, scal

    def z_all(self, pack):
        self.parts = [pack] + [self.ring.z(pack, k) for k in (1, 2, 3)]

    def xy_first(self, *riders):
        h1, h2, *rest = zcat(self.seq, self.scal, self.parts, self.parts[0].shape[0] // 2, *riders)
        self.both = h1, self.ring.x(h1), h2, self.ring.y(h2)
        return rest[0] if riders else None

    def xy_second(self, h1, h2):
        self.h1, self.h2 = h1, h2
        self.y1, self.x2 = self.ring.y(self.h1), self.ring.x(self.h2)

    def core(self):
        both = self.ring.c(merge(self.seq, self.h1, self.y1, self.h2, self.x2))
        self.other = [(both, i) for i in range(4)]
        return both

    def pieces(self):
        return [self.h1, self.y1, *self.other[:2], self.h2, self.x2, *self.other[2:]]


def rows_at(first, rows):
    return lambda scal: (pl.ds(first, rows),)


class Scatter:
    def __init__(self, ring, grads):
        self.ring = ring
        self.keep, self.send = grads
        self.rows = self.keep.shape[4]

    def core(self, send):
        self.got = self.ring.c(send)
        return self.got

    def both(self, *index):
        return [(v, lambda scal: index, True) for v in (self.keep, self.got)]

    def first(self, sums, x, y, at=0):
        self.at1 = at
        r = 4 * self.rows
        for h, out in ((0, x), (1, y)):
            for s in range(2):
                sums.add(out, rows_at(at + s * r, r), self.both(h, 1, s), r)

    def second(self, sums, x, y, at=0):
        self.at2 = at
        r = 4 * self.rows
        for h, got, out in ((0, self.x1st, y), (1, self.y1st, x)):
            sums.add(out, rows_at(at, r), self.both(h, 0, 1) + [(got, rows_at(self.at1 + r, r), False)], r)

    def block(self, sums, out, where, z):
        n = self.rows
        for h, a, b in ((0, self.x1st, self.y2nd), (1, self.y1st, self.x2nd)):

            def local(scal, h=h):
                return (h, 0, 0, z(scal))

            def sent(first):
                return lambda scal: (pl.ds(pl.multiple_of(first + z(scal) * n, 16), n),)

            sources = [(v, local, False) for v in (self.keep, self.got)]
            sources += [(a, sent(self.at1), False), (b, sent(self.at2), False)]
            sums.add(out, where(h * n, n), sources, n)

    def third_pair(self, sums):
        outs = [sums.out(2, 2 * self.rows) for _ in range(2)]
        for k in (1, 0):
            for i in range(2):

                def z(scal, k=k, i=i):
                    high = scal[2] // 2
                    return 2 * (1 - high if k else high) + i

                self.block(sums, outs[k], lambda first, n, i=i: lambda scal: (i, pl.ds(first, n)), z)
        return outs


def third_direct(sums, *chunks):
    outs = [sums.out(sum(2 * c.rows for c in chunks)) for _ in range(4)]
    for k in (1, 2, 3, 0):
        at = 0
        for c in chunks:
            c.block(sums, outs[k], lambda first, n, at=at: rows_at(at + first, n), lambda scal, k=k: lax.rem(scal[2] + k, 4))
            at += 2 * c.rows
    return outs


def fourth(sums, out, at, keep, got):
    rows = keep.shape[1]
    where = lambda scal: (1 - lax.rem(scal[2], 2),)
    sums.add(out, rows_at(at, rows), [(keep, where, False), (got, where, False)], rows)


def proj_bias(vec):
    full = jnp.concatenate([vec[BQ], jnp.zeros((D,), F32), vec[BV]]).reshape(4, 9 * HD)
    return jnp.concatenate(
        [full[:, :512].reshape(2048), jnp.pad(full[:, 512:], ((0, 0), (0, 64))).reshape(512)]
    ).reshape(1, 2560)


def fast_shards(ring, inputs, lengths, in_projection, out_projection, up_weight, down_weight, norm_gains, biases, hidden_gains, hidden_biases, cotangent):
    plan = Plan(True)
    seq = Seq(True)
    dpi, fi = lax.axis_index("dp"), lax.axis_index("fsdp")
    xme = dpi % ring.X
    place = jnp.stack([dpi // ring.X, xme, fi // 2, fi % 2]).astype(jnp.int32)
    scal = jnp.concatenate([lengths[0], place, jnp.zeros((2,), jnp.int32)])

    a, b, c, d = (Gather(seq, ring, scal) for _ in range(4))
    a.z_all(pack_a(seq, 0, in_projection, out_projection))
    q1, q2 = pack_c(seq, 1, down_weight)
    q1, q2 = join(seq, q1, ring.x(q1), q2, ring.y(q2))
    q1_got, q2_got = ring.y(q1), ring.x(q2)
    seq.hold(q1_got, q2_got)
    a.xy_first()
    b.z_all(pack_vec(seq, up_weight, down_weight, (norm_gains, biases, hidden_gains, hidden_biases)))
    cd = pack_ab(seq, 1, (in_projection, out_projection, up_weight))
    seq.hold(b.parts[1])
    a.xy_second(*pile(seq, scal, a.both, ((0, 48),)))
    seq.hold(a.y1, a.x2)
    b.xy_first()
    c.z_all(cd)
    q = merge(seq, q1, q1_got, q2, q2_got)
    seq.hold(a.core(), c.parts[3])
    h, own, vecs, hids, pb = pile_vec(seq, scal, b.both)
    b.xy_second(*h)
    b.own = ring.c(own)
    kept = [None, None]
    x = inputs
    x1, a1, un, p, o, a2 = call_attn_fwd(seq, plan, scal, x, vecs[0], pb[0], a.pieces(), 0)
    seq.hold(b.y1, b.x2, b.own)
    rest = ring.c(c.xy_first(b.y1, b.x2))
    b.other = [(b.own, 0), (rest, 0), (b.own, 1), (rest, 1)]
    seq.hold(rest)
    h = pile(seq, scal, c.both, ((0, 48), (48, 48)), (q, ring.z_xor(q, 1)))
    c.xy_second(*h[:2])
    d.xy_second(*h[2:4])
    parts_q = h[4:]
    got_q = [ring.z_xor(v, 2) for v in parts_q]
    x2, a3, sl, n4, a4 = call_ff_fwd(seq, plan, scal, x1, vecs[0], hids[0], b.pieces(), 0, 1)
    kept[0] = (x, x1, a1, un, p, o, a2, a3, sl, n4, a4)
    x = x2
    seq.hold(d.y1, d.x2, got_q[0])
    c.core()
    d.core()
    x1, a1, un, p, o, a2 = call_attn_fwd(seq, plan, scal, x, vecs[1], pb[1], c.pieces(), 0)
    q1 = zquad(seq, scal, parts_q[0], got_q[0])
    (a3, sl, n4, a4), grads = call_ff_mid(seq, plan, scal, x1, cotangent, vecs[1], hids[1], d.pieces(), 0)
    q2 = zquad(seq, scal, parts_q[1], got_q[1], parts_q[2], got_q[2])
    pieces_c = [(v, i) for v in (q1, ring.c(q1), q2, ring.c(q2)) for i in range(2)]

    sc = Scatter(ring, grads)
    sc.core(sc.send)
    pieces = d.pieces() + pieces_c
    (dx1, gva1, gh1), grads = call_ff_bwd(seq, plan, scal, cotangent, x1, a3, sl, n4, a4, vecs[1], hids[1], pieces, 0, 0, True, False)
    sb = Scatter(ring, grads)

    sums = Sums(scal)
    sc.first(sums, sums.out(384), sums.out(384))
    seq.carry(sb.send)
    u, v = sums.run(seq, "sums_1")
    sb.core(*seq.carried)
    sc.x1st, sc.y1st = ring.x(u), ring.y(v)

    x1_last, a4_last = x1, a4
    (dy, gvb1), grads = call_attn_bwd(seq, plan, scal, dx1, x, a1, un, p, o, a2, vecs[1], c.pieces(), 0, ())
    sa = Scatter(ring, grads)

    sums = Sums(scal)
    outs = sums.out(576), sums.out(576)
    sc.second(sums, *outs)
    sb.first(sums, *outs, 192)
    seq.carry(sa.send)
    u, v = sums.run(seq, "sums_2")
    sa.core(*seq.carried)
    sb.x1st, sb.y1st = sc.x2nd, sc.y2nd = ring.x(u), ring.y(v)

    x, x1, a1, un, p, o, a2, a3, sl, n4, a4 = kept[0]
    s3 = Scatter(ring, call_down_grad(seq, plan, scal, dy, a4))
    s3.core(s3.send)
    (dx1, gva0, gh0), grads = call_ff_bwd(seq, plan, scal, dy, x1, a3, sl, n4, a4, vecs[0], hids[0], b.pieces(), 0, 1, False, False)
    s4 = Scatter(ring, grads)

    sums = Sums(scal)
    outs = sums.out(960), sums.out(960)
    sb.second(sums, *outs)
    sa.first(sums, *outs, 192)
    s3.first(sums, *outs, 576)
    sc.third_pair(sums)
    seq.carry(s4.send)
    u, v, keep_c, send = sums.run(seq, "sums_3")
    s4.core(*seq.carried)
    sa.x1st, sa.y1st = sb.x2nd, sb.y2nd = s3.x1st, s3.y1st = ring.x(u), ring.y(v)
    got_c = ring.z_xor(send, 2)

    others = (gva0, gva1, gvb1, gh0, gh1)
    (input_gradient, _), grads = call_attn_bwd(seq, plan, scal, dx1, x, a1, un, p, o, a2, vecs[0], a.pieces(), 0, others)
    s5 = Scatter(ring, grads)

    sums = Sums(scal)
    outs = sums.out(768), sums.out(768)
    sa.second(sums, *outs)
    s3.second(sums, *outs, 192)
    s4.first(sums, *outs, 384)
    sb.third_pair(sums)
    seq.hold(got_c)
    seq.carry(s5.send)
    u, v, keep_b, send = sums.run(seq, "sums_4")
    s5.core(*seq.carried)
    s4.x1st, s4.y1st = sa.x2nd, sa.y2nd = s3.x2nd, s3.y2nd = ring.x(u), ring.y(v)
    got_b = ring.z_xor(send, 2)
    outputs = call_ff_out(seq, plan, scal, x1_last, a4_last, vecs[1], pieces, 0)

    sums = Sums(scal)
    outs = sums.out(704), sums.out(704)
    s4.second(sums, *outs)
    s5.first(sums, *outs, 192)
    third_direct(sums, sa, s3)
    seq.hold(got_b)
    u, v, *res = sums.run(seq, "sums_5")
    s4.x2nd, s4.y2nd = s5.x1st, s5.y1st = ring.x(u), ring.y(v)
    parts1 = [res[0]] + [ring.z(res[k], k) for k in (1, 2, 3)]

    sums = Sums(scal)
    s5.second(sums, sums.out(256), sums.out(256))
    third_direct(sums, s4)
    seq.hold(*parts1[1:])
    u, v, *res = sums.run(seq, "sums_6")
    s5.x2nd, s5.y2nd = ring.x(u), ring.y(v)
    parts2 = [res[0]] + [ring.z(res[k], k) for k in (1, 2, 3)]

    sums = Sums(scal)
    third_direct(sums, s5)
    out = sums.out(192)
    fourth(sums, out, 0, keep_b, got_b)
    fourth(sums, out, 96, keep_c, got_c)
    seq.hold(*parts2[1:])
    res = sums.run(seq, "sums_7")
    parts3 = [res[0]] + [ring.z(res[k], k) for k in (1, 2, 3)]
    last = ring.z_xor(res[4], 1)
    g_in, g_out, g_up, g_down, vrows = finish(seq, scal, [keep_b, got_b, keep_c, got_c, last, *parts1, *parts2, *parts3])
    gv = jnp.stack([vrows[:10, :96], vrows[:10, 96:192]])
    gh = jnp.stack([vrows[26:29, :384], vrows[26:29, 384:]])
    return outputs, input_gradient, g_in, g_out, g_up, g_down, gv[:, :3], gv[:, 3:], gh[:, :1], gh[:, 1:]


def whole_shards(inputs, lengths, in_projection, out_projection, up_weight, down_weight, norm_gains, biases, hidden_gains, hidden_biases, cotangent):
    plan = Plan(False)
    seq = Seq(False)
    scal = jnp.concatenate([lengths[0], jnp.zeros((6,), jnp.int32)])

    def full(w):
        return lax.all_gather(lax.all_gather(w, "fsdp", axis=1, tiled=True), "dp", axis=0, tiled=True)

    def rows(v, width):
        return jnp.pad(lax.all_gather(v, "dp", axis=1, tiled=True).astype(F32), ((0, VROWS - v.shape[0]), (0, 0)))

    vecs, hids, pieces = [], [], []
    for l in range(LAYERS):
        qkv = full(in_projection[l]).reshape(D, 4, 9 * HD)
        out = full(out_projection[l]).reshape(D, 4, 192)
        a = jnp.concatenate([qkv[:, :, :512].reshape(D, 2048), jnp.concatenate([qkv[:, :, 512:], out], axis=2).reshape(D, 1024)], axis=1)
        b = full(up_weight[l])
        c = full(down_weight[l]).reshape(4, D, D).transpose(0, 2, 1)
        shape = (4, 2, 2, 48, FF)
        got = [a.reshape(shape), b.reshape(shape), c.reshape(4, 4, 2, 2, 48, D)]
        pieces.append(got)
        vecs.append(rows(jnp.concatenate([norm_gains[l], biases[l]], axis=0), D))
        hid = rows(jnp.concatenate([hidden_gains[l], hidden_biases[l]], axis=0), FF)
        hids.append(jnp.roll(hid, HROW, axis=0))
    pb = [proj_bias(v) for v in vecs]
    x = inputs
    kept = []
    for l in range(LAYERS):
        x1, a1, un, p, o, a2 = call_attn_fwd(seq, plan, scal, x, vecs[l], pb[l], pieces[l], 0)
        x2, a3, sl, n4, a4 = call_ff_fwd(seq, plan, scal, x1, vecs[l], hids[l], pieces[l], 0, 0)
        kept.append((x, x1, a1, un, p, o, a2, a3, sl, n4, a4))
        x = x2
    places = jnp.arange(inputs.shape[0], dtype=jnp.int32)[:, None]
    outputs = x * (seg_of(scal, places) < SEQS).astype(F32)
    dy = cotangent
    layer_grads = [None] * LAYERS
    for l in reversed(range(LAYERS)):
        x, x1, a1, un, p, o, a2, a3, sl, n4, a4 = kept[l]
        last = l == LAYERS - 1
        (dx1, gva, gh), (gb, gc) = call_ff_bwd(seq, plan, scal, dy, x1, a3, sl, n4, a4, vecs[l], hids[l], pieces[l], 0, 0, last, True)
        (dy, gvb), (ga,) = call_attn_bwd(seq, plan, scal, dx1, x, a1, un, p, o, a2, vecs[l], pieces[l], 0, ())
        layer_grads[l] = (ga, gb, gc, gva + gvb, gh)

    def scatter(g):
        g = lax.psum_scatter(g.astype(BF), "dp", scatter_dimension=0, tiled=True)
        return lax.psum_scatter(g, "fsdp", scatter_dimension=1, tiled=True).astype(F32)

    def scatter_rows(v):
        v = lax.psum_scatter(v.astype(BF), "dp", scatter_dimension=1, tiled=True).astype(F32)
        return lax.psum(v, "fsdp")

    res = []
    for l in range(LAYERS):
        ga, gb, gc, gv, gh = layer_grads[l]
        ga = ga.reshape(4, D, D).transpose(1, 0, 2)
        gv = scatter_rows(gv[:10])
        gh = scatter_rows(gh[HROW : HROW + 3])
        res.append(
            (
                scatter(ga[:, :, :576].reshape(D, 3 * D)),
                scatter(ga[:, :, 576:].reshape(D, D)),
                scatter(gb.reshape(4, D, D).transpose(1, 0, 2).reshape(D, FF)),
                scatter(gc.reshape(4, D, D).transpose(0, 2, 1).reshape(FF, D)),
                gv[:3],
                gv[3:],
                gh[:1],
                gh[1:],
            )
        )
    return (outputs, dy, *(jnp.stack([r[i] for r in res]) for i in range(8)))


def solution(mesh):
    dp, fsdp = mesh.shape["dp"], mesh.shape["fsdp"]
    both = P(("dp", "fsdp"), None)
    mat = P(None, "dp", "fsdp")
    row = P(None, None, "dp")
    ring = Ring(dp, fsdp)
    shards = functools.partial(fast_shards, ring) if (dp, fsdp) == (8, 4) else whole_shards
    return jax.shard_map(
        shards,
        mesh=mesh,
        in_specs=(both, both, mat, mat, mat, mat, row, row, row, row, both),
        out_specs=(both, both, mat, mat, mat, mat, row, row, row, row),
        check_vma=False,
    )
```

```python
import functools
import math

import jax
import jax.numpy as jnp
from jax import lax
from jax.experimental import pallas as pl
from jax.experimental.pallas import tpu as pltpu
from jax.sharding import PartitionSpec as P

HEADS = 12
HD = 64
LAYERS = 2
SEQS = 2
D = 768
FF = 3072
T = 256
EPS = 1e-05
BF = jnp.bfloat16
F32 = jnp.float32
MIB = 1 << 20

ANY = pl.BlockSpec(memory_space=pltpu.HBM)
SMEM = pl.BlockSpec(memory_space=pltpu.SMEM)
VMEM = pl.BlockSpec(memory_space=pltpu.VMEM)
LAZY = object()


class Lazy:
    def __init__(self, far, near, sem, out):
        self.near = near
        self.copy = pltpu.make_async_copy(near, far, sem) if out else pltpu.make_async_copy(far, near, sem)
        self.flying = False

    def begin(self):
        self.copy.start()
        self.flying = True

    def ready(self):
        if self.flying:
            self.copy.wait()
            self.flying = False
        return self.near


def begin(*operands):
    for v in operands:
        v.begin()

G1, G2, G3, C1, BQ, BV, C2, BO, C3, B2 = range(10)
VROWS = 16
HROW = 10
G4, B1, C4 = 10, 11, 12

RB = 32


def dot(a, b):
    return jnp.dot(a, b, preferred_element_type=F32)


def dot_nt(a, b):
    return lax.dot_general(a, b, (((1,), (1,)), ((), ())), preferred_element_type=F32)


def unit_lane(u):
    f, j = divmod(u, 9)
    return 512 * f + 64 * j if j < 8 else 2048 + 128 * f


def ln_stats(v):
    m = jnp.mean(v, axis=-1, keepdims=True)
    cen = v - m
    inv = lax.rsqrt(jnp.mean(cen * cen, axis=-1, keepdims=True) + EPS)
    return cen * inv, inv


def ln_back(dn, g, n, inv):
    e = dn * g
    dv = inv * (e - jnp.mean(e, axis=-1, keepdims=True) - n * jnp.mean(e * n, axis=-1, keepdims=True))
    return dv, jnp.sum(dn * n, axis=0, keepdims=True), jnp.sum(dn, axis=0, keepdims=True)


def seg_of(scal, places):
    e0 = scal[0]
    e1 = scal[0] + scal[1]
    return (places >= e0).astype(jnp.int32) + (places >= e1).astype(jnp.int32)


class Plan:
    def __init__(self, fast):
        self.fast = fast

    def load_a(self, scal, pieces, m, dst):
        if not self.fast:
            return [(pieces[0], dst)]
        out = []
        for h, ri, x, f, ref in self._pieces(scal, pieces):
            src = ref.at[ri, :, pl.ds(m * 48, 48)]
            out.append((src.at[:, :, pl.ds(0, 512)], dst.at[:, x, h, :, pl.ds(pl.multiple_of(f * 512, 512), 512)]))
            out.append((src.at[:, :, pl.ds(512, 256)], dst.at[:, x, h, :, pl.ds(pl.multiple_of(2048 + f * 256, 256), 256)]))
        return out

    def load_b(self, scal, pieces, m, dst):
        if not self.fast:
            return [(pieces[1], dst)]
        return [
            (ref.at[ri, :, pl.ds(m * 48, 48)], dst.at[:, x, h, :, pl.ds(pl.multiple_of(f * 768, 768), 768)])
            for h, ri, x, f, ref in self._pieces(scal, pieces)
        ]

    def load_c(self, scal, pieces, m, dst):
        if not self.fast:
            return [(pieces[2], dst)]
        pieces = pieces[-8:]
        return [
            (
                ref.at[ri, :, pl.ds(m * 48, 48), pl.ds(j * 384, 384)],
                dst.at[:, f, j, h, :, pl.ds(pl.multiple_of(x * 384, 384), 384)],
            )
            for h, ri, x, f, ref in self._pieces(scal, pieces)
            for j in range(2)
        ]

    def _pieces(self, scal, pieces):
        mx, my, mc = scal[3], scal[4], scal[5]
        for h in range(2):
            for bi in range(4):
                ro, rc = bi % 2, bi // 2
                for ri in range(2):
                    rx, ry = (ri, ro) if h == 0 else (ro, ri)
                    x = lax.rem(mx + rx, 2)
                    y = lax.rem(my + ry, 2)
                    c = lax.rem(mc + rc, 2)
                    yield h, ri, x, y * 2 + c, pieces[h * 4 + bi]


    def blocks(self, scal):
        if not self.fast:
            return [(f, 0, 0) for f in range(4)]
        my, mc = scal[4], scal[5]
        return [(lax.rem(my + ry, 2) * 2 + lax.rem(mc + rc, 2), rc, ry) for rc in (1, 0) for ry in (1, 0)]

    def store_ab(self, scal, src, outs, m, f, rc, ry):
        if not self.fast:
            return [(src, outs[0].at[f])]
        res = []
        for rx in range(2):
            x = lax.rem(scal[3] + rx, 2)
            for h in range(2):
                first, second = (rx, ry) if h == 0 else (ry, rx)
                res.append((src.at[:, x, h], outs[rc].at[h, first, second, :, pl.ds(m * 48, 48)]))
        return res

    def store_c(self, scal, src, outs, m):
        if not self.fast:
            return [(src, outs[1])]
        res = []
        for f, rc, ry in self.blocks(scal):
            for rx in range(2):
                x = lax.rem(scal[3] + rx, 2)
                for h in range(2):
                    first, second = (rx, ry) if h == 0 else (ry, rx)
                    for j in range(2):
                        res.append(
                            (
                                src.at[:, f, j, h, :, pl.ds(pl.multiple_of(x * 384, 384), 384)],
                                outs[rc].at[h, first, second, :, pl.ds(m * 48, 48), pl.ds(j * 384, 384)],
                            )
                        )
        return res

    def store_vec(self, scal, src, outs):
        res = []
        for _, rc, ry in self.blocks(scal):
            for rx in range(2):
                x = lax.rem(scal[3] + rx, 2)
                for h in range(2):
                    first, second = (rx, ry) if h == 0 else (ry, rx)
                    res.append((src.at[h, :, x], outs[rc].at[h, first, second, :, pl.ds(48, 16)]))
        return res


def flat(pieces):
    arrays, finds = [], []
    for piece in pieces:
        array, index = piece if isinstance(piece, tuple) else (piece, None)
        place = next((i for i, v in enumerate(arrays) if v is array), len(arrays))
        if place == len(arrays):
            arrays.append(array)
        finds.append((place, index))
    return arrays, lambda refs: [refs[i] if j is None else refs[i].at[j] for i, j in finds]


def start(copies, sems, base=0):
    made = [pltpu.make_async_copy(s, d, sems.at[base + i]) for i, (s, d) in enumerate(copies)]
    for c in made:
        c.start()
    return made


def wait(made):
    for c in made:
        c.wait()


def attn_fwd(plan, npieces, find, m, *refs):
    scal, x_in, vec_in, pb_in = refs[:4]
    pieces = find(refs[4 : 4 + npieces])
    x1_out, a1_out, un_out, p_out, o_out, a2_out = refs[4 + npieces : 10 + npieces]
    wa, sems = refs[10 + npieces :]
    begin(x_in, vec_in)
    loads = start(plan.load_a(scal, pieces, m, wa), sems)
    begin(pb_in)
    x_ref, vec_ref = x_in.ready(), vec_in.ready()
    n1, _ = ln_stats(x_ref[...])
    a1 = (n1 * vec_ref[G1 : G1 + 1] + vec_ref[C1 : C1 + 1]).astype(BF)
    a1_out.near[...] = a1
    a1_out.begin()
    seg_row = seg_of(scal, lax.broadcasted_iota(jnp.int32, (T, T), 1))
    seg_col = seg_of(scal, lax.broadcasted_iota(jnp.int32, (T, T), 0))
    same = seg_row == seg_col
    pb_ref, un_ref = pb_in.ready(), un_out.near
    wait(loads)
    for f in range(4):
        part = dot(a1, wa[:, :, :, :, 512 * f : 512 * f + 512].reshape(D, 512)) + pb_ref[0:1, 512 * f : 512 * f + 512]
        last = dot(a1, wa[:, :, :, :, 2048 + 256 * f : 2176 + 256 * f].reshape(D, 128)) + pb_ref[0:1, 2048 + 128 * f : 2176 + 128 * f]
        for j in range(9):
            u = 9 * f + j
            val = part[:, 64 * j : 64 * j + 64] if j < 8 else last[:, 0:64]
            val = val.astype(BF)
            if u < HEADS:
                val = val * BF(0.125)
            un_ref[u] = val
    un_out.begin()
    o_ref = o_out.near
    for h in range(HEADS):
        s = jnp.where(same, dot_nt(un_ref[h], un_ref[HEADS + h]), -1e30)
        ex = jnp.exp(s - jnp.max(s, axis=-1, keepdims=True))
        p = ex * (1.0 / jnp.sum(ex, axis=-1, keepdims=True))
        p_out.near[h] = p
        o_ref[:, 64 * h : 64 * h + 64] = dot(p.astype(BF), un_ref[2 * HEADS + h])
    p_out.begin()
    o_out.begin()
    n2, _ = ln_stats(o_ref[...])
    a2 = (n2 * vec_ref[G2 : G2 + 1] + vec_ref[C2 : C2 + 1]).astype(BF)
    a2_out.near[...] = a2
    a2_out.begin()
    z = [dot(a2, wa[:, :, :, :, 2048 + 256 * f : 2304 + 256 * f].reshape(D, 256))[:, 64:] for f in range(4)]
    x1_out.near[...] = x_ref[...] + (jnp.concatenate(z, axis=1) + vec_ref[BO : BO + 1])
    x1_out.begin()


def hidden_rows(hid_ref, sl_ref, n4_ref, a4_ref):
    def rows_step(i, carry):
        rows = pl.ds(i * RB, RB)
        total = jnp.zeros((RB, 1), F32)
        for f in range(4):
            cols = slice(768 * f, 768 * f + 768)
            u = n4_ref[rows, cols]
            phi_c = 0.5 * (1.0 + lax.erf(u * (1.0 / math.sqrt(2.0))))
            r = u * phi_c
            sl_ref[rows, cols] = phi_c + u * (jnp.exp(-0.5 * u * u) * (1.0 / math.sqrt(2.0 * math.pi)))
            n4_ref[rows, cols] = r
            total += jnp.sum(r, axis=-1, keepdims=True)
        mean = total * (1.0 / FF)
        total = jnp.zeros((RB, 1), F32)
        for f in range(4):
            cols = slice(768 * f, 768 * f + 768)
            cen = n4_ref[rows, cols] - mean
            total += jnp.sum(cen * cen, axis=-1, keepdims=True)
        inv = lax.rsqrt(total * (1.0 / FF) + EPS)
        for f in range(4):
            cols = slice(768 * f, 768 * f + 768)
            n4 = (n4_ref[rows, cols] - mean) * inv
            n4_ref[rows, cols] = n4
            a4_ref[rows, cols] = (n4 * hid_ref[G4 : G4 + 1, cols] + hid_ref[C4 : C4 + 1, cols]).astype(BF)
            sl_ref[rows, cols] = sl_ref[rows, cols] * inv
        return carry

    lax.fori_loop(0, T // RB, rows_step, 0)


def hidden(x1_in, vec_in, hid_in, wb, load_b, a3_out, sl_out, n4_out, a4_out):
    x1_ref, vec_ref = x1_in.ready(), vec_in.ready()
    n3, _ = ln_stats(x1_ref[...])
    a3 = (n3 * vec_ref[G3 : G3 + 1] + vec_ref[C3 : C3 + 1]).astype(BF)
    a3_out.near[...] = a3
    a3_out.begin()
    hid_ref = hid_in.ready()
    n4_ref = n4_out.near
    wait(load_b)
    for f in range(4):
        cols = slice(768 * f, 768 * f + 768)
        n4_ref[:, cols] = dot(a3, wb[:, :, :, :, cols].reshape(D, 768)) + hid_ref[B1 : B1 + 1, cols]
    hidden_rows(hid_ref, sl_out.near, n4_ref, a4_out.near)
    begin(a4_out, n4_out, sl_out)


def down(x1_in, vec_in, a4_ref, wc):
    x1_ref, vec_ref = x1_in.ready(), vec_in.ready()
    acc = dot_nt(a4_ref[:, 0:768], wc[0].reshape(D, 768))
    for z in range(1, 4):
        acc += dot_nt(a4_ref[:, 768 * z : 768 * z + 768], wc[z].reshape(D, 768))
    return x1_ref[...] + (acc + vec_ref[B2 : B2 + 1])


def valid_rows(scal):
    seg = seg_of(scal, lax.broadcasted_iota(jnp.int32, (T, 1), 0))
    return (seg < SEQS).astype(F32)


def ff_fwd(plan, npieces, find, mb, mc, *refs):
    scal, x1_in, vec_in, hid_in = refs[:4]
    pieces = find(refs[4 : 4 + npieces])
    x2_out, a3_out, sl_out, n4_out, a4_out = refs[4 + npieces : 9 + npieces]
    wb, wc, sems = refs[9 + npieces :]
    begin(x1_in, vec_in)
    load_b = start(plan.load_b(scal, pieces, mb, wb), sems)
    begin(hid_in)
    load_c = start(plan.load_c(scal, pieces, mc, wc), sems, len(load_b))
    hidden(x1_in, vec_in, hid_in, wb, load_b, a3_out, sl_out, n4_out, a4_out)
    wait(load_c)
    x2_out.near[...] = down(x1_in, vec_in, a4_out.near, wc)
    x2_out.begin()


def ff_mid(plan, npieces, find, nouts, mb, *refs):
    scal, x1_in, dy_in, vec_in, hid_in = refs[:5]
    pieces = find(refs[5 : 5 + npieces])
    a3_out, sl_out, n4_out, a4_out = refs[5 + npieces : 9 + npieces]
    outs = refs[9 + npieces : 9 + npieces + nouts]
    wb, gc, sems = refs[9 + npieces + nouts :]
    begin(x1_in, vec_in)
    load_b = start(plan.load_b(scal, pieces, mb, wb), sems)
    begin(hid_in, dy_in)
    hidden(x1_in, vec_in, hid_in, wb, load_b, a3_out, sl_out, n4_out, a4_out)
    dz2t = (dy_in.ready()[...] * valid_rows(scal)).astype(BF).T
    for z in range(4):
        gc[z] = dot(dz2t, a4_out.near[:, 768 * z : 768 * z + 768]).astype(BF).reshape(4, 2, 2, 48, 768)
    wait(start(plan.store_c(scal, gc, outs, 0), sems, len(load_b)))


def down_grad(plan, nouts, *refs):
    scal, dy_in, a4_in = refs[:3]
    outs = refs[3 : 3 + nouts]
    gc, sems = refs[3 + nouts :]
    begin(dy_in, a4_in)
    dz2t = dy_in.ready()[...].astype(BF).T
    a4_ref = a4_in.ready()
    for z in range(4):
        gc[z] = dot(dz2t, a4_ref[:, 768 * z : 768 * z + 768]).astype(BF).reshape(4, 2, 2, 48, 768)
    wait(start(plan.store_c(scal, gc, outs, 0), sems))


def ff_out(plan, npieces, find, mc, *refs):
    scal, x1_in, a4_in, vec_in = refs[:4]
    pieces = find(refs[4 : 4 + npieces])
    out, wc, sems = refs[4 + npieces :]
    load_c = start(plan.load_c(scal, pieces, mc, wc), sems)
    begin(a4_in, x1_in, vec_in)
    wait(load_c)
    out.near[...] = down(x1_in, vec_in, a4_in.ready(), wc) * valid_rows(scal)
    out.begin()


def ff_bwd(plan, npieces, find, nouts, mb, mc, last, with_c, *refs):
    scal, dy_in, x1_in, a3_in, sl_in, n4_in, a4_in, vec_in, hid_in = refs[:9]
    pieces = find(refs[9 : 9 + npieces])
    dx1_out, gv_out, gh_out = refs[9 + npieces : 12 + npieces]
    outs = refs[12 + npieces : 12 + npieces + nouts]
    wb, wc, gb, da4, du_ref, sems = refs[12 + npieces + nouts : 18 + npieces + nouts]
    gc = refs[18 + npieces + nouts] if with_c else None
    begin(dy_in)
    load_c = start(plan.load_c(scal, pieces, mc, wc), sems)
    if with_c:
        begin(a4_in)
    begin(n4_in, hid_in, sl_in)
    load_b = start(plan.load_b(scal, pieces, mb, wb), sems, len(load_c))
    begin(a3_in, x1_in, vec_in)
    base = len(load_c) + len(load_b)
    gv_ref, gh_ref = gv_out.near, gh_out.near
    dy = dy_in.ready()[...]
    if last:
        dy = dy * valid_rows(scal)
    dz2 = dy.astype(BF)
    gv_ref[...] = jnp.zeros_like(gv_ref)
    gh_ref[...] = jnp.zeros_like(gh_ref)
    gv_ref[B2 : B2 + 1] = jnp.sum(dz2.astype(F32), axis=0, keepdims=True)
    dz2t = dz2.T if with_c else None
    wait(load_c)
    for z in range(4):
        cols = slice(768 * z, 768 * z + 768)
        da4[:, cols] = dot(dz2, wc[z].reshape(D, 768))
        if with_c:
            gc[z] = dot(dz2t, a4_in.ready()[:, cols]).astype(BF).reshape(4, 2, 2, 48, 768)
    saves = start(plan.store_c(scal, gc, outs, 1), sems, base) if with_c else []
    base += len(saves)
    n4_ref, hid_ref, sl_ref = n4_in.ready(), hid_in.ready(), sl_in.ready()

    def rows_step(i, carry):
        rows = pl.ds(i * RB, RB)
        s1 = jnp.zeros((RB, 1), F32)
        s2 = jnp.zeros((RB, 1), F32)
        for z in range(4):
            cols = slice(768 * z, 768 * z + 768)
            da = da4[rows, cols]
            n4 = n4_ref[rows, cols]
            dn = da * n4
            e = da * hid_ref[G4 : G4 + 1, cols]
            da4[rows, cols] = e
            s1 += jnp.sum(e, axis=-1, keepdims=True)
            s2 += jnp.sum(e * n4, axis=-1, keepdims=True)
            gh_ref[G4 : G4 + 1, cols] += jnp.sum(dn, axis=0, keepdims=True)
            gh_ref[C4 : C4 + 1, cols] += jnp.sum(da, axis=0, keepdims=True)
        s1 = s1 * (1.0 / FF)
        s2 = s2 * (1.0 / FF)
        for z in range(4):
            cols = slice(768 * z, 768 * z + 768)
            du = (sl_ref[rows, cols] * (da4[rows, cols] - s1 - n4_ref[rows, cols] * s2)).astype(BF)
            du_ref[rows, cols] = du
            gh_ref[B1 : B1 + 1, cols] += jnp.sum(du.astype(F32), axis=0, keepdims=True)
        return carry

    lax.fori_loop(0, T // RB, rows_step, 0)
    gh_out.begin()
    a3t = a3_in.ready()[...].T
    wait(load_b)
    da3 = jnp.zeros((T, D), F32)
    for i, (f, rc, ry) in enumerate(plan.blocks(scal)):
        cols = pl.ds(pl.multiple_of(f * 768, 768), 768)
        du = du_ref[:, cols]
        gb[i] = dot(a3t, du).astype(BF).reshape(4, 2, 2, 48, 768)
        more = start(plan.store_ab(scal, gb.at[i], outs, 0, f, rc, ry), sems, base)
        base += len(more)
        saves += more
        da3 += dot_nt(du, wb[:, :, :, :, cols].reshape(D, 768))
    n3, inv3 = ln_stats(x1_in.ready()[...])
    vec_ref = vec_in.ready()
    part, dg3, dc3 = ln_back(da3, vec_ref[G3 : G3 + 1], n3, inv3)
    gv_ref[G3 : G3 + 1] = dg3
    gv_ref[C3 : C3 + 1] = dc3
    dx1_out.near[...] = dy + part
    begin(dx1_out, gv_out)
    wait(saves)


def attn_bwd(plan, npieces, find, nouts, m, fold, *refs):
    scal, dx1_in, x_in, a1_in, un_in, p_in, o_in, a2_in, vec_in = refs[:9]
    pos = 9
    others = refs[pos : pos + (5 if fold else 0)]
    pos += len(others)
    pieces = find(refs[pos : pos + npieces])
    pos += npieces
    dx_out, gv_out = refs[pos : pos + 2]
    outs = refs[pos + 2 : pos + 2 + nouts]
    scratch = refs[pos + 2 + nouts :]
    wa, ga, dpm, dzp, do_ref = scratch[:5]
    vblk = scratch[5] if fold else None
    sems = scratch[-1]
    begin(dx1_in)
    loads = start(plan.load_a(scal, pieces, m, wa), sems)
    begin(o_in, vec_in, un_in, p_in, a1_in, a2_in, x_in, *others)
    base = len(loads)
    gv_ref = gv_out.near
    dx1 = dx1_in.ready()[...]
    dz = dx1.astype(BF)
    gv_ref[...] = jnp.zeros_like(gv_ref)
    gv_ref[BO : BO + 1] = jnp.sum(dz.astype(F32), axis=0, keepdims=True)
    dzp[...] = jnp.concatenate(
        [jnp.concatenate([jnp.zeros((T, 64), BF), dz[:, 192 * f : 192 * f + 192]], axis=1) for f in range(4)], axis=1
    )
    n2, inv2 = ln_stats(o_in.ready()[...])
    vec_ref = vec_in.ready()
    wait(loads)
    da2 = dot_nt(dzp[...], wa[:, :, :, :, 2048:3072].reshape(D, 1024))
    do, dg2, dc2 = ln_back(da2, vec_ref[G2 : G2 + 1], n2, inv2)
    gv_ref[G2 : G2 + 1] = dg2
    gv_ref[C2 : C2 + 1] = dc2
    do = do.astype(BF)
    for f in range(4):
        dpm[:, 2048 + 256 * f : 2304 + 256 * f] = jnp.zeros((T, 256), BF)
    un_ref, p_ref = un_in.ready(), p_in.ready()
    for h in range(HEADS):
        doh = do[:, 64 * h : 64 * h + 64]
        p = p_ref[h]
        q, k, v = un_ref[h], un_ref[HEADS + h], un_ref[2 * HEADS + h]
        dv = dot(p.astype(BF).T, doh)
        dp = dot_nt(doh, v)
        delta = jnp.sum(p * dp, axis=-1, keepdims=True)
        ds = (p * (dp - delta)).astype(BF)
        dq = dot(ds, k) * 0.125
        dk = dot(ds.T, q)
        for which, grad in ((0, dq), (1, dk), (2, dv)):
            u = which * HEADS + h
            f, j = divmod(u, 9)
            lane = 512 * f + 64 * j if j < 8 else 2048 + 256 * f
            grad = grad.astype(BF)
            dpm[:, lane : lane + 64] = grad
            if which != 1:
                row = BQ if which == 0 else BV
                gv_ref[row : row + 1, 64 * h : 64 * h + 64] = jnp.sum(grad.astype(F32), axis=0, keepdims=True)
    a1t = a1_in.ready()[...].T
    a2t = a2_in.ready()[...].T
    saves = []
    for i, (f, rc, ry) in enumerate(plan.blocks(scal)):
        main = dpm[:, pl.ds(pl.multiple_of(f * 512, 512), 512)]
        tail = dpm[:, pl.ds(pl.multiple_of(2048 + f * 256, 256), 256)]
        ga[i, :, :, :, :, 0:512] = dot(a1t, main).astype(BF).reshape(4, 2, 2, 48, 512)
        ga[i, :, :, :, :, 512:768] = (
            (dot(a1t, tail) + dot(a2t, dzp[:, pl.ds(pl.multiple_of(f * 256, 256), 256)])).astype(BF).reshape(4, 2, 2, 48, 256)
        )
        more = start(plan.store_ab(scal, ga.at[i], outs, m, f, rc, ry), sems, base)
        base += len(more)
        saves += more
    da1 = dot_nt(dpm[...], wa[...].reshape(D, FF))
    n1, inv1 = ln_stats(x_in.ready()[...])
    part, dg1, dc1 = ln_back(da1, vec_ref[G1 : G1 + 1], n1, inv1)
    gv_ref[G1 : G1 + 1] = dg1
    gv_ref[C1 : C1 + 1] = dc1
    dx_out.near[...] = dx1 + part
    begin(dx_out, gv_out)
    if fold:
        va0, vb1, va1, gh0, gh1 = (r.ready()[...] for r in others)
        v0 = gv_ref[...] + va0
        v1 = vb1 + va1
        for d in range(8):
            c96 = slice(96 * d, 96 * d + 96)
            c384 = slice(384 * d, 384 * d + 384)
            low = jnp.concatenate([v0[:, c96], v1[:, c96], jnp.zeros((VROWS, 576), F32)], axis=1)
            vblk[0, d // 2, d % 2] = low.astype(BF)
            vblk[1, d // 2, d % 2] = jnp.concatenate([gh0[:, c384], gh1[:, c384]], axis=1).astype(BF)
        more = start(plan.store_vec(scal, vblk, outs), sems, base)
        saves += more
    wait(saves)


def cost(flops, nbytes):
    return pl.CostEstimate(flops=int(flops), bytes_accessed=int(nbytes), transcendentals=0)


class Seq:
    def __init__(self, chained):
        self.chained = chained
        self.token = None
        self.held = []
        self.carrying = []
        self.carried = []

    def hold(self, *arrays):
        self.held += arrays

    def carry(self, *arrays):
        self.carrying = list(arrays)

    def __call__(self, kernel, out_shape, in_specs, out_specs, args, scratch=(), mib=24, **options):
        deps = [self.token] if self.chained and self.token is not None else []
        deps += self.held
        carried = self.carrying
        self.held, self.carrying = [], []
        parts = {i: v[1] for i, v in enumerate(args) if isinstance(v, tuple)}
        args = [v[0] if isinstance(v, tuple) else v for v in args]
        n, k, m, q = len(args), len(deps), len(carried), len(out_shape)
        lazy_in = [i for i, v in enumerate(in_specs) if v is LAZY]
        lazy_out = [i for i, v in enumerate(out_specs) if v is LAZY]
        lazy_scratch = [pltpu.VMEM(args[i].shape[i in parts :], args[i].dtype) for i in lazy_in]
        lazy_scratch += [pltpu.VMEM(out_shape[i].shape, out_shape[i].dtype) for i in lazy_out]
        if lazy_scratch:
            lazy_scratch.append(pltpu.SemaphoreType.DMA((len(lazy_scratch),)))

        def body(*refs):
            first = n + k + m
            ins, outs = list(refs[:n]), list(refs[first : first + q])
            rest = list(refs[first + q + m :])
            near = rest[len(scratch) :]
            made = []
            for j, (group, i) in enumerate([(ins, i) for i in lazy_in] + [(outs, i) for i in lazy_out]):
                if group is ins and i in parts:
                    group[i] = group[i].at[parts[i]]
                made.append(Lazy(group[i], near[j], near[-1].at[j], group is outs))
                group[i] = made[-1]
            kernel(*ins, *outs, *rest[: len(scratch)])
            for v in made:
                v.ready()

        res = pl.pallas_call(
            body,
            out_shape=tuple(out_shape) + tuple(S(v.shape, v.dtype) for v in carried),
            in_specs=[ANY if v is LAZY else v for v in in_specs] + [ANY] * (k + m),
            out_specs=tuple(ANY if v is LAZY else v for v in out_specs) + (ANY,) * m,
            scratch_shapes=list(scratch) + lazy_scratch,
            input_output_aliases={n + k + i: q + i for i in range(m)},
            compiler_params=pltpu.CompilerParams(vmem_limit_bytes=mib * MIB),
            **options,
        )(*args, *deps, *carried)
        self.token = res[0]
        self.carried = list(res[q:])
        return res[:q]


WA = pltpu.VMEM((4, 2, 2, 48, FF), BF)
WC = pltpu.VMEM((4, 4, 2, 2, 48, D), BF)
S = jax.ShapeDtypeStruct
WBYTES = D * FF * 2


def call_attn_fwd(seq, plan, scal, x, vec, pbias, pieces, m, weight=1.0):
    pieces, find = flat(pieces)
    n = len(pieces)
    return seq(
        functools.partial(attn_fwd, plan, n, find, m),
        (S((T, D), F32), S((T, D), BF), S((36, T, HD), BF), S((HEADS, T, T), F32), S((T, D), F32), S((T, D), BF)),
        [SMEM, LAZY, LAZY, LAZY] + [ANY] * n,
        [LAZY] * 6,
        (scal, x, vec, pbias, *pieces),
        [WA, pltpu.SemaphoreType.DMA((32,))],
        cost_estimate=cost(weight * 2 * T * D * FF * 6, weight * WBYTES),
        name="attn_fwd",
        mib=64,
    )


def call_ff_fwd(seq, plan, scal, x1, vec, hid, pieces, mb, mc, weight=1.0):
    pieces, find = flat(pieces)
    n = len(pieces)
    return seq(
        functools.partial(ff_fwd, plan, n, find, mb, mc),
        (S((T, D), F32), S((T, D), BF), S((T, FF), F32), S((T, FF), F32), S((T, FF), BF)),
        [SMEM, LAZY, LAZY, LAZY] + [ANY] * n,
        [LAZY] * 5,
        (scal, x1, vec, hid, *pieces),
        [WA, WC, pltpu.SemaphoreType.DMA((48,))],
        cost_estimate=cost(weight * 2 * T * D * FF * 6, weight * 2 * WBYTES),
        name="ff_fwd",
        mib=64,
    )


def call_ff_mid(seq, plan, scal, x1, dy, vec, hid, pieces, mb):
    pieces, find = flat(pieces)
    n = len(pieces)
    g = grad_shapes(plan, 1)
    res = seq(
        functools.partial(ff_mid, plan, n, find, len(g), mb),
        (S((T, D), BF), S((T, FF), F32), S((T, FF), F32), S((T, FF), BF), *g),
        [SMEM] + [LAZY] * 4 + [ANY] * n,
        [LAZY] * 4 + [ANY] * len(g),
        (scal, x1, dy, vec, hid, *pieces),
        [WA, WC, pltpu.SemaphoreType.DMA((48,))],
        cost_estimate=cost(2 * T * D * FF * 6, 2 * WBYTES + 8e6),
        name="ff_mid",
        mib=64,
    )
    return res[:4], res[4:]


def call_down_grad(seq, plan, scal, dy, a4):
    g = grad_shapes(plan, 1)
    return seq(
        functools.partial(down_grad, plan, len(g)),
        g,
        [SMEM, LAZY, LAZY],
        [ANY] * len(g),
        (scal, dy, a4),
        [WC, pltpu.SemaphoreType.DMA((32,))],
        cost_estimate=cost(2 * T * D * FF, WBYTES + 3e6),
        name="ff_down_grad",
        mib=64,
    )


def call_ff_out(seq, plan, scal, x1, a4, vec, pieces, mc):
    pieces, find = flat(pieces)
    n = len(pieces)
    return seq(
        functools.partial(ff_out, plan, n, find, mc),
        [S((T, D), F32)],
        [SMEM, LAZY, LAZY, LAZY] + [ANY] * n,
        [LAZY],
        (scal, x1, a4, vec, *pieces),
        [WC, pltpu.SemaphoreType.DMA((32,))],
        cost_estimate=cost(2 * T * D * FF * 3, WBYTES + 3e6),
        name="ff_out",
        mib=64,
    )[0]


def grad_shapes(plan, n, extra=0):
    if not plan.fast:
        return [S((4, 4, 2, 2, 48, D), BF)] * n
    return [S((2, 2, 2, 4, n * 48 + extra, D), BF)] * 2


def call_ff_bwd(seq, plan, scal, dy, x1, a3, sl, n4, a4, vec, hid, pieces, mb, mc, last, with_c):
    pieces, find = flat(pieces)
    n = len(pieces)
    g = grad_shapes(plan, 2 if with_c else 1)
    res = seq(
        functools.partial(ff_bwd, plan, n, find, len(g), mb, mc, last, with_c),
        (S((T, D), F32), S((VROWS, D), F32), S((VROWS, FF), F32), *g),
        [SMEM] + [LAZY] * 8 + [ANY] * n,
        [LAZY] * 3 + [ANY] * len(g),
        (scal, dy, x1, a3, sl, n4, a4, vec, hid, *pieces),
        [WA, WC, WC, pltpu.VMEM((T, FF), F32), pltpu.VMEM((T, FF), BF), pltpu.SemaphoreType.DMA((112,))] + [WC] * with_c,
        cost_estimate=cost(2 * T * D * FF * 8, 4 * WBYTES + 8e6),
        name="ff_bwd",
        mib=64,
    )
    return res[:3], res[3:]


def call_attn_bwd(seq, plan, scal, dx1, x, a1, un, p, o, a2, vec, pieces, m, others, weight=1.0):
    pieces, find = flat(pieces)
    n = len(pieces)
    fold = len(others) > 0
    g = grad_shapes(plan, 1, 16 if fold else 0)
    vblk = [pltpu.VMEM((2, 4, 2, VROWS, D), BF)] if fold else []
    res = seq(
        functools.partial(attn_bwd, plan, n, find, len(g), m, fold),
        (S((T, D), F32), S((VROWS, D), F32), *g),
        [SMEM] + [LAZY] * (8 + len(others)) + [ANY] * n,
        [LAZY] * 2 + [ANY] * len(g),
        (scal, dx1, x, a1, un, p, o, a2, vec, *others, *pieces),
        [WA, WC, pltpu.VMEM((T, FF), BF), pltpu.VMEM((T, 1024), BF), pltpu.VMEM((T, D), BF), *vblk, pltpu.SemaphoreType.DMA((64,))],
        cost_estimate=cost(weight * 2 * T * D * FF * 8, weight * (2 * WBYTES + 8e6)),
        name="attn_bwd",
        mib=64,
    )
    return res[:2], res[2:]


def shift(n, k):
    return [(i, (i + k) % n) for i in range(n)]


class Ring:
    def __init__(self, dp, fsdp):
        self.X = fsdp // 2
        self.Z = dp // self.X
        self.dp, self.fsdp = dp, fsdp

    def z(self, v, k):
        return lax.ppermute(v, "dp", [(z * self.X + x, (z + k) % self.Z * self.X + x) for z in range(self.Z) for x in range(self.X)])

    def z_xor(self, v, k):
        return lax.ppermute(v, "dp", [(i, i ^ (k * self.X)) for i in range(self.dp)])

    def x(self, v):
        return lax.ppermute(v, "dp", [(i, i ^ 1) for i in range(self.dp)])

    def y(self, v):
        return lax.ppermute(v, "fsdp", [(i, i ^ 2) for i in range(self.fsdp)])

    def c(self, v):
        return lax.ppermute(v, "fsdp", [(i, i ^ 1) for i in range(self.fsdp)])


def pack_a_kernel(l, wqkv, wo, out):
    out[...] = jnp.concatenate([wqkv[l], wo[l]], axis=1)


def pack_a(seq, l, wqkv, wo):
    return seq(
        functools.partial(pack_a_kernel, l),
        [S((96, D), BF)],
        [VMEM] * 2,
        [VMEM],
        (wqkv, wo),
        cost_estimate=cost(0, 4 * 96 * D),
        name="pack_a",
    )[0]


def pack_bc_rows(l, w1, w2, out, first, second):
    t = w2[l]
    for i, at in enumerate((first, second)):
        out[at : at + 48] = w1[l, 48 * i : 48 * i + 48]
        for j in range(2):
            out[at + 48 : at + 96, 384 * j : 384 * j + 384] = t[96 * j + 48 * i : 96 * j + 48 * i + 48]


def pack_bc_kernel(l, w1, w2, out):
    pack_bc_rows(l, w1, w2, out, 0, 96)


def pack_bc(seq, l, w1, w2):
    return seq(
        functools.partial(pack_bc_kernel, l),
        [S((192, D), BF)],
        [VMEM] * 2,
        [VMEM],
        (w1, w2),
        cost_estimate=cost(0, 4 * 192 * D),
        name="pack_bc",
    )[0]


def pack_ab_kernel(l, wqkv, wo, w1, ng, bi, hg, hb, out):
    def column(v, u, w, first):
        v = jnp.concatenate([v.astype(F32), u.astype(F32)], axis=0)
        parts = [jnp.zeros((first, w), F32)] if first else []
        return jnp.concatenate(parts + [v, jnp.zeros((VROWS - first - v.shape[0], w), F32)], axis=0)

    a = jnp.concatenate([wqkv[l], wo[l]], axis=1)
    for i in range(2):
        out[112 * i : 112 * i + 48] = a[48 * i : 48 * i + 48]
        out[112 * i + 48 : 112 * i + 96] = w1[l, 48 * i : 48 * i + 48]
    low = [column(ng[i], bi[i], 96, 0) for i in range(LAYERS)]
    hid = [column(hg[i], hb[i], 384, HROW) for i in range(LAYERS)]
    low = jnp.concatenate(low + [jnp.zeros((VROWS, 576), F32)], axis=1)
    out[96:112] = (low + jnp.concatenate(hid, axis=1)).astype(BF)
    out[208:224] = jnp.zeros((VROWS, D), BF)


def pack_ab(seq, l, weights, vectors):
    return seq(
        functools.partial(pack_ab_kernel, l),
        [S((224, D), BF)],
        [VMEM] * 7,
        [VMEM],
        (*weights, *vectors),
        cost_estimate=cost(0, 4 * 224 * D),
        name="pack_ab",
    )[0]


def pack_c_kernel(l, w2, o1, o2):
    t = w2[l]
    for i, out in enumerate((o1, o2)):
        for j in range(2):
            out[:, 384 * j : 384 * j + 384] = t[96 * j + 48 * i : 96 * j + 48 * i + 48]


def pack_c(seq, l, w2):
    return seq(
        functools.partial(pack_c_kernel, l),
        [S((48, D), BF)] * 2,
        [VMEM],
        [VMEM] * 2,
        (w2,),
        cost_estimate=cost(0, 4 * 96 * D),
        name="pack_c",
    )


def join_kernel(a, b, c, d, o1, o2):
    o1[0] = a[...]
    o1[1] = b[...]
    o2[0] = c[...]
    o2[1] = d[...]


def join(seq, *parts):
    shape = S((2, *parts[0].shape), BF)
    return seq(join_kernel, [shape] * 2, [VMEM] * 4, [VMEM] * 2, parts, cost_estimate=cost(0, 16 * parts[0].size), name="join")


Q_CUTS = ((0, 2), (2, 1), (3, 1))


def zquad_kernel(scal, *refs):
    high = scal[2] // 2
    out = refs[-1]
    first = 0
    for k in range(0, len(refs) - 1, 2):
        rows = refs[k].shape[1]
        for part, pos in ((refs[k], high), (refs[k + 1], 1 - high)):
            for i in range(2):
                for r in range(rows):
                    for ri in range(2):
                        out[first + r, ri, 2 * pos + i] = part[i, r, ri]
        first += rows


def zquad(seq, scal, *parts):
    return seq(
        zquad_kernel,
        [S((2, 2, 4, 48, D), BF)],
        [SMEM] + [VMEM] * len(parts),
        [VMEM],
        (scal, *parts),
        cost_estimate=cost(0, 64 * 48 * D),
        name="zquad",
        mib=64,
    )[0]


def zcat_kernel(r1, scal, *refs):
    n = (len(refs) - 2) if len(refs) == 6 else (len(refs) - 3)
    o1, o2 = refs[n : n + 2]
    for k, ref in enumerate(refs[:4]):
        z = lax.rem(scal[2] + 4 - k, 4)
        o1[z] = ref[0:r1]
        o2[z] = ref[r1:]
    for i, ref in enumerate(refs[4:n]):
        refs[-1][i] = ref[...]


def zcat(seq, scal, parts, r1, *riders):
    r2 = parts[0].shape[0] - r1
    outs = [S((4, r1, D), BF), S((4, r2, D), BF)]
    if riders:
        outs.append(S((len(riders), *riders[0].shape), BF))
    return seq(
        functools.partial(zcat_kernel, r1),
        outs,
        [SMEM] + [VMEM] * (4 + len(riders)),
        [VMEM] * len(outs),
        (scal, *parts, *riders),
        cost_estimate=cost(0, 8 * (r1 + r2) * D * 2),
        name="zcat",
    )


def pile_kernel(cuts, h1, x1, h2, y2, *outs):
    for i, (first, rows) in enumerate(cuts):
        mine = pl.ds(first, rows)
        for j, parts in enumerate(((h1, x1), (h2, y2))):
            for k, part in enumerate(parts):
                outs[2 * i + j][k] = part[:, mine]
                if len(outs) > 2 * len(cuts):
                    outs[-1][j, k] = part[:, mine]


def pile(seq, parts, cuts, again=False):
    outs = [S((2, 4, rows, D), BF) for _, rows in cuts for _ in range(2)]
    if again:
        outs.append(S((2, *outs[0].shape), BF))
    return seq(
        functools.partial(pile_kernel, cuts),
        outs,
        [VMEM] * 4,
        [VMEM] * len(outs),
        parts,
        cost_estimate=cost(0, 64 * sum(rows for _, rows in cuts) * D),
        name="pile",
    )


def pile_last_kernel(cuts, scal, h1, x1, h2, y2, q, q_got, *refs):
    n = 2 * len(cuts)
    pile_kernel(cuts, h1, x1, h2, y2, *refs[:n])
    low = lax.rem(scal[2], 2)
    for (first, rows), out in zip(Q_CUTS, refs[n:]):
        out[low] = q[first : first + rows]
        out[1 - low] = q_got[first : first + rows]
    vecs, hids, biases = refs[-3:]
    own = lax.convert_element_type(scal[3] == 0, F32)
    for l in range(LAYERS):
        low, high = [], []
        for z in range(4):
            mine, other = h1[z, 96:112].astype(F32), x1[z, 96:112].astype(F32)
            for rows in (own * mine + (1 - own) * other, own * other + (1 - own) * mine):
                low.append(rows[:, 96 * l : 96 * l + 96])
                high.append(rows[:, 384 * l : 384 * l + 384])
        vec = jnp.concatenate(low, axis=1)
        vecs[l] = vec
        hids[l] = jnp.concatenate(high, axis=1)
        bias = jnp.concatenate([vec[BQ : BQ + 1], jnp.zeros((1, D), F32), vec[BV : BV + 1]], axis=1)
        parts = [bias[:, 576 * f : 576 * f + 512] for f in range(4)]
        for f in range(4):
            parts += [bias[:, 576 * f + 512 : 576 * f + 576], jnp.zeros((1, 64), F32)]
        biases[l] = jnp.concatenate(parts, axis=1)


def pile_last(seq, scal, parts, cuts, q, q_got):
    outs = [S((2, 4, rows, D), BF) for _, rows in cuts for _ in range(2)]
    outs += [S((2, rows, *q.shape[1:]), BF) for _, rows in Q_CUTS]
    outs += [S((LAYERS, VROWS, D), F32), S((LAYERS, VROWS, FF), F32), S((LAYERS, 1, 2560), F32)]
    res = seq(
        functools.partial(pile_last_kernel, cuts),
        outs,
        [SMEM] + [VMEM] * 6,
        [VMEM] * len(outs),
        (scal, *parts, q, q_got),
        cost_estimate=cost(0, 64 * sum(rows for _, rows in cuts) * D),
        name="pile_last",
    )
    n = 2 * len(cuts)
    return res[:n], res[n : n + 3], *([(v, l) for l in range(LAYERS)] for v in res[n + 3 :])


def merge_kernel(*refs):
    for i, ref in enumerate(refs[:-1]):
        refs[-1][i] = ref[...]


def merge(seq, *parts):
    shape = (len(parts), *parts[0].shape)
    return seq(merge_kernel, [S(shape, BF)], [VMEM] * len(parts), [VMEM], parts, cost_estimate=cost(0, 4 * math.prod(shape)), name="merge")[0]


def total(refs):
    out = refs[0].astype(F32)
    for r in refs[1:]:
        out = out + r.astype(F32)
    return out


class Sums:
    def __init__(self, scal):
        self.scal = scal
        self.arrays = []
        self.outs = []
        self.sums = []

    def source(self, array):
        for i, v in enumerate(self.arrays):
            if v is array:
                return i
        self.arrays.append(array)
        return len(self.arrays) - 1

    def out(self, *shape):
        self.outs.append(shape)
        return len(self.outs) - 1

    def add(self, out, where, sources, rows):
        self.sums.append((out, where, [(self.source(v), at, deep) for v, at, deep in sources], rows))

    def run(self, seq, name):
        n, q = len(self.arrays), len(self.outs)
        copies = sum(len(v[2]) for v in self.sums)
        sums = self.sums

        def kernel(scal, *refs):
            arrays, outs = refs[:n], refs[n : n + q]
            ins, made, sems = refs[n + q : n + q + copies], refs[n + q + copies : -1], refs[-1]
            pairs = [(arrays[i].at[at(scal)], ins[j]) for j, (i, at, _) in enumerate(v for t in sums for v in t[2])]
            loads = start(pairs, sems)
            saves, first = [], 0
            for t, (out, where, sources, rows) in enumerate(sums):
                mine = range(first, first + len(sources))
                first += len(sources)
                wait([loads[j] for j in mine])
                made[t][...] = total([ins[j][...].reshape(rows, D) for j in mine]).astype(BF)
                saves += start([(made[t], outs[out].at[where(scal)])], sems, copies + t)
            wait(saves)

        scratch = [pltpu.VMEM((4, t[3] // 4, D) if deep else (t[3], D), BF) for t in sums for _, _, deep in t[2]]
        scratch += [pltpu.VMEM((t[3], D), BF) for t in sums]
        return seq(
            kernel,
            [S((*v, D), BF) for v in self.outs],
            [SMEM] + [ANY] * n,
            [ANY] * q,
            (self.scal, *self.arrays),
            scratch + [pltpu.SemaphoreType.DMA((copies + len(sums),))],
            cost_estimate=cost(0, 2 * D * sum(t[3] * (1 + len(t[2])) for t in sums)),
            name=name,
            mib=64,
        )


def finish_kernel(scal, *refs):
    in_out, out_out, up_out, down_out, gain_out, bias_out, hgain_out, hbias_out = refs[14:]
    i = lax.rem(scal[2], 2)
    c1 = total([refs[0][i], refs[1][i], refs[4][0:96]])
    ba1 = total([refs[2][i], refs[3][i], refs[4][96:288]])
    c0 = total([refs[5][i], refs[6][i], refs[4][288:384]])
    b0 = total([refs[7][i], refs[8][i], refs[9][...]])
    rows_a = total([r[...] for r in refs[10:14]])
    for l in range(LAYERS):
        for r in range(3):
            gain_out[r, l : l + 1] = rows_a[48 + r : 49 + r, 96 * l : 96 * l + 96]
        for r in range(7):
            bias_out[r, l : l + 1] = rows_a[51 + r : 52 + r, 96 * l : 96 * l + 96]
        hid = rows_a[112 + HROW : 115 + HROW, 384 * l : 384 * l + 384]
        hgain_out[0, l : l + 1] = hid[0:1]
        hbias_out[0, l : l + 1] = hid[1:2]
        hbias_out[1, l : l + 1] = hid[2:3]
    a0 = jnp.concatenate([rows_a[:48], rows_a[64:112]], axis=0)
    for l, a, b, c in ((0, a0, b0, c0), (1, ba1[96:], ba1[:96], c1)):
        in_out[l] = a[:, :576]
        out_out[l] = a[:, 576:]
        up_out[l] = b
        for j in range(2):
            down_out[l, 96 * j : 96 * j + 96] = c[:, 384 * j : 384 * j + 384]


def finish(seq, scal, parts):
    return seq(
        finish_kernel,
        [S((2, 96, 576), F32), S((2, 96, 192), F32), S((2, 96, D), F32), S((2, 192, 384), F32), S((3, 2, 96), F32), S((7, 2, 96), F32), S((1, 2, 384), F32), S((2, 2, 384), F32)],
        [SMEM] + [VMEM] * len(parts),
        [VMEM] * 8,
        (scal, *parts),
        cost_estimate=cost(0, 8e6),
        name="finish",
        mib=64,
    )


class Gather:
    def __init__(self, seq, ring, scal):
        self.seq, self.ring, self.scal = seq, ring, scal

    def z_all(self, pack):
        self.parts = [pack] + [self.ring.z(pack, k) for k in (1, 2, 3)]

    def xy_first(self, *riders):
        h1, h2, *rest = zcat(self.seq, self.scal, self.parts, self.parts[0].shape[0] // 2, *riders)
        self.both = h1, self.ring.x(h1), h2, self.ring.y(h2)
        return rest[0] if riders else None

    def xy_second(self, h1, h2):
        self.h1, self.h2 = h1, h2
        self.y1, self.x2 = self.ring.y(self.h1), self.ring.x(self.h2)

    def core(self):
        both = self.ring.c(merge(self.seq, self.h1, self.y1, self.h2, self.x2))
        self.other = [(both, i) for i in range(4)]
        return both

    def pieces(self):
        return [self.h1, self.y1, *self.other[:2], self.h2, self.x2, *self.other[2:]]


def rows_at(first, rows):
    return lambda scal: (pl.ds(first, rows),)


class Scatter:
    def __init__(self, ring, grads):
        self.ring = ring
        self.keep, self.send = grads
        self.rows = self.keep.shape[4]

    def core(self, send):
        self.got = self.ring.c(send)
        return self.got

    def both(self, *index):
        return [(v, lambda scal: index, True) for v in (self.keep, self.got)]

    def first(self, sums, x, y, at=0):
        self.at1 = at
        r = 4 * self.rows
        for h, out in ((0, x), (1, y)):
            for s in range(2):
                sums.add(out, rows_at(at + s * r, r), self.both(h, 1, s), r)

    def second(self, sums, x, y, at=0):
        self.at2 = at
        r = 4 * self.rows
        for h, got, out in ((0, self.x1st, y), (1, self.y1st, x)):
            sums.add(out, rows_at(at, r), self.both(h, 0, 1) + [(got, rows_at(self.at1 + r, r), False)], r)

    def block(self, sums, out, where, z):
        n = self.rows
        for h, a, b in ((0, self.x1st, self.y2nd), (1, self.y1st, self.x2nd)):

            def local(scal, h=h):
                return (h, 0, 0, z(scal))

            def sent(first):
                return lambda scal: (pl.ds(pl.multiple_of(first + z(scal) * n, 16), n),)

            sources = [(v, local, False) for v in (self.keep, self.got)]
            sources += [(a, sent(self.at1), False), (b, sent(self.at2), False)]
            sums.add(out, where(h * n, n), sources, n)


def third_pair(sums, *chunks):
    outs = [sums.out(2, sum(2 * c.rows for c in chunks)) for _ in range(2)]
    for k in (1, 0):
        for i in range(2):

            def z(scal, k=k, i=i):
                high = scal[2] // 2
                return 2 * (1 - high if k else high) + i

            at = 0
            for c in chunks:
                c.block(sums, outs[k], lambda first, n, i=i, at=at: lambda scal: (i, pl.ds(at + first, n)), z)
                at += 2 * c.rows
    return outs


def third_direct(sums, *chunks):
    outs = [sums.out(sum(2 * c.rows for c in chunks)) for _ in range(4)]
    for k in (1, 2, 3, 0):
        at = 0
        for c in chunks:
            c.block(sums, outs[k], lambda first, n, at=at: rows_at(at + first, n), lambda scal, k=k: lax.rem(scal[2] + k, 4))
            at += 2 * c.rows
    return outs


def fourth(sums, out, at, keep, got):
    rows = keep.shape[1]
    where = lambda scal: (1 - lax.rem(scal[2], 2),)
    sums.add(out, rows_at(at, rows), [(keep, where, False), (got, where, False)], rows)


def proj_bias(vec):
    full = jnp.concatenate([vec[BQ], jnp.zeros((D,), F32), vec[BV]]).reshape(4, 9 * HD)
    return jnp.concatenate(
        [full[:, :512].reshape(2048), jnp.pad(full[:, 512:], ((0, 0), (0, 64))).reshape(512)]
    ).reshape(1, 2560)


def fast_shards(ring, inputs, lengths, in_projection, out_projection, up_weight, down_weight, norm_gains, biases, hidden_gains, hidden_biases, cotangent):
    plan = Plan(True)
    seq = Seq(True)
    dpi, fi = lax.axis_index("dp"), lax.axis_index("fsdp")
    xme = dpi % ring.X
    place = jnp.stack([dpi // ring.X, xme, fi // 2, fi % 2]).astype(jnp.int32)
    scal = jnp.concatenate([lengths[0], place, jnp.zeros((2,), jnp.int32)])

    down_weight = down_weight.transpose(0, 2, 1)

    a, b, c, d = (Gather(seq, ring, scal) for _ in range(4))
    a.z_all(pack_a(seq, 0, in_projection, out_projection))
    q1, q2 = pack_c(seq, 1, down_weight)
    q1, q2 = join(seq, q1, ring.x(q1), q2, ring.y(q2))
    q1_got, q2_got = ring.y(q1), ring.x(q2)
    seq.hold(q1_got, q2_got)
    a.xy_first()
    b.z_all(pack_bc(seq, 0, up_weight, down_weight))
    cd = pack_ab(seq, 1, (in_projection, out_projection, up_weight), (norm_gains, biases, hidden_gains, hidden_biases))
    seq.hold(b.parts[1])
    a.xy_second(*pile(seq, a.both, ((0, 48),)))
    seq.hold(a.y1, a.x2)
    b.xy_first()
    c.z_all(cd)
    q = merge(seq, q1, q1_got, q2, q2_got)
    seq.hold(a.core(), c.parts[3])
    *h, own = pile(seq, b.both, ((0, 96),), True)
    b.xy_second(*h)
    b.own = ring.c(own)
    kept = [None, None]
    x = inputs
    seq.hold(b.y1, b.x2, b.own)
    rest = ring.c(c.xy_first(b.y1, b.x2))
    b.other = [(b.own, 0), (rest, 0), (b.own, 1), (rest, 1)]
    seq.hold(rest)
    h, parts_q, vecs, hids, pb = pile_last(seq, scal, c.both, ((0, 48), (48, 48)), q, ring.z_xor(q, 1))
    c.xy_second(*h[:2])
    d.xy_second(*h[2:])
    x1, a1, un, p, o, a2 = call_attn_fwd(seq, plan, scal, x, vecs[0], pb[0], a.pieces(), 0, 0.01)
    got_q = [ring.z_xor(v, 2) for v in parts_q]
    x2, a3, sl, n4, a4 = call_ff_fwd(seq, plan, scal, x1, vecs[0], hids[0], b.pieces(), 0, 1, 0.01)
    kept[0] = (x, x1, a1, un, p, o, a2, a3, sl, n4, a4)
    x = x2
    seq.hold(d.y1, d.x2, got_q[0])
    c.core()
    d.core()
    x1, a1, un, p, o, a2 = call_attn_fwd(seq, plan, scal, x, vecs[1], pb[1], c.pieces(), 0)
    q1 = zquad(seq, scal, parts_q[0], got_q[0])
    (a3, sl, n4, a4), grads = call_ff_mid(seq, plan, scal, x1, cotangent, vecs[1], hids[1], d.pieces(), 0)
    q2 = zquad(seq, scal, parts_q[1], got_q[1], parts_q[2], got_q[2])
    pieces_c = [(v, i) for v in (q1, ring.c(q1), q2, ring.c(q2)) for i in range(2)]

    sc = Scatter(ring, grads)
    sc.core(sc.send)
    pieces = d.pieces() + pieces_c
    (dx1, gva1, gh1), grads = call_ff_bwd(seq, plan, scal, cotangent, x1, a3, sl, n4, a4, vecs[1], hids[1], pieces, 0, 0, True, False)
    sb = Scatter(ring, grads)

    sums = Sums(scal)
    sc.first(sums, sums.out(384), sums.out(384))
    seq.carry(sb.send)
    u, v = sums.run(seq, "sums_1")
    sb.core(*seq.carried)
    sc.x1st, sc.y1st = ring.x(u), ring.y(v)

    x1_last, a4_last = x1, a4
    (dy, gvb1), grads = call_attn_bwd(seq, plan, scal, dx1, x, a1, un, p, o, a2, vecs[1], c.pieces(), 0, ())
    sa = Scatter(ring, grads)

    sums = Sums(scal)
    sc.second(sums, sums.out(192), sums.out(192))
    seq.carry(sa.send)
    u, v = sums.run(seq, "sums_2a")
    sa.core(*seq.carried)
    sc.x2nd, sc.y2nd = ring.x(u), ring.y(v)

    x, x1, a1, un, p, o, a2, a3, sl, n4, a4 = kept[0]
    s3 = Scatter(ring, call_down_grad(seq, plan, scal, dy, a4))

    sums = Sums(scal)
    outs = sums.out(768), sums.out(768)
    sb.first(sums, *outs)
    sa.first(sums, *outs, 384)
    third_pair(sums, sc)
    seq.carry(s3.send)
    u, v, keep_c, send = sums.run(seq, "sums_2b")
    got_c = ring.z_xor(send, 2)
    s3.core(*seq.carried)
    sb.x1st, sb.y1st = sa.x1st, sa.y1st = ring.x(u), ring.y(v)

    (dx1, gva0, gh0), grads = call_ff_bwd(seq, plan, scal, dy, x1, a3, sl, n4, a4, vecs[0], hids[0], b.pieces(), 0, 1, False, False)
    s4 = Scatter(ring, grads)

    sums = Sums(scal)
    outs = sums.out(384), sums.out(384)
    sb.second(sums, *outs)
    sa.second(sums, *outs, 192)
    s3.first(sums, sums.out(384), sums.out(384))
    seq.hold(got_c)
    seq.carry(s4.send)
    u, v, u3, v3 = sums.run(seq, "sums_3")
    s4.core(*seq.carried)
    sb.x2nd, sb.y2nd = sa.x2nd, sa.y2nd = ring.x(u), ring.y(v)
    s3.x1st, s3.y1st = ring.x(u3), ring.y(v3)

    others = (gva0, gva1, gvb1, gh0, gh1)
    (input_gradient, _), grads = call_attn_bwd(seq, plan, scal, dx1, x, a1, un, p, o, a2, vecs[0], a.pieces(), 0, others, 0.01)
    s5 = Scatter(ring, grads)

    sums = Sums(scal)
    third_pair(sums, sb, sa)
    keep_ba, send = sums.run(seq, "sums_4a")
    got_ba = ring.z_xor(send, 2)

    sums = Sums(scal)
    outs = sums.out(576), sums.out(576)
    s3.second(sums, *outs)
    s4.first(sums, *outs, 192)
    seq.carry(s5.send)
    u, v = sums.run(seq, "sums_4b")
    s5.core(*seq.carried)
    s4.x1st, s4.y1st = s3.x2nd, s3.y2nd = ring.x(u), ring.y(v)
    outputs = call_ff_out(seq, plan, scal, x1_last, a4_last, vecs[1], pieces, 0)

    sums = Sums(scal)
    s5.first(sums, sums.out(512), sums.out(512))
    u, v = sums.run(seq, "sums_4c")
    s5.x1st, s5.y1st = ring.x(u), ring.y(v)

    sums = Sums(scal)
    s4.second(sums, sums.out(192), sums.out(192))
    third_pair(sums, s3)
    seq.hold(got_ba)
    u, v, keep_c0, send = sums.run(seq, "sums_5")
    s4.x2nd, s4.y2nd = ring.x(u), ring.y(v)
    got_c0 = ring.z_xor(send, 2)

    sums = Sums(scal)
    s5.second(sums, sums.out(256), sums.out(256))
    third_pair(sums, s4)
    out = sums.out(384)
    fourth(sums, out, 0, keep_c, got_c)
    fourth(sums, out, 96, keep_ba, got_ba)
    fourth(sums, out, 288, keep_c0, got_c0)
    u, v, keep_b0, send, last1 = sums.run(seq, "sums_6")
    s5.x2nd, s5.y2nd = ring.x(u), ring.y(v)
    got_b0 = ring.z_xor(send, 2)
    last1 = ring.z_xor(last1, 1)

    sums = Sums(scal)
    third_direct(sums, s5)
    out = sums.out(96)
    fourth(sums, out, 0, keep_b0, got_b0)
    seq.hold(last1)
    *parts, last0 = sums.run(seq, "sums_7")
    parts = parts[:1] + [ring.z(parts[k], k) for k in (1, 2, 3)]
    last0 = ring.z_xor(last0, 1)
    grads = finish(seq, scal, [keep_c, got_c, keep_ba, got_ba, last1, keep_c0, got_c0, keep_b0, got_b0, last0, *parts])
    down, *rows = grads[3:]
    return outputs, input_gradient, *grads[:3], down.transpose(0, 2, 1), *(v.transpose(1, 0, 2) for v in rows)


def whole_shards(inputs, lengths, in_projection, out_projection, up_weight, down_weight, norm_gains, biases, hidden_gains, hidden_biases, cotangent):
    plan = Plan(False)
    seq = Seq(False)
    scal = jnp.concatenate([lengths[0], jnp.zeros((6,), jnp.int32)])

    def full(w):
        return lax.all_gather(lax.all_gather(w, "fsdp", axis=1, tiled=True), "dp", axis=0, tiled=True)

    def rows(v, width):
        return jnp.pad(lax.all_gather(v, "dp", axis=1, tiled=True).astype(F32), ((0, VROWS - v.shape[0]), (0, 0)))

    vecs, hids, pieces = [], [], []
    for l in range(LAYERS):
        qkv = full(in_projection[l]).reshape(D, 4, 9 * HD)
        out = full(out_projection[l]).reshape(D, 4, 192)
        a = jnp.concatenate([qkv[:, :, :512].reshape(D, 2048), jnp.concatenate([qkv[:, :, 512:], out], axis=2).reshape(D, 1024)], axis=1)
        b = full(up_weight[l])
        c = full(down_weight[l]).reshape(4, D, D).transpose(0, 2, 1)
        shape = (4, 2, 2, 48, FF)
        got = [a.reshape(shape), b.reshape(shape), c.reshape(4, 4, 2, 2, 48, D)]
        pieces.append(got)
        vecs.append(rows(jnp.concatenate([norm_gains[l], biases[l]], axis=0), D))
        hid = rows(jnp.concatenate([hidden_gains[l], hidden_biases[l]], axis=0), FF)
        hids.append(jnp.roll(hid, HROW, axis=0))
    pb = [proj_bias(v) for v in vecs]
    x = inputs
    kept = []
    for l in range(LAYERS):
        x1, a1, un, p, o, a2 = call_attn_fwd(seq, plan, scal, x, vecs[l], pb[l], pieces[l], 0)
        x2, a3, sl, n4, a4 = call_ff_fwd(seq, plan, scal, x1, vecs[l], hids[l], pieces[l], 0, 0)
        kept.append((x, x1, a1, un, p, o, a2, a3, sl, n4, a4))
        x = x2
    places = jnp.arange(inputs.shape[0], dtype=jnp.int32)[:, None]
    outputs = x * (seg_of(scal, places) < SEQS).astype(F32)
    dy = cotangent
    layer_grads = [None] * LAYERS
    for l in reversed(range(LAYERS)):
        x, x1, a1, un, p, o, a2, a3, sl, n4, a4 = kept[l]
        last = l == LAYERS - 1
        (dx1, gva, gh), (gb, gc) = call_ff_bwd(seq, plan, scal, dy, x1, a3, sl, n4, a4, vecs[l], hids[l], pieces[l], 0, 0, last, True)
        (dy, gvb), (ga,) = call_attn_bwd(seq, plan, scal, dx1, x, a1, un, p, o, a2, vecs[l], pieces[l], 0, ())
        layer_grads[l] = (ga, gb, gc, gva + gvb, gh)

    def scatter(g):
        g = lax.psum_scatter(g.astype(BF), "dp", scatter_dimension=0, tiled=True)
        return lax.psum_scatter(g, "fsdp", scatter_dimension=1, tiled=True).astype(F32)

    def scatter_rows(v):
        v = lax.psum_scatter(v.astype(BF), "dp", scatter_dimension=1, tiled=True).astype(F32)
        return lax.psum(v, "fsdp")

    res = []
    for l in range(LAYERS):
        ga, gb, gc, gv, gh = layer_grads[l]
        ga = ga.reshape(4, D, D).transpose(1, 0, 2)
        gv = scatter_rows(gv[:10])
        gh = scatter_rows(gh[HROW : HROW + 3])
        res.append(
            (
                scatter(ga[:, :, :576].reshape(D, 3 * D)),
                scatter(ga[:, :, 576:].reshape(D, D)),
                scatter(gb.reshape(4, D, D).transpose(1, 0, 2).reshape(D, FF)),
                scatter(gc.reshape(4, D, D).transpose(0, 2, 1).reshape(FF, D)),
                gv[:3],
                gv[3:],
                gh[:1],
                gh[1:],
            )
        )
    return (outputs, dy, *(jnp.stack([r[i] for r in res]) for i in range(8)))


def solution(mesh):
    dp, fsdp = mesh.shape["dp"], mesh.shape["fsdp"]
    both = P(("dp", "fsdp"), None)
    mat = P(None, "dp", "fsdp")
    row = P(None, None, "dp")
    ring = Ring(dp, fsdp)
    shards = functools.partial(fast_shards, ring) if (dp, fsdp) == (8, 4) else whole_shards
    return jax.shard_map(
        shards,
        mesh=mesh,
        in_specs=(both, both, mat, mat, mat, mat, row, row, row, row, both),
        out_specs=(both, both, mat, mat, mat, mat, row, row, row, row),
        check_vma=False,
    )
```

```python
import functools
import math

import jax
import jax.numpy as jnp
from jax import lax
from jax.experimental import pallas as pl
from jax.experimental.pallas import tpu as pltpu
from jax.sharding import PartitionSpec as P

HEADS = 12
HD = 64
LAYERS = 2
SEQS = 2
D = 768
FF = 3072
T = 256
EPS = 1e-05
BF = jnp.bfloat16
F32 = jnp.float32
MIB = 1 << 20

ANY = pl.BlockSpec(memory_space=pltpu.HBM)
SMEM = pl.BlockSpec(memory_space=pltpu.SMEM)
VMEM = pl.BlockSpec(memory_space=pltpu.VMEM)
LAZY = object()


class Lazy:
    def __init__(self, far, near, sem, out):
        self.near = near
        self.copy = pltpu.make_async_copy(near, far, sem) if out else pltpu.make_async_copy(far, near, sem)
        self.flying = False

    def begin(self):
        self.copy.start()
        self.flying = True

    def ready(self):
        if self.flying:
            self.copy.wait()
            self.flying = False
        return self.near


def begin(*operands):
    for v in operands:
        v.begin()

G1, G2, G3, C1, BQ, BV, C2, BO, C3, B2 = range(10)
VROWS = 16
HROW = 10
G4, B1, C4 = 10, 11, 12

RB = 64


def dot(a, b):
    return jnp.dot(a, b, preferred_element_type=F32)


def dot_nt(a, b):
    return lax.dot_general(a, b, (((1,), (1,)), ((), ())), preferred_element_type=F32)


def ln_stats(v):
    m = jnp.mean(v, axis=-1, keepdims=True)
    cen = v - m
    inv = lax.rsqrt(jnp.mean(cen * cen, axis=-1, keepdims=True) + EPS)
    return cen * inv, inv


def ln_back(dn, g, n, inv):
    e = dn * g
    dv = inv * (e - jnp.mean(e, axis=-1, keepdims=True) - n * jnp.mean(e * n, axis=-1, keepdims=True))
    return dv, jnp.sum(dn * n, axis=0, keepdims=True), jnp.sum(dn, axis=0, keepdims=True)


def seg_of(scal, places):
    e0 = scal[0]
    e1 = scal[0] + scal[1]
    return (places >= e0).astype(jnp.int32) + (places >= e1).astype(jnp.int32)


class Plan:
    def __init__(self, fast):
        self.fast = fast

    def load_a(self, scal, pieces, m, dst):
        if not self.fast:
            return [(pieces[0], dst)]
        out = []
        for h, ri, x, f, ref in self._pieces(scal, pieces):
            src = ref.at[ri, :, pl.ds(m * 48, 48)]
            out.append((src.at[:, :, pl.ds(0, 512)], dst.at[:, x, h, :, pl.ds(pl.multiple_of(f * 512, 512), 512)]))
            out.append((src.at[:, :, pl.ds(512, 256)], dst.at[:, x, h, :, pl.ds(pl.multiple_of(2048 + f * 256, 256), 256)]))
        return out

    def load_b(self, scal, pieces, m, dst):
        if not self.fast:
            return [(pieces[1], dst)]
        return [
            (ref.at[ri, :, pl.ds(m * 48, 48)], dst.at[:, x, h, :, pl.ds(pl.multiple_of(f * 768, 768), 768)])
            for h, ri, x, f, ref in self._pieces(scal, pieces)
        ]

    def load_c(self, scal, pieces, m, dst):
        if not self.fast:
            return [(pieces[2], dst)]
        pieces = pieces[-8:]
        return [
            (
                ref.at[ri, :, pl.ds(m * 48, 48), pl.ds(j * 384, 384)],
                dst.at[:, f, j, h, :, pl.ds(pl.multiple_of(x * 384, 384), 384)],
            )
            for h, ri, x, f, ref in self._pieces(scal, pieces)
            for j in range(2)
        ]

    def _pieces(self, scal, pieces):
        mx, my, mc = scal[3], scal[4], scal[5]
        for h in range(2):
            for bi in range(4):
                ro, rc = bi % 2, bi // 2
                for ri in range(2):
                    rx, ry = (ri, ro) if h == 0 else (ro, ri)
                    x = lax.rem(mx + rx, 2)
                    y = lax.rem(my + ry, 2)
                    c = lax.rem(mc + rc, 2)
                    yield h, ri, x, y * 2 + c, pieces[h * 4 + bi]


    def blocks(self, scal):
        if not self.fast:
            return [(f, 0, 0) for f in range(4)]
        my, mc = scal[4], scal[5]
        return [(lax.rem(my + ry, 2) * 2 + lax.rem(mc + rc, 2), rc, ry) for rc in (1, 0) for ry in (1, 0)]

    @staticmethod
    def half(outs, rc, h):
        return outs[1 + h] if rc == 1 and len(outs) == 3 else outs[rc].at[h]

    def store_ab(self, scal, src, outs, m, f, rc, ry):
        if not self.fast:
            return [(src, outs[0].at[f])]
        res = []
        for rx in range(2):
            x = lax.rem(scal[3] + rx, 2)
            for h in range(2):
                first, second = (rx, ry) if h == 0 else (ry, rx)
                res.append((src.at[:, x, h], outs[rc].at[h, first, second, :, pl.ds(m * 48, 48)]))
        return res

    def store_c(self, scal, src, outs, m):
        if not self.fast:
            return [(src, outs[1])]
        res = []
        for f, rc, ry in self.blocks(scal):
            for rx in range(2):
                x = lax.rem(scal[3] + rx, 2)
                for h in range(2):
                    first, second = (rx, ry) if h == 0 else (ry, rx)
                    for j in range(2):
                        res.append(
                            (
                                src.at[:, f, j, h, :, pl.ds(pl.multiple_of(x * 384, 384), 384)],
                                self.half(outs, rc, h).at[first, second, :, pl.ds(m * 48, 48), pl.ds(j * 384, 384)],
                            )
                        )
        return res

    def store_vec(self, scal, src, outs):
        res = []
        for _, rc, ry in self.blocks(scal):
            for rx in range(2):
                x = lax.rem(scal[3] + rx, 2)
                for h in range(2):
                    first, second = (rx, ry) if h == 0 else (ry, rx)
                    res.append((src.at[h, :, x], outs[rc].at[h, first, second, :, pl.ds(48, 16)]))
        return res


def flat(pieces):
    arrays, finds = [], []
    for piece in pieces:
        array, index = piece if isinstance(piece, tuple) else (piece, None)
        place = next((i for i, v in enumerate(arrays) if v is array), len(arrays))
        if place == len(arrays):
            arrays.append(array)
        finds.append((place, index))
    return arrays, lambda refs: [refs[i] if j is None else refs[i].at[j] for i, j in finds]


def start(copies, sems, base=0):
    made = [pltpu.make_async_copy(s, d, sems.at[base + i]) for i, (s, d) in enumerate(copies)]
    for c in made:
        c.start()
    return made


def wait(made):
    for c in made:
        c.wait()


def attn_fwd(plan, npieces, find, m, *refs):
    scal, x_in, vec_in, pb_in = refs[:4]
    pieces = find(refs[4 : 4 + npieces])
    x1_out, a1_out, un_out, p_out, o_out, a2_out = refs[4 + npieces : 10 + npieces]
    wa, sems = refs[10 + npieces :]
    begin(x_in, vec_in)
    loads = start(plan.load_a(scal, pieces, m, wa), sems)
    begin(pb_in)
    x_ref, vec_ref = x_in.ready(), vec_in.ready()
    n1, _ = ln_stats(x_ref[...])
    a1 = (n1 * vec_ref[G1 : G1 + 1] + vec_ref[C1 : C1 + 1]).astype(BF)
    a1_out.near[...] = a1
    a1_out.begin()
    seg_row = seg_of(scal, lax.broadcasted_iota(jnp.int32, (T, T), 1))
    seg_col = seg_of(scal, lax.broadcasted_iota(jnp.int32, (T, T), 0))
    same = seg_row == seg_col
    pb_ref, un_ref = pb_in.ready(), un_out.near
    wait(loads)
    for f in range(4):
        part = dot(a1, wa[:, :, :, :, 512 * f : 512 * f + 512].reshape(D, 512)) + pb_ref[0:1, 512 * f : 512 * f + 512]
        last = dot(a1, wa[:, :, :, :, 2048 + 256 * f : 2176 + 256 * f].reshape(D, 128)) + pb_ref[0:1, 2048 + 128 * f : 2176 + 128 * f]
        for j in range(9):
            u = 9 * f + j
            val = part[:, 64 * j : 64 * j + 64] if j < 8 else last[:, 0:64]
            val = val.astype(BF)
            if u < HEADS:
                val = val * BF(0.125)
            un_ref[u] = val
    un_out.begin()
    o_ref = o_out.near
    for h in range(HEADS):
        s = jnp.where(same, dot_nt(un_ref[h], un_ref[HEADS + h]), -1e30)
        ex = jnp.exp(s - jnp.max(s, axis=-1, keepdims=True))
        p = ex * (1.0 / jnp.sum(ex, axis=-1, keepdims=True))
        p_out.near[h] = p
        o_ref[:, 64 * h : 64 * h + 64] = dot(p.astype(BF), un_ref[2 * HEADS + h])
    p_out.begin()
    o_out.begin()
    n2, _ = ln_stats(o_ref[...])
    a2 = (n2 * vec_ref[G2 : G2 + 1] + vec_ref[C2 : C2 + 1]).astype(BF)
    a2_out.near[...] = a2
    a2_out.begin()
    z = [dot(a2, wa[:, :, :, :, 2048 + 256 * f : 2304 + 256 * f].reshape(D, 256))[:, 64:] for f in range(4)]
    x1_out.near[...] = x_ref[...] + (jnp.concatenate(z, axis=1) + vec_ref[BO : BO + 1])
    x1_out.begin()


def hidden_rows(hid_ref, sl_ref, n4_ref, a4_ref):
    def rows_step(i, carry):
        rows = pl.ds(i * RB, RB)
        total = jnp.zeros((RB, 1), F32)
        for f in range(4):
            cols = slice(768 * f, 768 * f + 768)
            u = n4_ref[rows, cols]
            phi_c = 0.5 * (1.0 + lax.erf(u * (1.0 / math.sqrt(2.0))))
            r = u * phi_c
            sl_ref[rows, cols] = phi_c + u * (jnp.exp(-0.5 * u * u) * (1.0 / math.sqrt(2.0 * math.pi)))
            n4_ref[rows, cols] = r
            total += jnp.sum(r, axis=-1, keepdims=True)
        mean = total * (1.0 / FF)
        total = jnp.zeros((RB, 1), F32)
        for f in range(4):
            cols = slice(768 * f, 768 * f + 768)
            cen = n4_ref[rows, cols] - mean
            total += jnp.sum(cen * cen, axis=-1, keepdims=True)
        inv = lax.rsqrt(total * (1.0 / FF) + EPS)
        for f in range(4):
            cols = slice(768 * f, 768 * f + 768)
            n4 = (n4_ref[rows, cols] - mean) * inv
            n4_ref[rows, cols] = n4
            a4_ref[rows, cols] = (n4 * hid_ref[G4 : G4 + 1, cols] + hid_ref[C4 : C4 + 1, cols]).astype(BF)
            sl_ref[rows, cols] = sl_ref[rows, cols] * inv
        return carry

    lax.fori_loop(0, T // RB, rows_step, 0)


def hidden(x1_in, vec_in, hid_in, wb, load_b, a3_out, sl_out, n4_out, a4_out):
    x1_ref, vec_ref = x1_in.ready(), vec_in.ready()
    n3, _ = ln_stats(x1_ref[...])
    a3 = (n3 * vec_ref[G3 : G3 + 1] + vec_ref[C3 : C3 + 1]).astype(BF)
    a3_out.near[...] = a3
    a3_out.begin()
    hid_ref = hid_in.ready()
    n4_ref = n4_out.near
    wait(load_b)
    for f in range(4):
        cols = slice(768 * f, 768 * f + 768)
        n4_ref[:, cols] = dot(a3, wb[:, :, :, :, cols].reshape(D, 768)) + hid_ref[B1 : B1 + 1, cols]
    hidden_rows(hid_ref, sl_out.near, n4_ref, a4_out.near)
    begin(a4_out, n4_out, sl_out)


def down(x1_in, vec_in, a4_ref, wc):
    x1_ref, vec_ref = x1_in.ready(), vec_in.ready()
    acc = dot_nt(a4_ref[:, 0:768], wc[0].reshape(D, 768))
    for z in range(1, 4):
        acc += dot_nt(a4_ref[:, 768 * z : 768 * z + 768], wc[z].reshape(D, 768))
    return x1_ref[...] + (acc + vec_ref[B2 : B2 + 1])


def valid_rows(scal):
    seg = seg_of(scal, lax.broadcasted_iota(jnp.int32, (T, 1), 0))
    return (seg < SEQS).astype(F32)


def ff_fwd(plan, npieces, find, mb, mc, *refs):
    scal, x1_in, vec_in, hid_in = refs[:4]
    pieces = find(refs[4 : 4 + npieces])
    x2_out, a3_out, sl_out, n4_out, a4_out = refs[4 + npieces : 9 + npieces]
    wb, wc, sems = refs[9 + npieces :]
    begin(x1_in, vec_in)
    load_b = start(plan.load_b(scal, pieces, mb, wb), sems)
    begin(hid_in)
    load_c = start(plan.load_c(scal, pieces, mc, wc), sems, len(load_b))
    hidden(x1_in, vec_in, hid_in, wb, load_b, a3_out, sl_out, n4_out, a4_out)
    wait(load_c)
    x2_out.near[...] = down(x1_in, vec_in, a4_out.near, wc)
    x2_out.begin()


def ff_mid(plan, npieces, find, nouts, mb, *refs):
    scal, x1_in, dy_in, vec_in, hid_in = refs[:5]
    pieces = find(refs[5 : 5 + npieces])
    a3_out, sl_out, n4_out, a4_out = refs[5 + npieces : 9 + npieces]
    outs = refs[9 + npieces : 9 + npieces + nouts]
    wb, gc, sems = refs[9 + npieces + nouts :]
    begin(x1_in, vec_in)
    load_b = start(plan.load_b(scal, pieces, mb, wb), sems)
    begin(hid_in, dy_in)
    hidden(x1_in, vec_in, hid_in, wb, load_b, a3_out, sl_out, n4_out, a4_out)
    dz2t = (dy_in.ready()[...] * valid_rows(scal)).astype(BF).T
    for z in range(4):
        gc[z] = dot(dz2t, a4_out.near[:, 768 * z : 768 * z + 768]).astype(BF).reshape(4, 2, 2, 48, 768)
    wait(start(plan.store_c(scal, gc, outs, 0), sems, len(load_b)))


def down_grad(plan, nouts, *refs):
    scal, dy_in, a4_in = refs[:3]
    outs = refs[3 : 3 + nouts]
    gc, sems = refs[3 + nouts :]
    begin(dy_in, a4_in)
    dz2t = dy_in.ready()[...].astype(BF).T
    a4_ref = a4_in.ready()
    for z in range(4):
        gc[z] = dot(dz2t, a4_ref[:, 768 * z : 768 * z + 768]).astype(BF).reshape(4, 2, 2, 48, 768)
    wait(start(plan.store_c(scal, gc, outs, 0), sems))


def ff_out(plan, npieces, find, mc, *refs):
    scal, x1_in, a4_in, vec_in = refs[:4]
    pieces = find(refs[4 : 4 + npieces])
    out, wc, sems = refs[4 + npieces :]
    load_c = start(plan.load_c(scal, pieces, mc, wc), sems)
    begin(a4_in, x1_in, vec_in)
    wait(load_c)
    out.near[...] = down(x1_in, vec_in, a4_in.ready(), wc) * valid_rows(scal)
    out.begin()


def eights(v):
    return jnp.sum(v.reshape(v.shape[0] // 8, 8, v.shape[1]), axis=0)


def ff_bwd(plan, npieces, find, nouts, mb, mc, last, with_c, *refs):
    scal, dy_in, x1_in, a3_in, sl_in, n4_in, a4_in, vec_in, hid_in = refs[:9]
    pieces = find(refs[9 : 9 + npieces])
    dx1_out, gv_out, gh_out = refs[9 + npieces : 12 + npieces]
    outs = refs[12 + npieces : 12 + npieces + nouts]
    wb, wc, gb, da4, du_ref, sums, sems = refs[12 + npieces + nouts : 19 + npieces + nouts]
    gc = refs[19 + npieces + nouts] if with_c else None
    begin(dy_in)
    load_c = start(plan.load_c(scal, pieces, mc, wc), sems)
    if with_c:
        begin(a4_in)
    begin(n4_in, hid_in, sl_in)
    load_b = start(plan.load_b(scal, pieces, mb, wb), sems, len(load_c))
    begin(a3_in, x1_in, vec_in)
    base = len(load_c) + len(load_b)
    gv_ref, gh_ref = gv_out.near, gh_out.near
    dy = dy_in.ready()[...]
    if last:
        dy = dy * valid_rows(scal)
    dz2 = dy.astype(BF)
    gv_ref[...] = jnp.zeros_like(gv_ref)
    gh_ref[...] = jnp.zeros_like(gh_ref)
    sums[...] = jnp.zeros_like(sums)
    gv_ref[B2 : B2 + 1] = jnp.sum(dz2.astype(F32), axis=0, keepdims=True)
    dz2t = dz2.T if with_c else None
    wait(load_c)
    for z in range(4):
        cols = slice(768 * z, 768 * z + 768)
        da4[:, cols] = dot(dz2, wc[z].reshape(D, 768))
        if with_c:
            gc[z] = dot(dz2t, a4_in.ready()[:, cols]).astype(BF).reshape(4, 2, 2, 48, 768)
    saves = start(plan.store_c(scal, gc, outs, 1), sems, base) if with_c else []
    base += len(saves)
    n4_ref, hid_ref, sl_ref = n4_in.ready(), hid_in.ready(), sl_in.ready()

    def rows_step(i, carry):
        rows = pl.ds(i * RB, RB)
        s1 = jnp.zeros((RB, 1), F32)
        s2 = jnp.zeros((RB, 1), F32)
        for z in range(4):
            cols = slice(768 * z, 768 * z + 768)
            da = da4[rows, cols]
            n4 = n4_ref[rows, cols]
            dn = da * n4
            e = da * hid_ref[G4 : G4 + 1, cols]
            da4[rows, cols] = e
            s1 += jnp.sum(e, axis=-1, keepdims=True)
            s2 += jnp.sum(e * n4, axis=-1, keepdims=True)
            sums[0, :, cols] += eights(dn)
            sums[1, :, cols] += eights(da)
        s1 = s1 * (1.0 / FF)
        s2 = s2 * (1.0 / FF)
        for z in range(4):
            cols = slice(768 * z, 768 * z + 768)
            du = (sl_ref[rows, cols] * (da4[rows, cols] - s1 - n4_ref[rows, cols] * s2)).astype(BF)
            du_ref[rows, cols] = du
            sums[2, :, cols] += eights(du.astype(F32))
        return carry

    lax.fori_loop(0, T // RB, rows_step, 0)
    for i, row in enumerate((G4, C4, B1)):
        gh_ref[row : row + 1] = jnp.sum(sums[i], axis=0, keepdims=True)
    gh_out.begin()
    a3t = a3_in.ready()[...].T
    wait(load_b)
    da3 = jnp.zeros((T, D), F32)
    for i, (f, rc, ry) in enumerate(plan.blocks(scal)):
        cols = pl.ds(pl.multiple_of(f * 768, 768), 768)
        du = du_ref[:, cols]
        gb[i] = dot(a3t, du).astype(BF).reshape(4, 2, 2, 48, 768)
        more = start(plan.store_ab(scal, gb.at[i], outs, 0, f, rc, ry), sems, base)
        base += len(more)
        saves += more
        da3 += dot_nt(du, wb[:, :, :, :, cols].reshape(D, 768))
    n3, inv3 = ln_stats(x1_in.ready()[...])
    vec_ref = vec_in.ready()
    part, dg3, dc3 = ln_back(da3, vec_ref[G3 : G3 + 1], n3, inv3)
    gv_ref[G3 : G3 + 1] = dg3
    gv_ref[C3 : C3 + 1] = dc3
    dx1_out.near[...] = dy + part
    begin(dx1_out, gv_out)
    wait(saves)


def attn_bwd(plan, npieces, find, nouts, m, fold, *refs):
    scal, dx1_in, x_in, a1_in, un_in, p_in, o_in, a2_in, vec_in = refs[:9]
    pos = 9
    others = refs[pos : pos + (5 if fold else 0)]
    pos += len(others)
    pieces = find(refs[pos : pos + npieces])
    pos += npieces
    dx_out, gv_out = refs[pos : pos + 2]
    outs = refs[pos + 2 : pos + 2 + nouts]
    scratch = refs[pos + 2 + nouts :]
    wa, ga, dpm, dzp, do_ref = scratch[:5]
    vblk = scratch[5] if fold else None
    sems = scratch[-1]
    begin(dx1_in)
    loads = start(plan.load_a(scal, pieces, m, wa), sems)
    begin(o_in, vec_in, un_in, p_in, a1_in, a2_in, x_in, *others)
    base = len(loads)
    gv_ref = gv_out.near
    dx1 = dx1_in.ready()[...]
    dz = dx1.astype(BF)
    gv_ref[...] = jnp.zeros_like(gv_ref)
    gv_ref[BO : BO + 1] = jnp.sum(dz.astype(F32), axis=0, keepdims=True)
    dzp[...] = jnp.concatenate(
        [jnp.concatenate([jnp.zeros((T, 64), BF), dz[:, 192 * f : 192 * f + 192]], axis=1) for f in range(4)], axis=1
    )
    n2, inv2 = ln_stats(o_in.ready()[...])
    vec_ref = vec_in.ready()
    wait(loads)
    da2 = dot_nt(dzp[...], wa[:, :, :, :, 2048:3072].reshape(D, 1024))
    do, dg2, dc2 = ln_back(da2, vec_ref[G2 : G2 + 1], n2, inv2)
    gv_ref[G2 : G2 + 1] = dg2
    gv_ref[C2 : C2 + 1] = dc2
    do = do.astype(BF)
    for f in range(4):
        dpm[:, 2048 + 256 * f : 2304 + 256 * f] = jnp.zeros((T, 256), BF)
    un_ref, p_ref = un_in.ready(), p_in.ready()
    do_t = do.T
    for h in range(HEADS):
        doh = do[:, 64 * h : 64 * h + 64]
        p = p_ref[h]
        q, k, v = un_ref[h], un_ref[HEADS + h], un_ref[2 * HEADS + h]
        dv = dot(do_t[64 * h : 64 * h + 64], p.astype(BF)).T
        dp = dot_nt(doh, v)
        delta = jnp.sum(p * dp, axis=-1, keepdims=True)
        ds = (p * (dp - delta)).astype(BF)
        dq = dot(ds, k) * 0.125
        dk = dot(q.T, ds).T
        for which, grad in ((0, dq), (1, dk), (2, dv)):
            u = which * HEADS + h
            f, j = divmod(u, 9)
            lane = 512 * f + 64 * j if j < 8 else 2048 + 256 * f
            grad = grad.astype(BF)
            dpm[:, lane : lane + 64] = grad
            if which != 1:
                row = BQ if which == 0 else BV
                gv_ref[row : row + 1, 64 * h : 64 * h + 64] = jnp.sum(grad.astype(F32), axis=0, keepdims=True)
    a1t = a1_in.ready()[...].T
    a2t = a2_in.ready()[...].T
    saves = []
    for i, (f, rc, ry) in enumerate(plan.blocks(scal)):
        main = dpm[:, pl.ds(pl.multiple_of(f * 512, 512), 512)]
        tail = dpm[:, pl.ds(pl.multiple_of(2048 + f * 256, 256), 256)]
        ga[i, :, :, :, :, 0:512] = dot(a1t, main).astype(BF).reshape(4, 2, 2, 48, 512)
        ga[i, :, :, :, :, 512:768] = (
            (dot(a1t, tail) + dot(a2t, dzp[:, pl.ds(pl.multiple_of(f * 256, 256), 256)])).astype(BF).reshape(4, 2, 2, 48, 256)
        )
        more = start(plan.store_ab(scal, ga.at[i], outs, m, f, rc, ry), sems, base)
        base += len(more)
        saves += more
    da1 = dot_nt(dpm[...], wa[...].reshape(D, FF))
    n1, inv1 = ln_stats(x_in.ready()[...])
    part, dg1, dc1 = ln_back(da1, vec_ref[G1 : G1 + 1], n1, inv1)
    gv_ref[G1 : G1 + 1] = dg1
    gv_ref[C1 : C1 + 1] = dc1
    dx_out.near[...] = dx1 + part
    begin(dx_out, gv_out)
    if fold:
        va0, vb1, va1, gh0, gh1 = (r.ready()[...] for r in others)
        v0 = gv_ref[...] + va0
        v1 = vb1 + va1
        for d in range(8):
            c96 = slice(96 * d, 96 * d + 96)
            c384 = slice(384 * d, 384 * d + 384)
            low = jnp.concatenate([v0[:, c96], v1[:, c96], jnp.zeros((VROWS, 576), F32)], axis=1)
            vblk[0, d // 2, d % 2] = low.astype(BF)
            vblk[1, d // 2, d % 2] = jnp.concatenate([gh0[:, c384], gh1[:, c384]], axis=1).astype(BF)
        more = start(plan.store_vec(scal, vblk, outs), sems, base)
        saves += more
    wait(saves)


def cost(flops, nbytes):
    return pl.CostEstimate(flops=int(flops), bytes_accessed=int(nbytes), transcendentals=0)


class Seq:
    def __init__(self, chained):
        self.chained = chained
        self.token = None
        self.held = []
        self.carrying = []
        self.carried = []

    def hold(self, *arrays):
        self.held += arrays

    def carry(self, *arrays):
        self.carrying = list(arrays)

    def __call__(self, kernel, out_shape, in_specs, out_specs, args, scratch=(), mib=24, **options):
        deps = [self.token] if self.chained and self.token is not None else []
        deps += self.held
        carried = self.carrying
        self.held, self.carrying = [], []
        parts = {i: v[1] for i, v in enumerate(args) if isinstance(v, tuple)}
        args = [v[0] if isinstance(v, tuple) else v for v in args]
        n, k, m, q = len(args), len(deps), len(carried), len(out_shape)
        lazy_in = [i for i, v in enumerate(in_specs) if v is LAZY]
        lazy_out = [i for i, v in enumerate(out_specs) if v is LAZY]
        lazy_scratch = [pltpu.VMEM(args[i].shape[i in parts :], args[i].dtype) for i in lazy_in]
        lazy_scratch += [pltpu.VMEM(out_shape[i].shape, out_shape[i].dtype) for i in lazy_out]
        if lazy_scratch:
            lazy_scratch.append(pltpu.SemaphoreType.DMA((len(lazy_scratch),)))

        def body(*refs):
            first = n + k + m
            ins, outs = list(refs[:n]), list(refs[first : first + q])
            rest = list(refs[first + q + m :])
            near = rest[len(scratch) :]
            made = []
            for j, (group, i) in enumerate([(ins, i) for i in lazy_in] + [(outs, i) for i in lazy_out]):
                if group is ins and i in parts:
                    group[i] = group[i].at[parts[i]]
                made.append(Lazy(group[i], near[j], near[-1].at[j], group is outs))
                group[i] = made[-1]
            kernel(*ins, *outs, *rest[: len(scratch)])
            for v in made:
                v.ready()

        res = pl.pallas_call(
            body,
            out_shape=tuple(out_shape) + tuple(S(v.shape, v.dtype) for v in carried),
            in_specs=[ANY if v is LAZY else v for v in in_specs] + [ANY] * (k + m),
            out_specs=tuple(ANY if v is LAZY else v for v in out_specs) + (ANY,) * m,
            scratch_shapes=list(scratch) + lazy_scratch,
            input_output_aliases={n + k + i: q + i for i in range(m)},
            compiler_params=pltpu.CompilerParams(vmem_limit_bytes=mib * MIB),
            **options,
        )(*args, *deps, *carried)
        self.token = res[0]
        self.carried = list(res[q:])
        return res[:q]


WA = pltpu.VMEM((4, 2, 2, 48, FF), BF)
WC = pltpu.VMEM((4, 4, 2, 2, 48, D), BF)
S = jax.ShapeDtypeStruct
WBYTES = D * FF * 2


def call_attn_fwd(seq, plan, scal, x, vec, pbias, pieces, m, weight=1.0):
    pieces, find = flat(pieces)
    n = len(pieces)
    return seq(
        functools.partial(attn_fwd, plan, n, find, m),
        (S((T, D), F32), S((T, D), BF), S((36, T, HD), BF), S((HEADS, T, T), F32), S((T, D), F32), S((T, D), BF)),
        [SMEM, LAZY, LAZY, LAZY] + [ANY] * n,
        [LAZY] * 6,
        (scal, x, vec, pbias, *pieces),
        [WA, pltpu.SemaphoreType.DMA((32,))],
        cost_estimate=cost(weight * 2 * T * D * FF * 6, weight * WBYTES),
        name="attn_fwd",
        mib=64,
    )


def call_ff_fwd(seq, plan, scal, x1, vec, hid, pieces, mb, mc, weight=1.0):
    pieces, find = flat(pieces)
    n = len(pieces)
    return seq(
        functools.partial(ff_fwd, plan, n, find, mb, mc),
        (S((T, D), F32), S((T, D), BF), S((T, FF), F32), S((T, FF), F32), S((T, FF), BF)),
        [SMEM, LAZY, LAZY, LAZY] + [ANY] * n,
        [LAZY] * 5,
        (scal, x1, vec, hid, *pieces),
        [WA, WC, pltpu.SemaphoreType.DMA((48,))],
        cost_estimate=cost(weight * 2 * T * D * FF * 6, weight * 2 * WBYTES),
        name="ff_fwd",
        mib=64,
    )


def call_ff_mid(seq, plan, scal, x1, dy, vec, hid, pieces, mb):
    pieces, find = flat(pieces)
    n = len(pieces)
    g = grad_shapes(plan, 1)
    res = seq(
        functools.partial(ff_mid, plan, n, find, len(g), mb),
        (S((T, D), BF), S((T, FF), F32), S((T, FF), F32), S((T, FF), BF), *g),
        [SMEM] + [LAZY] * 4 + [ANY] * n,
        [LAZY] * 4 + [ANY] * len(g),
        (scal, x1, dy, vec, hid, *pieces),
        [WA, WC, pltpu.SemaphoreType.DMA((48,))],
        cost_estimate=cost(2 * T * D * FF * 6, 2 * WBYTES + 8e6),
        name="ff_mid",
        mib=64,
    )
    return res[:4], res[4:]


def call_down_grad(seq, plan, scal, dy, a4):
    g = grad_shapes(plan, 1, split=True)
    return seq(
        functools.partial(down_grad, plan, len(g)),
        g,
        [SMEM, LAZY, LAZY],
        [ANY] * len(g),
        (scal, dy, a4),
        [WC, pltpu.SemaphoreType.DMA((32,))],
        cost_estimate=cost(T * D, T * D),
        name="ff_down_grad",
        mib=64,
    )


def call_ff_out(seq, plan, scal, x1, a4, vec, pieces, mc):
    pieces, find = flat(pieces)
    n = len(pieces)
    return seq(
        functools.partial(ff_out, plan, n, find, mc),
        [S((T, D), F32)],
        [SMEM, LAZY, LAZY, LAZY] + [ANY] * n,
        [LAZY],
        (scal, x1, a4, vec, *pieces),
        [WC, pltpu.SemaphoreType.DMA((32,))],
        cost_estimate=cost(2 * T * D * FF * 3, WBYTES + 3e6),
        name="ff_out",
        mib=64,
    )[0]


def grad_shapes(plan, n, extra=0, split=False):
    if not plan.fast:
        return [S((4, 4, 2, 2, 48, D), BF)] * n
    shape = (2, 2, 2, 4, n * 48 + extra, D)
    return [S(shape, BF)] + ([S(shape[1:], BF)] * 2 if split else [S(shape, BF)])


def call_ff_bwd(seq, plan, scal, dy, x1, a3, sl, n4, a4, vec, hid, pieces, mb, mc, last, with_c, weight=1.0):
    pieces, find = flat(pieces)
    n = len(pieces)
    g = grad_shapes(plan, 2 if with_c else 1)
    res = seq(
        functools.partial(ff_bwd, plan, n, find, len(g), mb, mc, last, with_c),
        (S((T, D), F32), S((VROWS, D), F32), S((VROWS, FF), F32), *g),
        [SMEM] + [LAZY] * 8 + [ANY] * n,
        [LAZY] * 3 + [ANY] * len(g),
        (scal, dy, x1, a3, sl, n4, a4, vec, hid, *pieces),
        [WA, WC, WC, pltpu.VMEM((T, FF), F32), pltpu.VMEM((T, FF), BF), pltpu.VMEM((3, 8, FF), F32), pltpu.SemaphoreType.DMA((112,))] + [WC] * with_c,
        cost_estimate=cost(weight * 2 * T * D * FF * 8, weight * 4 * WBYTES),
        name="ff_bwd",
        mib=64,
    )
    return res[:3], res[3:]


def call_attn_bwd(seq, plan, scal, dx1, x, a1, un, p, o, a2, vec, pieces, m, others, weight=1.0):
    pieces, find = flat(pieces)
    n = len(pieces)
    fold = len(others) > 0
    g = grad_shapes(plan, 1, 16 if fold else 0)
    vblk = [pltpu.VMEM((2, 4, 2, VROWS, D), BF)] if fold else []
    res = seq(
        functools.partial(attn_bwd, plan, n, find, len(g), m, fold),
        (S((T, D), F32), S((VROWS, D), F32), *g),
        [SMEM] + [LAZY] * (8 + len(others)) + [ANY] * n,
        [LAZY] * 2 + [ANY] * len(g),
        (scal, dx1, x, a1, un, p, o, a2, vec, *others, *pieces),
        [WA, WC, pltpu.VMEM((T, FF), BF), pltpu.VMEM((T, 1024), BF), pltpu.VMEM((T, D), BF), *vblk, pltpu.SemaphoreType.DMA((64,))],
        cost_estimate=cost(weight * 2 * T * D * FF * 8, weight * (2 * WBYTES + 8e6)),
        name="attn_bwd",
        mib=64,
    )
    return res[:2], res[2:]


def shift(n, k):
    return [(i, (i + k) % n) for i in range(n)]


class Ring:
    def __init__(self, dp, fsdp):
        self.X = fsdp // 2
        self.Z = dp // self.X
        self.dp, self.fsdp = dp, fsdp

    def z(self, v, k):
        return lax.ppermute(v, "dp", [(z * self.X + x, (z + k) % self.Z * self.X + x) for z in range(self.Z) for x in range(self.X)])

    def z_xor(self, v, k):
        return lax.ppermute(v, "dp", [(i, i ^ (k * self.X)) for i in range(self.dp)])

    def x(self, v):
        return lax.ppermute(v, "dp", [(i, i ^ 1) for i in range(self.dp)])

    def y(self, v):
        return lax.ppermute(v, "fsdp", [(i, i ^ 2) for i in range(self.fsdp)])

    def c(self, v):
        return lax.ppermute(v, "fsdp", [(i, i ^ 1) for i in range(self.fsdp)])


def pack_a_kernel(l, wqkv, wo, out):
    out[...] = jnp.concatenate([wqkv[l], wo[l]], axis=1)


def pack_a(seq, l, wqkv, wo):
    return seq(
        functools.partial(pack_a_kernel, l),
        [S((96, D), BF)],
        [VMEM] * 2,
        [VMEM],
        (wqkv, wo),
        cost_estimate=cost(0, 4 * 96 * D),
        name="pack_a",
    )[0]


def pack_bc_rows(l, w1, w2, out, first, second):
    t = w2[l]
    for i, at in enumerate((first, second)):
        out[at : at + 48] = w1[l, 48 * i : 48 * i + 48]
        for j in range(2):
            out[at + 48 : at + 96, 384 * j : 384 * j + 384] = t[96 * j + 48 * i : 96 * j + 48 * i + 48]


def pack_bc_kernel(l, w1, w2, out):
    pack_bc_rows(l, w1, w2, out, 0, 96)


def pack_bc(seq, l, w1, w2):
    return seq(
        functools.partial(pack_bc_kernel, l),
        [S((192, D), BF)],
        [VMEM] * 2,
        [VMEM],
        (w1, w2),
        cost_estimate=cost(0, 4 * 192 * D),
        name="pack_bc",
    )[0]


def pack_ab_kernel(l, wqkv, wo, w1, ng, bi, hg, hb, out):
    def column(v, u, w, first):
        v = jnp.concatenate([v.astype(F32), u.astype(F32)], axis=0)
        parts = [jnp.zeros((first, w), F32)] if first else []
        return jnp.concatenate(parts + [v, jnp.zeros((VROWS - first - v.shape[0], w), F32)], axis=0)

    a = jnp.concatenate([wqkv[l], wo[l]], axis=1)
    for i in range(2):
        out[112 * i : 112 * i + 48] = a[48 * i : 48 * i + 48]
        out[112 * i + 48 : 112 * i + 96] = w1[l, 48 * i : 48 * i + 48]
    low = [column(ng[i], bi[i], 96, 0) for i in range(LAYERS)]
    hid = [column(hg[i], hb[i], 384, HROW) for i in range(LAYERS)]
    low = jnp.concatenate(low + [jnp.zeros((VROWS, 576), F32)], axis=1)
    out[96:112] = (low + jnp.concatenate(hid, axis=1)).astype(BF)
    out[208:224] = jnp.zeros((VROWS, D), BF)


def pack_ab(seq, l, weights, vectors):
    return seq(
        functools.partial(pack_ab_kernel, l),
        [S((224, D), BF)],
        [VMEM] * 7,
        [VMEM],
        (*weights, *vectors),
        cost_estimate=cost(0, 4 * 224 * D),
        name="pack_ab",
    )[0]


def pack_c_kernel(l, w2, o1, o2):
    t = w2[l]
    for i, out in enumerate((o1, o2)):
        for j in range(2):
            out[:, 384 * j : 384 * j + 384] = t[96 * j + 48 * i : 96 * j + 48 * i + 48]


def pack_c(seq, l, w2):
    return seq(
        functools.partial(pack_c_kernel, l),
        [S((48, D), BF)] * 2,
        [VMEM],
        [VMEM] * 2,
        (w2,),
        cost_estimate=cost(0, 4 * 96 * D),
        name="pack_c",
    )


def join_kernel(a, b, c, d, o1, o2):
    o1[0] = a[...]
    o1[1] = b[...]
    o2[0] = c[...]
    o2[1] = d[...]


def join(seq, *parts):
    shape = S((2, *parts[0].shape), BF)
    return seq(join_kernel, [shape] * 2, [VMEM] * 4, [VMEM] * 2, parts, cost_estimate=cost(0, 16 * parts[0].size), name="join")


Q_CUTS = ((0, 2), (2, 1), (3, 1))


def zquad_kernel(scal, *refs):
    high = scal[2] // 2
    out = refs[-1]
    first = 0
    for k in range(0, len(refs) - 1, 2):
        rows = refs[k].shape[1]
        for part, pos in ((refs[k], high), (refs[k + 1], 1 - high)):
            for i in range(2):
                for r in range(rows):
                    for ri in range(2):
                        out[first + r, ri, 2 * pos + i] = part[i, r, ri]
        first += rows


def zquad(seq, scal, *parts):
    return seq(
        zquad_kernel,
        [S((2, 2, 4, 48, D), BF)],
        [SMEM] + [VMEM] * len(parts),
        [VMEM],
        (scal, *parts),
        cost_estimate=cost(0, 64 * 48 * D),
        name="zquad",
        mib=64,
    )[0]


def zcat_kernel(r1, scal, *refs):
    n = (len(refs) - 2) if len(refs) == 6 else (len(refs) - 3)
    o1, o2 = refs[n : n + 2]
    for k, ref in enumerate(refs[:4]):
        z = lax.rem(scal[2] + 4 - k, 4)
        o1[z] = ref[0:r1]
        o2[z] = ref[r1:]
    for i, ref in enumerate(refs[4:n]):
        refs[-1][i] = ref[...]


def zcat(seq, scal, parts, r1, *riders):
    r2 = parts[0].shape[0] - r1
    outs = [S((4, r1, D), BF), S((4, r2, D), BF)]
    if riders:
        outs.append(S((len(riders), *riders[0].shape), BF))
    return seq(
        functools.partial(zcat_kernel, r1),
        outs,
        [SMEM] + [VMEM] * (4 + len(riders)),
        [VMEM] * len(outs),
        (scal, *parts, *riders),
        cost_estimate=cost(0, 8 * (r1 + r2) * D * 2),
        name="zcat",
    )


def pile_kernel(cuts, h1, x1, h2, y2, *outs):
    for i, (first, rows) in enumerate(cuts):
        mine = pl.ds(first, rows)
        for j, parts in enumerate(((h1, x1), (h2, y2))):
            for k, part in enumerate(parts):
                outs[2 * i + j][k] = part[:, mine]
                if len(outs) > 2 * len(cuts):
                    outs[-1][j, k] = part[:, mine]


def pile(seq, parts, cuts, again=False):
    outs = [S((2, 4, rows, D), BF) for _, rows in cuts for _ in range(2)]
    if again:
        outs.append(S((2, *outs[0].shape), BF))
    return seq(
        functools.partial(pile_kernel, cuts),
        outs,
        [VMEM] * 4,
        [VMEM] * len(outs),
        parts,
        cost_estimate=cost(0, 64 * sum(rows for _, rows in cuts) * D),
        name="pile",
    )


def pile_last_kernel(cuts, scal, h1, x1, h2, y2, q, q_got, *refs):
    n = 2 * len(cuts)
    pile_kernel(cuts, h1, x1, h2, y2, *refs[:n])
    low = lax.rem(scal[2], 2)
    for (first, rows), out in zip(Q_CUTS, refs[n:]):
        out[low] = q[first : first + rows]
        out[1 - low] = q_got[first : first + rows]
    vecs, hids, biases = refs[-3:]
    own = lax.convert_element_type(scal[3] == 0, F32)
    for l in range(LAYERS):
        low, high = [], []
        for z in range(4):
            mine, other = h1[z, 96:112].astype(F32), x1[z, 96:112].astype(F32)
            for rows in (own * mine + (1 - own) * other, own * other + (1 - own) * mine):
                low.append(rows[:, 96 * l : 96 * l + 96])
                high.append(rows[:, 384 * l : 384 * l + 384])
        vec = jnp.concatenate(low, axis=1)
        vecs[l] = vec
        hids[l] = jnp.concatenate(high, axis=1)
        bias = jnp.concatenate([vec[BQ : BQ + 1], jnp.zeros((1, D), F32), vec[BV : BV + 1]], axis=1)
        parts = [bias[:, 576 * f : 576 * f + 512] for f in range(4)]
        for f in range(4):
            parts += [bias[:, 576 * f + 512 : 576 * f + 576], jnp.zeros((1, 64), F32)]
        biases[l] = jnp.concatenate(parts, axis=1)


def pile_last(seq, scal, parts, cuts, q, q_got):
    outs = [S((2, 4, rows, D), BF) for _, rows in cuts for _ in range(2)]
    outs += [S((2, rows, *q.shape[1:]), BF) for _, rows in Q_CUTS]
    outs += [S((LAYERS, VROWS, D), F32), S((LAYERS, VROWS, FF), F32), S((LAYERS, 1, 2560), F32)]
    res = seq(
        functools.partial(pile_last_kernel, cuts),
        outs,
        [SMEM] + [VMEM] * 6,
        [VMEM] * len(outs),
        (scal, *parts, q, q_got),
        cost_estimate=cost(0, 64 * sum(rows for _, rows in cuts) * D),
        name="pile_last",
    )
    n = 2 * len(cuts)
    return res[:n], res[n : n + 3], *([(v, l) for l in range(LAYERS)] for v in res[n + 3 :])


def merge_kernel(*refs):
    for i, ref in enumerate(refs[:-1]):
        refs[-1][i] = ref[...]


def merge(seq, *parts):
    shape = (len(parts), *parts[0].shape)
    return seq(merge_kernel, [S(shape, BF)], [VMEM] * len(parts), [VMEM], parts, cost_estimate=cost(0, 4 * math.prod(shape)), name="merge")[0]


def total(refs):
    out = refs[0].astype(F32)
    for r in refs[1:]:
        out = out + r.astype(F32)
    return out


class Sums:
    def __init__(self, scal):
        self.scal = scal
        self.arrays = []
        self.outs = []
        self.sums = []

    def source(self, array):
        for i, v in enumerate(self.arrays):
            if v is array:
                return i
        self.arrays.append(array)
        return len(self.arrays) - 1

    def out(self, *shape):
        self.outs.append(shape)
        return len(self.outs) - 1

    def add(self, out, where, sources, rows):
        self.sums.append((out, where, [(self.source(v), at, deep) for v, at, deep in sources], rows))

    def run(self, seq, name):
        n, q = len(self.arrays), len(self.outs)
        copies = sum(len(v[2]) for v in self.sums)
        sums = self.sums

        def kernel(scal, *refs):
            arrays, outs = refs[:n], refs[n : n + q]
            ins, made, sems = refs[n + q : n + q + copies], refs[n + q + copies : -1], refs[-1]
            pairs = [(arrays[i].at[at(scal)], ins[j]) for j, (i, at, _) in enumerate(v for t in sums for v in t[2])]
            loads = start(pairs, sems)
            saves, first = [], 0
            for t, (out, where, sources, rows) in enumerate(sums):
                mine = range(first, first + len(sources))
                first += len(sources)
                wait([loads[j] for j in mine])
                made[t][...] = total([ins[j][...].reshape(rows, D) for j in mine]).astype(BF)
                saves += start([(made[t], outs[out].at[where(scal)])], sems, copies + t)
            wait(saves)

        scratch = [pltpu.VMEM((4, t[3] // 4, D) if deep else (t[3], D), BF) for t in sums for _, _, deep in t[2]]
        scratch += [pltpu.VMEM((t[3], D), BF) for t in sums]
        return seq(
            kernel,
            [S((*v, D), BF) for v in self.outs],
            [SMEM] + [ANY] * n,
            [ANY] * q,
            (self.scal, *self.arrays),
            scratch + [pltpu.SemaphoreType.DMA((copies + len(sums),))],
            cost_estimate=cost(0, 2 * D * sum(t[3] * (1 + len(t[2])) for t in sums)),
            name=name,
            mib=64,
        )


def finish_kernel(scal, *refs):
    in_out, out_out, up_out, down_out, gain_out, bias_out, hgain_out, hbias_out = refs[17:]
    i = lax.rem(scal[2], 2)
    c1 = total([refs[0][i], refs[1][i], refs[4][0:96]])
    c0 = total([refs[2][i], refs[3][i], refs[4][96:192]])
    ba1, b0, rows_a = (total([r[...] for r in refs[k : k + 4]]) for k in (5, 9, 13))
    for l in range(LAYERS):
        for r in range(3):
            gain_out[r, l : l + 1] = rows_a[48 + r : 49 + r, 96 * l : 96 * l + 96]
        for r in range(7):
            bias_out[r, l : l + 1] = rows_a[51 + r : 52 + r, 96 * l : 96 * l + 96]
        hid = rows_a[112 + HROW : 115 + HROW, 384 * l : 384 * l + 384]
        hgain_out[0, l : l + 1] = hid[0:1]
        hbias_out[0, l : l + 1] = hid[1:2]
        hbias_out[1, l : l + 1] = hid[2:3]
    a0 = jnp.concatenate([rows_a[:48], rows_a[64:112]], axis=0)
    for l, a, b, c in ((0, a0, b0, c0), (1, ba1[96:], ba1[:96], c1)):
        in_out[l] = a[:, :576]
        out_out[l] = a[:, 576:]
        up_out[l] = b
        for j in range(2):
            down_out[l, 96 * j : 96 * j + 96] = c[:, 384 * j : 384 * j + 384]


def finish(seq, scal, parts):
    return seq(
        finish_kernel,
        [S((2, 96, 576), F32), S((2, 96, 192), F32), S((2, 96, D), F32), S((2, 192, 384), F32), S((3, 2, 96), F32), S((7, 2, 96), F32), S((1, 2, 384), F32), S((2, 2, 384), F32)],
        [SMEM] + [VMEM] * len(parts),
        [VMEM] * 8,
        (scal, *parts),
        cost_estimate=cost(0, 8e6),
        name="finish",
        mib=64,
    )


class Gather:
    def __init__(self, seq, ring, scal):
        self.seq, self.ring, self.scal = seq, ring, scal

    def z_all(self, pack):
        self.parts = [pack] + [self.ring.z(pack, k) for k in (1, 2, 3)]

    def xy_first(self, *riders):
        h1, h2, *rest = zcat(self.seq, self.scal, self.parts, self.parts[0].shape[0] // 2, *riders)
        self.both = h1, self.ring.x(h1), h2, self.ring.y(h2)
        return rest[0] if riders else None

    def xy_second(self, h1, h2):
        self.h1, self.h2 = h1, h2
        self.y1, self.x2 = self.ring.y(self.h1), self.ring.x(self.h2)

    def core(self):
        both = self.ring.c(merge(self.seq, self.h1, self.y1, self.h2, self.x2))
        self.other = [(both, i) for i in range(4)]
        return both

    def pieces(self):
        return [self.h1, self.y1, *self.other[:2], self.h2, self.x2, *self.other[2:]]


def rows_at(first, rows):
    return lambda scal: (pl.ds(first, rows),)


class Scatter:
    def __init__(self, ring, grads):
        self.ring = ring
        self.keep, *self.send = grads
        self.rows = self.keep.shape[4]

    def core(self, *send):
        self.got = [self.ring.c(v) for v in send]
        return self.got

    def pair(self, index):
        if len(self.got) == 1:
            return [(v, index) for v in (self.keep, self.got[0])]
        return [(self.keep, index), (self.got[index(None)[0]], lambda scal: index(scal)[1:])]

    def both(self, *index):
        return [(v, at, True) for v, at in self.pair(lambda scal: index)]

    def first(self, sums, x, y, at=0):
        self.at1 = at
        r = 4 * self.rows
        for h, out in ((0, x), (1, y)):
            for s in range(2):
                sums.add(out, rows_at(at + s * r, r), self.both(h, 1, s), r)

    def second(self, sums, x, y, at=0):
        self.at2 = at
        r = 4 * self.rows
        for h, got, out in ((0, self.x1st, y), (1, self.y1st, x)):
            sums.add(out, rows_at(at, r), self.both(h, 0, 1) + [(got, rows_at(self.at1 + r, r), False)], r)

    def block(self, sums, out, where, z):
        n = self.rows
        for h, a, b in ((0, self.x1st, self.y2nd), (1, self.y1st, self.x2nd)):

            def local(scal, h=h):
                return (h, 0, 0, 0 if scal is None else z(scal))

            def sent(first):
                return lambda scal: (pl.ds(pl.multiple_of(first + z(scal) * n, 16), n),)

            sources = [(v, at, False) for v, at in self.pair(local)]
            sources += [(a, sent(self.at1), False), (b, sent(self.at2), False)]
            sums.add(out, where(h * n, n), sources, n)


def third_pair(sums, *chunks):
    outs = [sums.out(2, sum(2 * c.rows for c in chunks)) for _ in range(2)]
    for k in (1, 0):
        for i in range(2):

            def z(scal, k=k, i=i):
                high = scal[2] // 2
                return 2 * (1 - high if k else high) + i

            at = 0
            for c in chunks:
                c.block(sums, outs[k], lambda first, n, i=i, at=at: lambda scal: (i, pl.ds(at + first, n)), z)
                at += 2 * c.rows
    return outs


def third_direct(sums, *chunks):
    outs = [sums.out(sum(2 * c.rows for c in chunks)) for _ in range(4)]
    for k in (1, 2, 3, 0):
        at = 0
        for c in chunks:
            c.block(sums, outs[k], lambda first, n, at=at: rows_at(at + first, n), lambda scal, k=k: lax.rem(scal[2] + k, 4))
            at += 2 * c.rows
    return outs


def fourth(sums, out, at, keep, got):
    rows = keep.shape[1]
    where = lambda scal: (1 - lax.rem(scal[2], 2),)
    sums.add(out, rows_at(at, rows), [(keep, where, False), (got, where, False)], rows)


def proj_bias(vec):
    full = jnp.concatenate([vec[BQ], jnp.zeros((D,), F32), vec[BV]]).reshape(4, 9 * HD)
    return jnp.concatenate(
        [full[:, :512].reshape(2048), jnp.pad(full[:, 512:], ((0, 0), (0, 64))).reshape(512)]
    ).reshape(1, 2560)


def fast_shards(ring, inputs, lengths, in_projection, out_projection, up_weight, down_weight, norm_gains, biases, hidden_gains, hidden_biases, cotangent):
    plan = Plan(True)
    seq = Seq(True)
    dpi, fi = lax.axis_index("dp"), lax.axis_index("fsdp")
    xme = dpi % ring.X
    place = jnp.stack([dpi // ring.X, xme, fi // 2, fi % 2]).astype(jnp.int32)
    scal = jnp.concatenate([lengths[0], place, jnp.zeros((2,), jnp.int32)])

    down_weight = down_weight.transpose(0, 2, 1)

    a, b, c, d = (Gather(seq, ring, scal) for _ in range(4))
    a.z_all(pack_a(seq, 0, in_projection, out_projection))
    q1, q2 = pack_c(seq, 1, down_weight)
    q1, q2 = join(seq, q1, ring.x(q1), q2, ring.y(q2))
    q1_got, q2_got = ring.y(q1), ring.x(q2)
    seq.hold(q1_got, q2_got)
    a.xy_first()
    b.z_all(pack_bc(seq, 0, up_weight, down_weight))
    cd = pack_ab(seq, 1, (in_projection, out_projection, up_weight), (norm_gains, biases, hidden_gains, hidden_biases))
    seq.hold(b.parts[1])
    a.xy_second(*pile(seq, a.both, ((0, 48),)))
    seq.hold(a.y1, a.x2)
    b.xy_first()
    c.z_all(cd)
    q = merge(seq, q1, q1_got, q2, q2_got)
    seq.hold(a.core(), c.parts[3])
    *h, own = pile(seq, b.both, ((0, 96),), True)
    b.xy_second(*h)
    b.own = ring.c(own)
    kept = [None, None]
    x = inputs
    seq.hold(b.y1, b.x2, b.own)
    rest = ring.c(c.xy_first(b.y1, b.x2))
    b.other = [(b.own, 0), (rest, 0), (b.own, 1), (rest, 1)]
    seq.hold(rest)
    h, parts_q, vecs, hids, pb = pile_last(seq, scal, c.both, ((0, 48), (48, 48)), q, ring.z_xor(q, 1))
    c.xy_second(*h[:2])
    d.xy_second(*h[2:])
    x1, a1, un, p, o, a2 = call_attn_fwd(seq, plan, scal, x, vecs[0], pb[0], a.pieces(), 0, 0.01)
    got_q = [ring.z_xor(v, 2) for v in parts_q]
    x2, a3, sl, n4, a4 = call_ff_fwd(seq, plan, scal, x1, vecs[0], hids[0], b.pieces(), 0, 1, 0.01)
    kept[0] = (x, x1, a1, un, p, o, a2, a3, sl, n4, a4)
    x = x2
    seq.hold(d.y1, d.x2, got_q[0])
    c.core()
    d.core()
    x1, a1, un, p, o, a2 = call_attn_fwd(seq, plan, scal, x, vecs[1], pb[1], c.pieces(), 0)
    q1 = zquad(seq, scal, parts_q[0], got_q[0])
    (a3, sl, n4, a4), grads = call_ff_mid(seq, plan, scal, x1, cotangent, vecs[1], hids[1], d.pieces(), 0)
    seq.carry(grads[1])
    q2 = zquad(seq, scal, parts_q[1], got_q[1], parts_q[2], got_q[2])
    grads = grads[0], *seq.carried
    pieces_c = [(v, i) for v in (q1, ring.c(q1), q2, ring.c(q2)) for i in range(2)]

    sc = Scatter(ring, grads)
    sc.core(*sc.send)
    sums = Sums(scal)
    sc.first(sums, sums.out(384), sums.out(384))
    u, v = sums.run(seq, "sums_0")
    sc.x1st, sc.y1st = ring.x(u), ring.y(v)

    pieces = d.pieces() + pieces_c
    (dx1, gva1, gh1), grads = call_ff_bwd(seq, plan, scal, cotangent, x1, a3, sl, n4, a4, vecs[1], hids[1], pieces, 0, 0, True, False)
    sb = Scatter(ring, grads)

    sums = Sums(scal)
    sc.second(sums, sums.out(192), sums.out(192))
    seq.carry(*sb.send)
    u, v = sums.run(seq, "sums_1")
    sb.core(*seq.carried)
    sc.x2nd, sc.y2nd = ring.x(u), ring.y(v)

    x1_last, a4_last = x1, a4
    (dy, gvb1), grads = call_attn_bwd(seq, plan, scal, dx1, x, a1, un, p, o, a2, vecs[1], c.pieces(), 0, ())
    sa = Scatter(ring, grads)

    sums = Sums(scal)
    third_pair(sums, sc)
    seq.carry(*sa.send)
    keep_c, send = sums.run(seq, "sums_2a")
    sa.core(*seq.carried)
    got_c = ring.z_xor(send, 2)

    sums = Sums(scal)
    outs = sums.out(784), sums.out(784)
    sb.first(sums, *outs)
    sa.first(sums, *outs, 384)
    u, v = sums.run(seq, "sums_2b")
    sb.x1st, sb.y1st = sa.x1st, sa.y1st = ring.x(u), ring.y(v)

    x, x1, a1, un, p, o, a2, a3, sl, n4, a4 = kept[0]
    s3 = Scatter(ring, call_down_grad(seq, plan, scal, dy, a4))
    s3.core(*s3.send)

    (dx1, gva0, gh0), grads = call_ff_bwd(seq, plan, scal, dy, x1, a3, sl, n4, a4, vecs[0], hids[0], b.pieces(), 0, 1, False, False, 0.01)
    s4 = Scatter(ring, grads)

    sums = Sums(scal)
    outs = sums.out(384), sums.out(384)
    sb.second(sums, *outs)
    sa.second(sums, *outs, 192)
    s3.first(sums, sums.out(384), sums.out(384))
    seq.hold(got_c)
    seq.carry(*s4.send)
    u, v, u3, v3 = sums.run(seq, "sums_3")
    s4.core(*seq.carried)
    sb.x2nd, sb.y2nd = sa.x2nd, sa.y2nd = ring.x(u), ring.y(v)
    s3.x1st, s3.y1st = ring.x(u3), ring.y(v3)

    others = (gva0, gva1, gvb1, gh0, gh1)
    (input_gradient, _), grads = call_attn_bwd(seq, plan, scal, dx1, x, a1, un, p, o, a2, vecs[0], a.pieces(), 0, others, 0.01)
    s5 = Scatter(ring, grads)

    sums = Sums(scal)
    third_direct(sums, sb, sa)
    parts_ba = sums.run(seq, "sums_4a")
    parts_ba = [parts_ba[0]] + [ring.z(parts_ba[k], k) for k in (1, 2, 3)]

    sums = Sums(scal)
    outs = sums.out(576), sums.out(576)
    s3.second(sums, *outs)
    s4.first(sums, *outs, 192)
    seq.carry(*s5.send)
    u, v = sums.run(seq, "sums_4b")
    s5.core(*seq.carried)
    s4.x1st, s4.y1st = s3.x2nd, s3.y2nd = ring.x(u), ring.y(v)
    outputs = call_ff_out(seq, plan, scal, x1_last, a4_last, vecs[1], pieces, 0)

    sums = Sums(scal)
    s5.first(sums, sums.out(512), sums.out(512))
    u, v = sums.run(seq, "sums_4c")
    s5.x1st, s5.y1st = ring.x(u), ring.y(v)

    sums = Sums(scal)
    s4.second(sums, sums.out(192), sums.out(192))
    third_pair(sums, s3)
    seq.hold(*parts_ba[1:3])
    u, v, keep_c0, send = sums.run(seq, "sums_5")
    s4.x2nd, s4.y2nd = ring.x(u), ring.y(v)
    got_c0 = ring.z_xor(send, 2)

    sums = Sums(scal)
    s5.second(sums, sums.out(256), sums.out(256))
    third_direct(sums, s4)
    seq.hold(got_c0, parts_ba[3])
    u, v, *res = sums.run(seq, "sums_6")
    s5.x2nd, s5.y2nd = ring.x(u), ring.y(v)
    parts_b0 = [res[0]] + [ring.z(res[k], k) for k in (1, 2, 3)]

    sums = Sums(scal)
    third_direct(sums, s5)
    out = sums.out(192)
    fourth(sums, out, 0, keep_c, got_c)
    fourth(sums, out, 96, keep_c0, got_c0)
    seq.hold(*parts_b0[1:])
    *parts, last = sums.run(seq, "sums_7")
    parts = parts[:1] + [ring.z(parts[k], k) for k in (1, 2, 3)]
    last = ring.z_xor(last, 1)
    grads = finish(seq, scal, [keep_c, got_c, keep_c0, got_c0, last, *parts_ba, *parts_b0, *parts])
    down, *rows = grads[3:]
    return outputs, input_gradient, *grads[:3], down.transpose(0, 2, 1), *(v.transpose(1, 0, 2) for v in rows)


def whole_shards(inputs, lengths, in_projection, out_projection, up_weight, down_weight, norm_gains, biases, hidden_gains, hidden_biases, cotangent):
    plan = Plan(False)
    seq = Seq(False)
    scal = jnp.concatenate([lengths[0], jnp.zeros((6,), jnp.int32)])

    def full(w):
        return lax.all_gather(lax.all_gather(w, "fsdp", axis=1, tiled=True), "dp", axis=0, tiled=True)

    def rows(v, width):
        return jnp.pad(lax.all_gather(v, "dp", axis=1, tiled=True).astype(F32), ((0, VROWS - v.shape[0]), (0, 0)))

    vecs, hids, pieces = [], [], []
    for l in range(LAYERS):
        qkv = full(in_projection[l]).reshape(D, 4, 9 * HD)
        out = full(out_projection[l]).reshape(D, 4, 192)
        a = jnp.concatenate([qkv[:, :, :512].reshape(D, 2048), jnp.concatenate([qkv[:, :, 512:], out], axis=2).reshape(D, 1024)], axis=1)
        b = full(up_weight[l])
        c = full(down_weight[l]).reshape(4, D, D).transpose(0, 2, 1)
        shape = (4, 2, 2, 48, FF)
        got = [a.reshape(shape), b.reshape(shape), c.reshape(4, 4, 2, 2, 48, D)]
        pieces.append(got)
        vecs.append(rows(jnp.concatenate([norm_gains[l], biases[l]], axis=0), D))
        hid = rows(jnp.concatenate([hidden_gains[l], hidden_biases[l]], axis=0), FF)
        hids.append(jnp.roll(hid, HROW, axis=0))
    pb = [proj_bias(v) for v in vecs]
    x = inputs
    kept = []
    for l in range(LAYERS):
        x1, a1, un, p, o, a2 = call_attn_fwd(seq, plan, scal, x, vecs[l], pb[l], pieces[l], 0)
        x2, a3, sl, n4, a4 = call_ff_fwd(seq, plan, scal, x1, vecs[l], hids[l], pieces[l], 0, 0)
        kept.append((x, x1, a1, un, p, o, a2, a3, sl, n4, a4))
        x = x2
    places = jnp.arange(inputs.shape[0], dtype=jnp.int32)[:, None]
    outputs = x * (seg_of(scal, places) < SEQS).astype(F32)
    dy = cotangent
    layer_grads = [None] * LAYERS
    for l in reversed(range(LAYERS)):
        x, x1, a1, un, p, o, a2, a3, sl, n4, a4 = kept[l]
        last = l == LAYERS - 1
        (dx1, gva, gh), (gb, gc) = call_ff_bwd(seq, plan, scal, dy, x1, a3, sl, n4, a4, vecs[l], hids[l], pieces[l], 0, 0, last, True)
        (dy, gvb), (ga,) = call_attn_bwd(seq, plan, scal, dx1, x, a1, un, p, o, a2, vecs[l], pieces[l], 0, ())
        layer_grads[l] = (ga, gb, gc, gva + gvb, gh)

    def scatter(g):
        g = lax.psum_scatter(g.astype(BF), "dp", scatter_dimension=0, tiled=True)
        return lax.psum_scatter(g, "fsdp", scatter_dimension=1, tiled=True).astype(F32)

    def scatter_rows(v):
        v = lax.psum_scatter(v.astype(BF), "dp", scatter_dimension=1, tiled=True).astype(F32)
        return lax.psum(v, "fsdp")

    res = []
    for l in range(LAYERS):
        ga, gb, gc, gv, gh = layer_grads[l]
        ga = ga.reshape(4, D, D).transpose(1, 0, 2)
        gv = scatter_rows(gv[:10])
        gh = scatter_rows(gh[HROW : HROW + 3])
        res.append(
            (
                scatter(ga[:, :, :576].reshape(D, 3 * D)),
                scatter(ga[:, :, 576:].reshape(D, D)),
                scatter(gb.reshape(4, D, D).transpose(1, 0, 2).reshape(D, FF)),
                scatter(gc.reshape(4, D, D).transpose(0, 2, 1).reshape(FF, D)),
                gv[:3],
                gv[3:],
                gh[:1],
                gh[1:],
            )
        )
    return (outputs, dy, *(jnp.stack([r[i] for r in res]) for i in range(8)))


def solution(mesh):
    dp, fsdp = mesh.shape["dp"], mesh.shape["fsdp"]
    both = P(("dp", "fsdp"), None)
    mat = P(None, "dp", "fsdp")
    row = P(None, None, "dp")
    ring = Ring(dp, fsdp)
    shards = functools.partial(fast_shards, ring) if (dp, fsdp) == (8, 4) else whole_shards
    return jax.shard_map(
        shards,
        mesh=mesh,
        in_specs=(both, both, mat, mat, mat, mat, row, row, row, row, both),
        out_specs=(both, both, mat, mat, mat, mat, row, row, row, row),
        check_vma=False,
    )
```

```python
import functools
import math

import jax
import jax.numpy as jnp
from jax import lax
from jax.experimental import pallas as pl
from jax.experimental.pallas import tpu as pltpu
from jax.sharding import PartitionSpec as P

HEADS = 12
HD = 64
LAYERS = 2
SEQS = 2
D = 768
FF = 3072
T = 256
EPS = 1e-05
BF = jnp.bfloat16
F32 = jnp.float32
MIB = 1 << 20

ANY = pl.BlockSpec(memory_space=pltpu.HBM)
SMEM = pl.BlockSpec(memory_space=pltpu.SMEM)
VMEM = pl.BlockSpec(memory_space=pltpu.VMEM)
LAZY = object()


class Lazy:
    def __init__(self, far, near, sem, out):
        self.near = near
        self.copy = pltpu.make_async_copy(near, far, sem) if out else pltpu.make_async_copy(far, near, sem)
        self.flying = False

    def begin(self):
        self.copy.start()
        self.flying = True

    def ready(self):
        if self.flying:
            self.copy.wait()
            self.flying = False
        return self.near


def begin(*operands):
    for v in operands:
        v.begin()

G1, G2, G3, C1, BQ, BV, C2, BO, C3, B2 = range(10)
VROWS = 16
HROW = 10
G4, B1, C4 = 10, 11, 12

RB = 64


def dot(a, b):
    return jnp.dot(a, b, preferred_element_type=F32)


def dot_nt(a, b):
    return lax.dot_general(a, b, (((1,), (1,)), ((), ())), preferred_element_type=F32)


def ln_stats(v):
    m = jnp.mean(v, axis=-1, keepdims=True)
    cen = v - m
    inv = lax.rsqrt(jnp.mean(cen * cen, axis=-1, keepdims=True) + EPS)
    return cen * inv, inv


def ln_back(dn, g, n, inv):
    e = dn * g
    dv = inv * (e - jnp.mean(e, axis=-1, keepdims=True) - n * jnp.mean(e * n, axis=-1, keepdims=True))
    return dv, jnp.sum(dn * n, axis=0, keepdims=True), jnp.sum(dn, axis=0, keepdims=True)


def seg_of(scal, places):
    e0 = scal[0]
    e1 = scal[0] + scal[1]
    return (places >= e0).astype(jnp.int32) + (places >= e1).astype(jnp.int32)


class Plan:
    def __init__(self, fast):
        self.fast = fast

    def load_a(self, scal, pieces, m, dst):
        if not self.fast:
            return [(pieces[0], dst)]
        out = []
        for h, ri, x, f, ref in self._pieces(scal, pieces):
            src = ref.at[ri, :, pl.ds(m * 48, 48)]
            out.append((src.at[:, :, pl.ds(0, 512)], dst.at[:, x, h, :, pl.ds(pl.multiple_of(f * 512, 512), 512)]))
            out.append((src.at[:, :, pl.ds(512, 256)], dst.at[:, x, h, :, pl.ds(pl.multiple_of(2048 + f * 256, 256), 256)]))
        return out

    def load_b(self, scal, pieces, m, dst):
        if not self.fast:
            return [(pieces[1], dst)]
        return [
            (ref.at[ri, :, pl.ds(m * 48, 48)], dst.at[:, x, h, :, pl.ds(pl.multiple_of(f * 768, 768), 768)])
            for h, ri, x, f, ref in self._pieces(scal, pieces)
        ]

    def load_c(self, scal, pieces, m, dst):
        if not self.fast:
            return [(pieces[2], dst)]
        pieces = pieces[-8:]
        return [
            (
                ref.at[ri, :, pl.ds(m * 48, 48), pl.ds(j * 384, 384)],
                dst.at[:, f, j, h, :, pl.ds(pl.multiple_of(x * 384, 384), 384)],
            )
            for h, ri, x, f, ref in self._pieces(scal, pieces)
            for j in range(2)
        ]

    def _pieces(self, scal, pieces):
        mx, my, mc = scal[3], scal[4], scal[5]
        for h in range(2):
            for bi in range(4):
                ro, rc = bi % 2, bi // 2
                for ri in range(2):
                    rx, ry = (ri, ro) if h == 0 else (ro, ri)
                    x = lax.rem(mx + rx, 2)
                    y = lax.rem(my + ry, 2)
                    c = lax.rem(mc + rc, 2)
                    yield h, ri, x, y * 2 + c, pieces[h * 4 + bi]


    def blocks(self, scal):
        if not self.fast:
            return [(f, 0, 0) for f in range(4)]
        my, mc = scal[4], scal[5]
        return [(lax.rem(my + ry, 2) * 2 + lax.rem(mc + rc, 2), rc, ry) for rc in (1, 0) for ry in (1, 0)]

    @staticmethod
    def half(outs, rc, h):
        return outs[1 + h] if rc == 1 and len(outs) == 3 else outs[rc].at[h]

    def store_ab(self, scal, src, outs, m, f, rc, ry):
        if not self.fast:
            return [(src, outs[0].at[f])]
        res = []
        for rx in range(2):
            x = lax.rem(scal[3] + rx, 2)
            for h in range(2):
                first, second = (rx, ry) if h == 0 else (ry, rx)
                res.append((src.at[:, x, h], outs[rc].at[h, first, second, :, pl.ds(m * 48, 48)]))
        return res

    def store_c(self, scal, src, outs, m):
        if not self.fast:
            return [(src, outs[1])]
        res = []
        for f, rc, ry in self.blocks(scal):
            for rx in range(2):
                x = lax.rem(scal[3] + rx, 2)
                for h in range(2):
                    first, second = (rx, ry) if h == 0 else (ry, rx)
                    for j in range(2):
                        res.append(
                            (
                                src.at[:, f, j, h, :, pl.ds(pl.multiple_of(x * 384, 384), 384)],
                                self.half(outs, rc, h).at[first, second, :, pl.ds(m * 48, 48), pl.ds(j * 384, 384)],
                            )
                        )
        return res

    def store_vec(self, scal, src, outs):
        res = []
        for _, rc, ry in self.blocks(scal):
            for rx in range(2):
                x = lax.rem(scal[3] + rx, 2)
                for h in range(2):
                    first, second = (rx, ry) if h == 0 else (ry, rx)
                    res.append((src.at[h, :, x], outs[rc].at[h, first, second, :, pl.ds(48, 16)]))
        return res


def flat(pieces):
    arrays, finds = [], []
    for piece in pieces:
        array, index = piece if isinstance(piece, tuple) else (piece, None)
        place = next((i for i, v in enumerate(arrays) if v is array), len(arrays))
        if place == len(arrays):
            arrays.append(array)
        finds.append((place, index))
    return arrays, lambda refs: [refs[i] if j is None else refs[i].at[j] for i, j in finds]


def start(copies, sems, base=0):
    made = [pltpu.make_async_copy(s, d, sems.at[base + i]) for i, (s, d) in enumerate(copies)]
    for c in made:
        c.start()
    return made


def wait(made):
    for c in made:
        c.wait()


def attn_fwd(plan, npieces, find, m, *refs):
    scal, x_in, vec_in, pb_in = refs[:4]
    pieces = find(refs[4 : 4 + npieces])
    x1_out, a1_out, un_out, p_out, o_out, a2_out = refs[4 + npieces : 10 + npieces]
    wa, sems = refs[10 + npieces :]
    begin(x_in, vec_in)
    loads = start(plan.load_a(scal, pieces, m, wa), sems)
    begin(pb_in)
    x_ref, vec_ref = x_in.ready(), vec_in.ready()
    n1, _ = ln_stats(x_ref[...])
    a1 = (n1 * vec_ref[G1 : G1 + 1] + vec_ref[C1 : C1 + 1]).astype(BF)
    a1_out.near[...] = a1
    a1_out.begin()
    seg_row = seg_of(scal, lax.broadcasted_iota(jnp.int32, (T, T), 1))
    seg_col = seg_of(scal, lax.broadcasted_iota(jnp.int32, (T, T), 0))
    same = seg_row == seg_col
    pb_ref, un_ref = pb_in.ready(), un_out.near
    wait(loads)
    for f in range(4):
        part = dot(a1, wa[:, :, :, :, 512 * f : 512 * f + 512].reshape(D, 512)) + pb_ref[0:1, 512 * f : 512 * f + 512]
        last = dot(a1, wa[:, :, :, :, 2048 + 256 * f : 2176 + 256 * f].reshape(D, 128)) + pb_ref[0:1, 2048 + 128 * f : 2176 + 128 * f]
        for j in range(9):
            u = 9 * f + j
            val = part[:, 64 * j : 64 * j + 64] if j < 8 else last[:, 0:64]
            val = val.astype(BF)
            if u < HEADS:
                val = val * BF(0.125)
            un_ref[u] = val
    un_out.begin()
    o_ref = o_out.near
    for h in range(HEADS):
        s = jnp.where(same, dot_nt(un_ref[h], un_ref[HEADS + h]), -1e30)
        ex = jnp.exp(s - jnp.max(s, axis=-1, keepdims=True))
        p = ex * (1.0 / jnp.sum(ex, axis=-1, keepdims=True))
        p_out.near[h] = p
        o_ref[:, 64 * h : 64 * h + 64] = dot(p.astype(BF), un_ref[2 * HEADS + h])
    p_out.begin()
    o_out.begin()
    n2, _ = ln_stats(o_ref[...])
    a2 = (n2 * vec_ref[G2 : G2 + 1] + vec_ref[C2 : C2 + 1]).astype(BF)
    a2_out.near[...] = a2
    a2_out.begin()
    z = [dot(a2, wa[:, :, :, :, 2048 + 256 * f : 2304 + 256 * f].reshape(D, 256))[:, 64:] for f in range(4)]
    x1_out.near[...] = x_ref[...] + (jnp.concatenate(z, axis=1) + vec_ref[BO : BO + 1])
    x1_out.begin()


def hidden_rows(hid_ref, sl_ref, n4_ref, a4_ref):
    def rows_step(i, carry):
        rows = pl.ds(i * RB, RB)
        total = jnp.zeros((RB, 1), F32)
        for f in range(4):
            cols = slice(768 * f, 768 * f + 768)
            u = n4_ref[rows, cols]
            phi_c = 0.5 * (1.0 + lax.erf(u * (1.0 / math.sqrt(2.0))))
            r = u * phi_c
            sl_ref[rows, cols] = phi_c + u * (jnp.exp(-0.5 * u * u) * (1.0 / math.sqrt(2.0 * math.pi)))
            n4_ref[rows, cols] = r
            total += jnp.sum(r, axis=-1, keepdims=True)
        mean = total * (1.0 / FF)
        total = jnp.zeros((RB, 1), F32)
        for f in range(4):
            cols = slice(768 * f, 768 * f + 768)
            cen = n4_ref[rows, cols] - mean
            total += jnp.sum(cen * cen, axis=-1, keepdims=True)
        inv = lax.rsqrt(total * (1.0 / FF) + EPS)
        for f in range(4):
            cols = slice(768 * f, 768 * f + 768)
            n4 = (n4_ref[rows, cols] - mean) * inv
            n4_ref[rows, cols] = n4
            a4_ref[rows, cols] = (n4 * hid_ref[G4 : G4 + 1, cols] + hid_ref[C4 : C4 + 1, cols]).astype(BF)
            sl_ref[rows, cols] = sl_ref[rows, cols] * inv
        return carry

    lax.fori_loop(0, T // RB, rows_step, 0)


def hidden(x1_in, vec_in, hid_in, wb, load_b, a3_out, sl_out, n4_out, a4_out):
    x1_ref, vec_ref = x1_in.ready(), vec_in.ready()
    n3, _ = ln_stats(x1_ref[...])
    a3 = (n3 * vec_ref[G3 : G3 + 1] + vec_ref[C3 : C3 + 1]).astype(BF)
    a3_out.near[...] = a3
    a3_out.begin()
    hid_ref = hid_in.ready()
    n4_ref = n4_out.near
    wait(load_b)
    for f in range(4):
        cols = slice(768 * f, 768 * f + 768)
        n4_ref[:, cols] = dot(a3, wb[:, :, :, :, cols].reshape(D, 768)) + hid_ref[B1 : B1 + 1, cols]
    hidden_rows(hid_ref, sl_out.near, n4_ref, a4_out.near)
    begin(a4_out, n4_out, sl_out)


def down(x1_in, vec_in, a4_ref, wc):
    x1_ref, vec_ref = x1_in.ready(), vec_in.ready()
    acc = dot_nt(a4_ref[:, 0:768], wc[0].reshape(D, 768))
    for z in range(1, 4):
        acc += dot_nt(a4_ref[:, 768 * z : 768 * z + 768], wc[z].reshape(D, 768))
    return x1_ref[...] + (acc + vec_ref[B2 : B2 + 1])


def valid_rows(scal):
    seg = seg_of(scal, lax.broadcasted_iota(jnp.int32, (T, 1), 0))
    return (seg < SEQS).astype(F32)


def ff_fwd(plan, npieces, find, mb, mc, *refs):
    scal, x1_in, vec_in, hid_in = refs[:4]
    pieces = find(refs[4 : 4 + npieces])
    x2_out, a3_out, sl_out, n4_out, a4_out = refs[4 + npieces : 9 + npieces]
    wb, wc, sems = refs[9 + npieces :]
    begin(x1_in, vec_in)
    load_b = start(plan.load_b(scal, pieces, mb, wb), sems)
    begin(hid_in)
    load_c = start(plan.load_c(scal, pieces, mc, wc), sems, len(load_b))
    hidden(x1_in, vec_in, hid_in, wb, load_b, a3_out, sl_out, n4_out, a4_out)
    wait(load_c)
    x2_out.near[...] = down(x1_in, vec_in, a4_out.near, wc)
    x2_out.begin()


def ff_mid(plan, npieces, find, nouts, mb, *refs):
    scal, x1_in, dy_in, vec_in, hid_in = refs[:5]
    pieces = find(refs[5 : 5 + npieces])
    a3_out, sl_out, n4_out, a4_out = refs[5 + npieces : 9 + npieces]
    outs = refs[9 + npieces : 9 + npieces + nouts]
    wb, gc, sems = refs[9 + npieces + nouts :]
    begin(x1_in, vec_in)
    load_b = start(plan.load_b(scal, pieces, mb, wb), sems)
    begin(hid_in, dy_in)
    hidden(x1_in, vec_in, hid_in, wb, load_b, a3_out, sl_out, n4_out, a4_out)
    dz2t = (dy_in.ready()[...] * valid_rows(scal)).astype(BF).T
    for z in range(4):
        gc[z] = dot(dz2t, a4_out.near[:, 768 * z : 768 * z + 768]).astype(BF).reshape(4, 2, 2, 48, 768)
    wait(start(plan.store_c(scal, gc, outs, 0), sems, len(load_b)))


def down_grad(plan, nouts, *refs):
    scal, dy_in, a4_in = refs[:3]
    outs = refs[3 : 3 + nouts]
    gc, sems = refs[3 + nouts :]
    begin(dy_in, a4_in)
    dz2t = dy_in.ready()[...].astype(BF).T
    a4_ref = a4_in.ready()
    for z in range(4):
        gc[z] = dot(dz2t, a4_ref[:, 768 * z : 768 * z + 768]).astype(BF).reshape(4, 2, 2, 48, 768)
    wait(start(plan.store_c(scal, gc, outs, 0), sems))


def ff_out(plan, npieces, find, mc, *refs):
    scal, x1_in, a4_in, vec_in = refs[:4]
    pieces = find(refs[4 : 4 + npieces])
    out, wc, sems = refs[4 + npieces :]
    load_c = start(plan.load_c(scal, pieces, mc, wc), sems)
    begin(a4_in, x1_in, vec_in)
    wait(load_c)
    out.near[...] = down(x1_in, vec_in, a4_in.ready(), wc) * valid_rows(scal)
    out.begin()


def eights(v):
    return jnp.sum(v.reshape(v.shape[0] // 8, 8, v.shape[1]), axis=0)


def ff_bwd(plan, npieces, find, nouts, mb, mc, last, with_c, *refs):
    scal, dy_in, x1_in, a3_in, sl_in, n4_in, a4_in, vec_in, hid_in = refs[:9]
    pieces = find(refs[9 : 9 + npieces])
    dx1_out, gv_out, gh_out = refs[9 + npieces : 12 + npieces]
    outs = refs[12 + npieces : 12 + npieces + nouts]
    wb, wc, gb, da4, du_ref, sums, sems = refs[12 + npieces + nouts : 19 + npieces + nouts]
    gc = refs[19 + npieces + nouts] if with_c else None
    begin(dy_in)
    load_c = start(plan.load_c(scal, pieces, mc, wc), sems)
    if with_c:
        begin(a4_in)
    begin(n4_in, hid_in, sl_in)
    load_b = start(plan.load_b(scal, pieces, mb, wb), sems, len(load_c))
    begin(a3_in, x1_in, vec_in)
    base = len(load_c) + len(load_b)
    gv_ref, gh_ref = gv_out.near, gh_out.near
    dy = dy_in.ready()[...]
    if last:
        dy = dy * valid_rows(scal)
    dz2 = dy.astype(BF)
    gv_ref[...] = jnp.zeros_like(gv_ref)
    gh_ref[...] = jnp.zeros_like(gh_ref)
    sums[...] = jnp.zeros_like(sums)
    gv_ref[B2 : B2 + 1] = jnp.sum(dz2.astype(F32), axis=0, keepdims=True)
    dz2t = dz2.T if with_c else None
    wait(load_c)
    for z in range(4):
        cols = slice(768 * z, 768 * z + 768)
        da4[:, cols] = dot(dz2, wc[z].reshape(D, 768))
        if with_c:
            gc[z] = dot(dz2t, a4_in.ready()[:, cols]).astype(BF).reshape(4, 2, 2, 48, 768)
    saves = start(plan.store_c(scal, gc, outs, 1), sems, base) if with_c else []
    base += len(saves)
    n4_ref, hid_ref, sl_ref = n4_in.ready(), hid_in.ready(), sl_in.ready()

    def rows_step(i, carry):
        rows = pl.ds(i * RB, RB)
        s1 = jnp.zeros((RB, 1), F32)
        s2 = jnp.zeros((RB, 1), F32)
        for z in range(4):
            cols = slice(768 * z, 768 * z + 768)
            da = da4[rows, cols]
            n4 = n4_ref[rows, cols]
            dn = da * n4
            e = da * hid_ref[G4 : G4 + 1, cols]
            da4[rows, cols] = e
            s1 += jnp.sum(e, axis=-1, keepdims=True)
            s2 += jnp.sum(e * n4, axis=-1, keepdims=True)
            sums[0, :, cols] += eights(dn)
            sums[1, :, cols] += eights(da)
        s1 = s1 * (1.0 / FF)
        s2 = s2 * (1.0 / FF)
        for z in range(4):
            cols = slice(768 * z, 768 * z + 768)
            du = (sl_ref[rows, cols] * (da4[rows, cols] - s1 - n4_ref[rows, cols] * s2)).astype(BF)
            du_ref[rows, cols] = du
            sums[2, :, cols] += eights(du.astype(F32))
        return carry

    lax.fori_loop(0, T // RB, rows_step, 0)
    for i, row in enumerate((G4, C4, B1)):
        gh_ref[row : row + 1] = jnp.sum(sums[i], axis=0, keepdims=True)
    gh_out.begin()
    a3t = a3_in.ready()[...].T
    wait(load_b)
    da3 = jnp.zeros((T, D), F32)
    for i, (f, rc, ry) in enumerate(plan.blocks(scal)):
        cols = pl.ds(pl.multiple_of(f * 768, 768), 768)
        du = du_ref[:, cols]
        gb[i] = dot(a3t, du).astype(BF).reshape(4, 2, 2, 48, 768)
        more = start(plan.store_ab(scal, gb.at[i], outs, 0, f, rc, ry), sems, base)
        base += len(more)
        saves += more
        da3 += dot_nt(du, wb[:, :, :, :, cols].reshape(D, 768))
    n3, inv3 = ln_stats(x1_in.ready()[...])
    vec_ref = vec_in.ready()
    part, dg3, dc3 = ln_back(da3, vec_ref[G3 : G3 + 1], n3, inv3)
    gv_ref[G3 : G3 + 1] = dg3
    gv_ref[C3 : C3 + 1] = dc3
    dx1_out.near[...] = dy + part
    begin(dx1_out, gv_out)
    wait(saves)


def attn_bwd(plan, npieces, find, nouts, m, fold, *refs):
    scal, dx1_in, x_in, a1_in, un_in, p_in, o_in, a2_in, vec_in = refs[:9]
    pos = 9
    others = refs[pos : pos + (5 if fold else 0)]
    pos += len(others)
    pieces = find(refs[pos : pos + npieces])
    pos += npieces
    dx_out, gv_out = refs[pos : pos + 2]
    outs = refs[pos + 2 : pos + 2 + nouts]
    scratch = refs[pos + 2 + nouts :]
    wa, ga, dpm, dzp, do_ref = scratch[:5]
    vblk = scratch[5] if fold else None
    sems = scratch[-1]
    begin(dx1_in)
    loads = start(plan.load_a(scal, pieces, m, wa), sems)
    begin(o_in, vec_in, un_in, p_in, a1_in, a2_in, x_in, *others)
    base = len(loads)
    gv_ref = gv_out.near
    dx1 = dx1_in.ready()[...]
    dz = dx1.astype(BF)
    gv_ref[...] = jnp.zeros_like(gv_ref)
    gv_ref[BO : BO + 1] = jnp.sum(dz.astype(F32), axis=0, keepdims=True)
    dzp[...] = jnp.concatenate(
        [jnp.concatenate([jnp.zeros((T, 64), BF), dz[:, 192 * f : 192 * f + 192]], axis=1) for f in range(4)], axis=1
    )
    n2, inv2 = ln_stats(o_in.ready()[...])
    vec_ref = vec_in.ready()
    wait(loads)
    da2 = dot_nt(dzp[...], wa[:, :, :, :, 2048:3072].reshape(D, 1024))
    do, dg2, dc2 = ln_back(da2, vec_ref[G2 : G2 + 1], n2, inv2)
    gv_ref[G2 : G2 + 1] = dg2
    gv_ref[C2 : C2 + 1] = dc2
    do = do.astype(BF)
    for f in range(4):
        dpm[:, 2048 + 256 * f : 2304 + 256 * f] = jnp.zeros((T, 256), BF)
    un_ref, p_ref = un_in.ready(), p_in.ready()
    do_t = do.T
    for h in range(HEADS):
        doh = do[:, 64 * h : 64 * h + 64]
        p = p_ref[h]
        q, k, v = un_ref[h], un_ref[HEADS + h], un_ref[2 * HEADS + h]
        dv = dot(do_t[64 * h : 64 * h + 64], p.astype(BF)).T
        dp = dot_nt(doh, v)
        delta = jnp.sum(p * dp, axis=-1, keepdims=True)
        ds = (p * (dp - delta)).astype(BF)
        dq = dot(ds, k) * 0.125
        dk = dot(q.T, ds).T
        for which, grad in ((0, dq), (1, dk), (2, dv)):
            u = which * HEADS + h
            f, j = divmod(u, 9)
            lane = 512 * f + 64 * j if j < 8 else 2048 + 256 * f
            grad = grad.astype(BF)
            dpm[:, lane : lane + 64] = grad
            if which != 1:
                row = BQ if which == 0 else BV
                gv_ref[row : row + 1, 64 * h : 64 * h + 64] = jnp.sum(grad.astype(F32), axis=0, keepdims=True)
    a1t = a1_in.ready()[...].T
    a2t = a2_in.ready()[...].T
    saves = []
    for i, (f, rc, ry) in enumerate(plan.blocks(scal)):
        main = dpm[:, pl.ds(pl.multiple_of(f * 512, 512), 512)]
        tail = dpm[:, pl.ds(pl.multiple_of(2048 + f * 256, 256), 256)]
        ga[i, :, :, :, :, 0:512] = dot(a1t, main).astype(BF).reshape(4, 2, 2, 48, 512)
        ga[i, :, :, :, :, 512:768] = (
            (dot(a1t, tail) + dot(a2t, dzp[:, pl.ds(pl.multiple_of(f * 256, 256), 256)])).astype(BF).reshape(4, 2, 2, 48, 256)
        )
        more = start(plan.store_ab(scal, ga.at[i], outs, m, f, rc, ry), sems, base)
        base += len(more)
        saves += more
    da1 = dot_nt(dpm[...], wa[...].reshape(D, FF))
    n1, inv1 = ln_stats(x_in.ready()[...])
    part, dg1, dc1 = ln_back(da1, vec_ref[G1 : G1 + 1], n1, inv1)
    gv_ref[G1 : G1 + 1] = dg1
    gv_ref[C1 : C1 + 1] = dc1
    dx_out.near[...] = dx1 + part
    begin(dx_out, gv_out)
    if fold:
        va0, vb1, va1, gh0, gh1 = (r.ready()[...] for r in others)
        v0 = gv_ref[...] + va0
        v1 = vb1 + va1
        for d in range(8):
            c96 = slice(96 * d, 96 * d + 96)
            c384 = slice(384 * d, 384 * d + 384)
            low = jnp.concatenate([v0[:, c96], v1[:, c96], jnp.zeros((VROWS, 576), F32)], axis=1)
            vblk[0, d // 2, d % 2] = low.astype(BF)
            vblk[1, d // 2, d % 2] = jnp.concatenate([gh0[:, c384], gh1[:, c384]], axis=1).astype(BF)
        more = start(plan.store_vec(scal, vblk, outs), sems, base)
        saves += more
    wait(saves)


def cost(flops, nbytes):
    return pl.CostEstimate(flops=int(flops), bytes_accessed=int(nbytes), transcendentals=0)


class Seq:
    def __init__(self, chained):
        self.chained = chained
        self.token = None
        self.held = []
        self.carrying = []
        self.carried = []

    def hold(self, *arrays):
        self.held += arrays

    def carry(self, *arrays):
        self.carrying = list(arrays)

    def __call__(self, kernel, out_shape, in_specs, out_specs, args, scratch=(), mib=24, **options):
        deps = [self.token] if self.chained and self.token is not None else []
        deps += self.held
        carried = self.carrying
        self.held, self.carrying = [], []
        parts = {i: v[1] for i, v in enumerate(args) if isinstance(v, tuple)}
        args = [v[0] if isinstance(v, tuple) else v for v in args]
        n, k, m, q = len(args), len(deps), len(carried), len(out_shape)
        lazy_in = [i for i, v in enumerate(in_specs) if v is LAZY]
        lazy_out = [i for i, v in enumerate(out_specs) if v is LAZY]
        lazy_scratch = [pltpu.VMEM(args[i].shape[i in parts :], args[i].dtype) for i in lazy_in]
        lazy_scratch += [pltpu.VMEM(out_shape[i].shape, out_shape[i].dtype) for i in lazy_out]
        if lazy_scratch:
            lazy_scratch.append(pltpu.SemaphoreType.DMA((len(lazy_scratch),)))

        def body(*refs):
            first = n + k + m
            ins, outs = list(refs[:n]), list(refs[first : first + q])
            rest = list(refs[first + q + m :])
            near = rest[len(scratch) :]
            made = []
            for j, (group, i) in enumerate([(ins, i) for i in lazy_in] + [(outs, i) for i in lazy_out]):
                if group is ins and i in parts:
                    group[i] = group[i].at[parts[i]]
                made.append(Lazy(group[i], near[j], near[-1].at[j], group is outs))
                group[i] = made[-1]
            kernel(*ins, *outs, *rest[: len(scratch)])
            for v in made:
                v.ready()

        res = pl.pallas_call(
            body,
            out_shape=tuple(out_shape) + tuple(S(v.shape, v.dtype) for v in carried),
            in_specs=[ANY if v is LAZY else v for v in in_specs] + [ANY] * (k + m),
            out_specs=tuple(ANY if v is LAZY else v for v in out_specs) + (ANY,) * m,
            scratch_shapes=list(scratch) + lazy_scratch,
            input_output_aliases={n + k + i: q + i for i in range(m)},
            compiler_params=pltpu.CompilerParams(vmem_limit_bytes=mib * MIB),
            **options,
        )(*args, *deps, *carried)
        self.token = res[0]
        self.carried = list(res[q:])
        return res[:q]


WA = pltpu.VMEM((4, 2, 2, 48, FF), BF)
WC = pltpu.VMEM((4, 4, 2, 2, 48, D), BF)
S = jax.ShapeDtypeStruct
WBYTES = D * FF * 2


def call_attn_fwd(seq, plan, scal, x, vec, pbias, pieces, m, weight=1.0):
    pieces, find = flat(pieces)
    n = len(pieces)
    return seq(
        functools.partial(attn_fwd, plan, n, find, m),
        (S((T, D), F32), S((T, D), BF), S((36, T, HD), BF), S((HEADS, T, T), F32), S((T, D), F32), S((T, D), BF)),
        [SMEM, LAZY, LAZY, LAZY] + [ANY] * n,
        [LAZY] * 6,
        (scal, x, vec, pbias, *pieces),
        [WA, pltpu.SemaphoreType.DMA((32,))],
        cost_estimate=cost(weight * 2 * T * D * FF * 6, weight * WBYTES),
        name="attn_fwd",
        mib=64,
    )


def call_ff_fwd(seq, plan, scal, x1, vec, hid, pieces, mb, mc, weight=1.0):
    pieces, find = flat(pieces)
    n = len(pieces)
    return seq(
        functools.partial(ff_fwd, plan, n, find, mb, mc),
        (S((T, D), F32), S((T, D), BF), S((T, FF), F32), S((T, FF), F32), S((T, FF), BF)),
        [SMEM, LAZY, LAZY, LAZY] + [ANY] * n,
        [LAZY] * 5,
        (scal, x1, vec, hid, *pieces),
        [WA, WC, pltpu.SemaphoreType.DMA((48,))],
        cost_estimate=cost(weight * 2 * T * D * FF * 6, weight * 2 * WBYTES),
        name="ff_fwd",
        mib=64,
    )


def call_ff_mid(seq, plan, scal, x1, dy, vec, hid, pieces, mb):
    pieces, find = flat(pieces)
    n = len(pieces)
    g = grad_shapes(plan, 1)
    res = seq(
        functools.partial(ff_mid, plan, n, find, len(g), mb),
        (S((T, D), BF), S((T, FF), F32), S((T, FF), F32), S((T, FF), BF), *g),
        [SMEM] + [LAZY] * 4 + [ANY] * n,
        [LAZY] * 4 + [ANY] * len(g),
        (scal, x1, dy, vec, hid, *pieces),
        [WA, WC, pltpu.SemaphoreType.DMA((48,))],
        cost_estimate=cost(2 * T * D * FF * 6, 2 * WBYTES + 8e6),
        name="ff_mid",
        mib=64,
    )
    return res[:4], res[4:]


def call_down_grad(seq, plan, scal, dy, a4):
    g = grad_shapes(plan, 1, split=True)
    return seq(
        functools.partial(down_grad, plan, len(g)),
        g,
        [SMEM, LAZY, LAZY],
        [ANY] * len(g),
        (scal, dy, a4),
        [WC, pltpu.SemaphoreType.DMA((32,))],
        cost_estimate=cost(T * D, T * D),
        name="ff_down_grad",
        mib=64,
    )


def call_ff_out(seq, plan, scal, x1, a4, vec, pieces, mc):
    pieces, find = flat(pieces)
    n = len(pieces)
    return seq(
        functools.partial(ff_out, plan, n, find, mc),
        [S((T, D), F32)],
        [SMEM, LAZY, LAZY, LAZY] + [ANY] * n,
        [LAZY],
        (scal, x1, a4, vec, *pieces),
        [WC, pltpu.SemaphoreType.DMA((32,))],
        cost_estimate=cost(2 * T * D * FF * 3, WBYTES + 3e6),
        name="ff_out",
        mib=64,
    )[0]


def grad_shapes(plan, n, extra=0, split=False):
    if not plan.fast:
        return [S((4, 4, 2, 2, 48, D), BF)] * n
    shape = (2, 2, 2, 4, n * 48 + extra, D)
    return [S(shape, BF)] + ([S(shape[1:], BF)] * 2 if split else [S(shape, BF)])


def call_ff_bwd(seq, plan, scal, dy, x1, a3, sl, n4, a4, vec, hid, pieces, mb, mc, last, with_c, weight=1.0):
    pieces, find = flat(pieces)
    n = len(pieces)
    g = grad_shapes(plan, 2 if with_c else 1)
    res = seq(
        functools.partial(ff_bwd, plan, n, find, len(g), mb, mc, last, with_c),
        (S((T, D), F32), S((VROWS, D), F32), S((VROWS, FF), F32), *g),
        [SMEM] + [LAZY] * 8 + [ANY] * n,
        [LAZY] * 3 + [ANY] * len(g),
        (scal, dy, x1, a3, sl, n4, a4, vec, hid, *pieces),
        [WA, WC, WC, pltpu.VMEM((T, FF), F32), pltpu.VMEM((T, FF), BF), pltpu.VMEM((3, 8, FF), F32), pltpu.SemaphoreType.DMA((112,))] + [WC] * with_c,
        cost_estimate=cost(weight * 2 * T * D * FF * 8, weight * 4 * WBYTES),
        name="ff_bwd",
        mib=64,
    )
    return res[:3], res[3:]


def call_attn_bwd(seq, plan, scal, dx1, x, a1, un, p, o, a2, vec, pieces, m, others, weight=1.0):
    pieces, find = flat(pieces)
    n = len(pieces)
    fold = len(others) > 0
    g = grad_shapes(plan, 1, 16 if fold else 0)
    vblk = [pltpu.VMEM((2, 4, 2, VROWS, D), BF)] if fold else []
    res = seq(
        functools.partial(attn_bwd, plan, n, find, len(g), m, fold),
        (S((T, D), F32), S((VROWS, D), F32), *g),
        [SMEM] + [LAZY] * (8 + len(others)) + [ANY] * n,
        [LAZY] * 2 + [ANY] * len(g),
        (scal, dx1, x, a1, un, p, o, a2, vec, *others, *pieces),
        [WA, WC, pltpu.VMEM((T, FF), BF), pltpu.VMEM((T, 1024), BF), pltpu.VMEM((T, D), BF), *vblk, pltpu.SemaphoreType.DMA((64,))],
        cost_estimate=cost(weight * 2 * T * D * FF * 8, weight * (2 * WBYTES + 8e6)),
        name="attn_bwd",
        mib=64,
    )
    return res[:2], res[2:]


def shift(n, k):
    return [(i, (i + k) % n) for i in range(n)]


class Ring:
    def __init__(self, dp, fsdp):
        self.X = fsdp // 2
        self.Z = dp // self.X
        self.dp, self.fsdp = dp, fsdp

    def z(self, v, k):
        return lax.ppermute(v, "dp", [(z * self.X + x, (z + k) % self.Z * self.X + x) for z in range(self.Z) for x in range(self.X)])

    def z_xor(self, v, k):
        return lax.ppermute(v, "dp", [(i, i ^ (k * self.X)) for i in range(self.dp)])

    def x(self, v):
        return lax.ppermute(v, "dp", [(i, i ^ 1) for i in range(self.dp)])

    def y(self, v):
        return lax.ppermute(v, "fsdp", [(i, i ^ 2) for i in range(self.fsdp)])

    def c(self, v):
        return lax.ppermute(v, "fsdp", [(i, i ^ 1) for i in range(self.fsdp)])


def pack_a_kernel(l, wqkv, wo, out):
    out[...] = jnp.concatenate([wqkv[l], wo[l]], axis=1)


def pack_a(seq, l, wqkv, wo):
    return seq(
        functools.partial(pack_a_kernel, l),
        [S((96, D), BF)],
        [VMEM] * 2,
        [VMEM],
        (wqkv, wo),
        cost_estimate=cost(0, 4 * 96 * D),
        name="pack_a",
    )[0]


def pack_bc_rows(l, w1, w2, out, first, second):
    t = w2[l]
    for i, at in enumerate((first, second)):
        out[at : at + 48] = w1[l, 48 * i : 48 * i + 48]
        for j in range(2):
            out[at + 48 : at + 96, 384 * j : 384 * j + 384] = t[96 * j + 48 * i : 96 * j + 48 * i + 48]


def pack_bc_kernel(l, w1, w2, out):
    pack_bc_rows(l, w1, w2, out, 0, 96)


def pack_bc(seq, l, w1, w2):
    return seq(
        functools.partial(pack_bc_kernel, l),
        [S((192, D), BF)],
        [VMEM] * 2,
        [VMEM],
        (w1, w2),
        cost_estimate=cost(0, 4 * 192 * D),
        name="pack_bc",
    )[0]


def pack_ab_kernel(l, wqkv, wo, w1, ng, bi, hg, hb, out):
    def column(v, u, w, first):
        v = jnp.concatenate([v.astype(F32), u.astype(F32)], axis=0)
        parts = [jnp.zeros((first, w), F32)] if first else []
        return jnp.concatenate(parts + [v, jnp.zeros((VROWS - first - v.shape[0], w), F32)], axis=0)

    a = jnp.concatenate([wqkv[l], wo[l]], axis=1)
    for i in range(2):
        out[112 * i : 112 * i + 48] = a[48 * i : 48 * i + 48]
        out[112 * i + 48 : 112 * i + 96] = w1[l, 48 * i : 48 * i + 48]
    low = [column(ng[i], bi[i], 96, 0) for i in range(LAYERS)]
    hid = [column(hg[i], hb[i], 384, HROW) for i in range(LAYERS)]
    low = jnp.concatenate(low + [jnp.zeros((VROWS, 576), F32)], axis=1)
    out[96:112] = (low + jnp.concatenate(hid, axis=1)).astype(BF)
    out[208:224] = jnp.zeros((VROWS, D), BF)


def pack_ab(seq, l, weights, vectors):
    return seq(
        functools.partial(pack_ab_kernel, l),
        [S((224, D), BF)],
        [VMEM] * 7,
        [VMEM],
        (*weights, *vectors),
        cost_estimate=cost(0, 4 * 224 * D),
        name="pack_ab",
    )[0]


def pack_c_kernel(l, w2, o1, o2):
    t = w2[l]
    for i, out in enumerate((o1, o2)):
        for j in range(2):
            out[:, 384 * j : 384 * j + 384] = t[96 * j + 48 * i : 96 * j + 48 * i + 48]


def pack_c(seq, l, w2):
    return seq(
        functools.partial(pack_c_kernel, l),
        [S((48, D), BF)] * 2,
        [VMEM],
        [VMEM] * 2,
        (w2,),
        cost_estimate=cost(0, 4 * 96 * D),
        name="pack_c",
    )


Q_CUTS = ((0, 2), (2, 1), (3, 1))


def zquad_kernel(scal, *refs):
    high = scal[2] // 2
    out = refs[-1]
    first = 0
    for k in range(0, len(refs) - 1, 2):
        rows = refs[k].shape[1]
        for part, pos in ((refs[k], high), (refs[k + 1], 1 - high)):
            for i in range(2):
                for r in range(rows):
                    for ri in range(2):
                        out[first + r, ri, 2 * pos + i] = part[i, r, ri]
        first += rows


def zquad(seq, scal, *parts):
    return seq(
        zquad_kernel,
        [S((4, 2, 4, 48, D), BF)],
        [SMEM] + [VMEM] * len(parts),
        [VMEM],
        (scal, *parts),
        cost_estimate=cost(0, 64 * 48 * D),
        name="zquad",
        mib=64,
    )[0]


def zcat_kernel(r1, scal, *refs):
    n = (len(refs) - 2) if len(refs) == 6 else (len(refs) - 3)
    o1, o2 = refs[n : n + 2]
    for k, ref in enumerate(refs[:4]):
        z = lax.rem(scal[2] + 4 - k, 4)
        o1[z] = ref[0:r1]
        o2[z] = ref[r1:]
    for i, ref in enumerate(refs[4:n]):
        refs[-1][i] = ref[...]


def zcat(seq, scal, parts, r1, *riders):
    r2 = parts[0].shape[0] - r1
    outs = [S((4, r1, D), BF), S((4, r2, D), BF)]
    if riders:
        outs.append(S((len(riders), *riders[0].shape), BF))
    return seq(
        functools.partial(zcat_kernel, r1),
        outs,
        [SMEM] + [VMEM] * (4 + len(riders)),
        [VMEM] * len(outs),
        (scal, *parts, *riders),
        cost_estimate=cost(0, 8 * (r1 + r2) * D * 2),
        name="zcat",
    )


def pile_kernel(cuts, h1, x1, h2, y2, *outs):
    for i, (first, rows) in enumerate(cuts):
        mine = pl.ds(first, rows)
        for j, parts in enumerate(((h1, x1), (h2, y2))):
            for k, part in enumerate(parts):
                outs[2 * i + j][k] = part[:, mine]
                if len(outs) > 2 * len(cuts):
                    outs[-1][j, k] = part[:, mine]


def pile(seq, parts, cuts, again=False):
    outs = [S((2, 4, rows, D), BF) for _, rows in cuts for _ in range(2)]
    if again:
        outs.append(S((2, *outs[0].shape), BF))
    return seq(
        functools.partial(pile_kernel, cuts),
        outs,
        [VMEM] * 4,
        [VMEM] * len(outs),
        parts,
        cost_estimate=cost(0, 64 * sum(rows for _, rows in cuts) * D),
        name="pile",
    )


def pile_last_kernel(cuts, scal, h1, x1, h2, y2, q, q_got, *refs):
    n = 2 * len(cuts)
    pile_kernel(cuts, h1, x1, h2, y2, *refs[:n])
    low = lax.rem(scal[2], 2)
    for (first, rows), out in zip(Q_CUTS, refs[n:]):
        out[low] = q[first : first + rows]
        out[1 - low] = q_got[first : first + rows]
    vecs, hids, biases = refs[-3:]
    own = lax.convert_element_type(scal[3] == 0, F32)
    for l in range(LAYERS):
        low, high = [], []
        for z in range(4):
            mine, other = h1[z, 96:112].astype(F32), x1[z, 96:112].astype(F32)
            for rows in (own * mine + (1 - own) * other, own * other + (1 - own) * mine):
                low.append(rows[:, 96 * l : 96 * l + 96])
                high.append(rows[:, 384 * l : 384 * l + 384])
        vec = jnp.concatenate(low, axis=1)
        vecs[l] = vec
        hids[l] = jnp.concatenate(high, axis=1)
        bias = jnp.concatenate([vec[BQ : BQ + 1], jnp.zeros((1, D), F32), vec[BV : BV + 1]], axis=1)
        parts = [bias[:, 576 * f : 576 * f + 512] for f in range(4)]
        for f in range(4):
            parts += [bias[:, 576 * f + 512 : 576 * f + 576], jnp.zeros((1, 64), F32)]
        biases[l] = jnp.concatenate(parts, axis=1)


def pile_last(seq, scal, parts, cuts, q, q_got):
    outs = [S((2, 4, rows, D), BF) for _, rows in cuts for _ in range(2)]
    outs += [S((2, rows, *q.shape[1:]), BF) for _, rows in Q_CUTS]
    outs += [S((LAYERS, VROWS, D), F32), S((LAYERS, VROWS, FF), F32), S((LAYERS, 1, 2560), F32)]
    res = seq(
        functools.partial(pile_last_kernel, cuts),
        outs,
        [SMEM] + [VMEM] * 6,
        [VMEM] * len(outs),
        (scal, *parts, q, q_got),
        cost_estimate=cost(0, 64 * sum(rows for _, rows in cuts) * D),
        name="pile_last",
    )
    n = 2 * len(cuts)
    return res[:n], res[n : n + 3], *([(v, l) for l in range(LAYERS)] for v in res[n + 3 :])


def merge_kernel(*refs):
    for i, ref in enumerate(refs[:-1]):
        refs[-1][i] = ref[...]


def merge(seq, *parts):
    shape = (len(parts), *parts[0].shape)
    return seq(merge_kernel, [S(shape, BF)], [VMEM] * len(parts), [VMEM], parts, cost_estimate=cost(0, 4 * math.prod(shape)), name="merge")[0]


def total(refs):
    out = refs[0].astype(F32)
    for r in refs[1:]:
        out = out + r.astype(F32)
    return out


class Sums:
    def __init__(self, scal):
        self.scal = scal
        self.arrays = []
        self.outs = []
        self.sums = []

    def source(self, array):
        for i, v in enumerate(self.arrays):
            if v is array:
                return i
        self.arrays.append(array)
        return len(self.arrays) - 1

    def out(self, *shape):
        self.outs.append(shape)
        return len(self.outs) - 1

    def add(self, out, where, sources, rows):
        self.sums.append((out, where, [(self.source(v), at, deep) for v, at, deep in sources], rows))

    def run(self, seq, name):
        n, q = len(self.arrays), len(self.outs)
        copies = sum(len(v[2]) for v in self.sums)
        sums = self.sums

        def kernel(scal, *refs):
            arrays, outs = refs[:n], refs[n : n + q]
            ins, made, sems = refs[n + q : n + q + copies], refs[n + q + copies : -1], refs[-1]
            pairs = [(arrays[i].at[at(scal)], ins[j]) for j, (i, at, _) in enumerate(v for t in sums for v in t[2])]
            loads = start(pairs, sems)
            saves, first = [], 0
            for t, (out, where, sources, rows) in enumerate(sums):
                mine = range(first, first + len(sources))
                first += len(sources)
                wait([loads[j] for j in mine])
                made[t][...] = total([ins[j][...].reshape(rows, D) for j in mine]).astype(BF)
                saves += start([(made[t], outs[out].at[where(scal)])], sems, copies + t)
            wait(saves)

        scratch = [pltpu.VMEM((4, t[3] // 4, D) if deep else (t[3], D), BF) for t in sums for _, _, deep in t[2]]
        scratch += [pltpu.VMEM((t[3], D), BF) for t in sums]
        return seq(
            kernel,
            [S((*v, D), BF) for v in self.outs],
            [SMEM] + [ANY] * n,
            [ANY] * q,
            (self.scal, *self.arrays),
            scratch + [pltpu.SemaphoreType.DMA((copies + len(sums),))],
            cost_estimate=cost(0, 2 * D * sum(t[3] * (1 + len(t[2])) for t in sums)),
            name=name,
            mib=64,
        )


def finish_kernel(scal, *refs):
    in_out, out_out, up_out, down_out, gain_out, bias_out, hgain_out, hbias_out = refs[17:]
    i = lax.rem(scal[2], 2)
    c1 = total([refs[0][i], refs[1][i], refs[4][0:96]])
    c0 = total([refs[2][i], refs[3][i], refs[4][96:192]])
    ba1, b0, rows_a = (total([r[...] for r in refs[k : k + 4]]) for k in (5, 9, 13))
    for l in range(LAYERS):
        for r in range(3):
            gain_out[r, l : l + 1] = rows_a[48 + r : 49 + r, 96 * l : 96 * l + 96]
        for r in range(7):
            bias_out[r, l : l + 1] = rows_a[51 + r : 52 + r, 96 * l : 96 * l + 96]
        hid = rows_a[112 + HROW : 115 + HROW, 384 * l : 384 * l + 384]
        hgain_out[0, l : l + 1] = hid[0:1]
        hbias_out[0, l : l + 1] = hid[1:2]
        hbias_out[1, l : l + 1] = hid[2:3]
    a0 = jnp.concatenate([rows_a[:48], rows_a[64:112]], axis=0)
    for l, a, b, c in ((0, a0, b0, c0), (1, ba1[96:], ba1[:96], c1)):
        in_out[l] = a[:, :576]
        out_out[l] = a[:, 576:]
        up_out[l] = b
        for j in range(2):
            down_out[l, 96 * j : 96 * j + 96] = c[:, 384 * j : 384 * j + 384]


def finish(seq, scal, parts):
    return seq(
        finish_kernel,
        [S((2, 96, 576), F32), S((2, 96, 192), F32), S((2, 96, D), F32), S((2, 192, 384), F32), S((3, 2, 96), F32), S((7, 2, 96), F32), S((1, 2, 384), F32), S((2, 2, 384), F32)],
        [SMEM] + [VMEM] * len(parts),
        [VMEM] * 8,
        (scal, *parts),
        cost_estimate=cost(0, 8e6),
        name="finish",
        mib=64,
    )


def head_kernel(scal, p0, p1, p2, p3, q1, q2, xo, yo):
    for k, ref in enumerate((p0, p1, p2, p3)):
        at = pl.ds(pl.multiple_of(lax.rem(scal[2] + 4 - k, 4) * 48, 48), 48)
        xo[at] = ref[0:48]
        yo[at] = ref[48:96]
    xo[192:240] = q1[...]
    yo[192:240] = q2[...]


def head_second_kernel(xo, x1, yo, y2, yo2, xo2):
    for out, own, got in ((yo2, xo, x1), (xo2, yo, y2)):
        out[0:192] = own[0:192]
        out[192:384] = got[0:192]
        out[384:432] = own[192:240]
        out[432:480] = got[192:240]


def head_merge_kernel(h1, y1, h2, x2, out, q):
    for i, ref in enumerate((h1, y1, h2, x2)):
        for j in range(2):
            for z in range(4):
                at = 192 * j + 48 * z
                out[i, j, z] = ref[at : at + 48]
            q[i, j] = ref[384 + 48 * j : 432 + 48 * j]


class Gather:
    def __init__(self, seq, ring, scal):
        self.seq, self.ring, self.scal = seq, ring, scal

    def z_all(self, pack):
        self.parts = [pack] + [self.ring.z(pack, k) for k in (1, 2, 3)]

    def xy_first(self, *riders):
        h1, h2, *rest = zcat(self.seq, self.scal, self.parts, self.parts[0].shape[0] // 2, *riders)
        self.both = h1, self.ring.x(h1), h2, self.ring.y(h2)
        return rest[0] if riders else None

    def xy_second(self, h1, h2):
        self.h1, self.h2 = h1, h2
        self.y1, self.x2 = self.ring.y(self.h1), self.ring.x(self.h2)

    def core(self):
        both = self.ring.c(merge(self.seq, self.h1, self.y1, self.h2, self.x2))
        self.other = [(both, i) for i in range(4)]
        return both

    def pieces(self):
        return [self.h1, self.y1, *self.other[:2], self.h2, self.x2, *self.other[2:]]


def rows_at(first, rows):
    return lambda scal: (pl.ds(first, rows),)


class Scatter:
    def __init__(self, ring, grads):
        self.ring = ring
        self.keep, *self.send = grads
        self.rows = self.keep.shape[4]

    def core(self, *send):
        self.got = [self.ring.c(v) for v in send]
        return self.got

    def pair(self, index):
        if len(self.got) == 1:
            return [(v, index) for v in (self.keep, self.got[0])]
        return [(self.keep, index), (self.got[index(None)[0]], lambda scal: index(scal)[1:])]

    def both(self, *index):
        return [(v, at, True) for v, at in self.pair(lambda scal: index)]

    def first(self, sums, x, y, at=0):
        self.at1 = at
        r = 4 * self.rows
        for h, out in ((0, x), (1, y)):
            for s in range(2):
                sums.add(out, rows_at(at + s * r, r), self.both(h, 1, s), r)

    def second(self, sums, x, y, at=0):
        self.at2 = at
        r = 4 * self.rows
        for h, got, out in ((0, self.x1st, y), (1, self.y1st, x)):
            sums.add(out, rows_at(at, r), self.both(h, 0, 1) + [(got, rows_at(self.at1 + r, r), False)], r)

    def block(self, sums, out, where, z):
        n = self.rows
        for h, a, b in ((0, self.x1st, self.y2nd), (1, self.y1st, self.x2nd)):

            def local(scal, h=h):
                return (h, 0, 0, 0 if scal is None else z(scal))

            def sent(first):
                return lambda scal: (pl.ds(pl.multiple_of(first + z(scal) * n, 16), n),)

            sources = [(v, at, False) for v, at in self.pair(local)]
            sources += [(a, sent(self.at1), False), (b, sent(self.at2), False)]
            sums.add(out, where(h * n, n), sources, n)


def third_pair(sums, *chunks):
    outs = [sums.out(2, sum(2 * c.rows for c in chunks)) for _ in range(2)]
    for k in (1, 0):
        for i in range(2):

            def z(scal, k=k, i=i):
                high = scal[2] // 2
                return 2 * (1 - high if k else high) + i

            at = 0
            for c in chunks:
                c.block(sums, outs[k], lambda first, n, i=i, at=at: lambda scal: (i, pl.ds(at + first, n)), z)
                at += 2 * c.rows
    return outs


def third_direct(sums, *chunks):
    outs = [sums.out(sum(2 * c.rows for c in chunks)) for _ in range(4)]
    for k in (1, 2, 3, 0):
        at = 0
        for c in chunks:
            c.block(sums, outs[k], lambda first, n, at=at: rows_at(at + first, n), lambda scal, k=k: lax.rem(scal[2] + k, 4))
            at += 2 * c.rows
    return outs


def fourth(sums, out, at, keep, got):
    rows = keep.shape[1]
    where = lambda scal: (1 - lax.rem(scal[2], 2),)
    sums.add(out, rows_at(at, rows), [(keep, where, False), (got, where, False)], rows)


def proj_bias(vec):
    full = jnp.concatenate([vec[BQ], jnp.zeros((D,), F32), vec[BV]]).reshape(4, 9 * HD)
    return jnp.concatenate(
        [full[:, :512].reshape(2048), jnp.pad(full[:, 512:], ((0, 0), (0, 64))).reshape(512)]
    ).reshape(1, 2560)


def fast_shards(ring, inputs, lengths, in_projection, out_projection, up_weight, down_weight, norm_gains, biases, hidden_gains, hidden_biases, cotangent):
    plan = Plan(True)
    seq = Seq(True)
    dpi, fi = lax.axis_index("dp"), lax.axis_index("fsdp")
    xme = dpi % ring.X
    place = jnp.stack([dpi // ring.X, xme, fi // 2, fi % 2]).astype(jnp.int32)
    scal = jnp.concatenate([lengths[0], place, jnp.zeros((2,), jnp.int32)])

    down_weight = down_weight.transpose(0, 2, 1)

    a, b, c, d = (Gather(seq, ring, scal) for _ in range(4))
    a.z_all(pack_a(seq, 0, in_projection, out_projection))
    q1, q2 = pack_c(seq, 1, down_weight)
    two = S((240, D), BF)
    xo, yo = seq(head_kernel, [two] * 2, [SMEM] + [VMEM] * 6, [VMEM] * 2, (scal, *a.parts, q1, q2), cost_estimate=cost(0, 2e6), name="head")
    x1, y2 = ring.x(xo), ring.y(yo)
    b.z_all(pack_bc(seq, 0, up_weight, down_weight))
    cd = pack_ab(seq, 1, (in_projection, out_projection, up_weight), (norm_gains, biases, hidden_gains, hidden_biases))
    seq.hold(b.parts[1])
    two = S((480, D), BF)
    h1, h2 = seq(head_second_kernel, [two] * 2, [VMEM] * 4, [VMEM] * 2, (xo, x1, yo, y2), cost_estimate=cost(0, 2e6), name="head_second")
    y1, x2 = ring.y(h1), ring.x(h2)
    seq.hold(y1, x2)
    b.xy_first()
    c.z_all(cd)
    shapes = [S((4, 2, 4, 48, D), BF), S((4, 2, 48, D), BF)]
    own, q = seq(head_merge_kernel, shapes, [VMEM] * 4, [VMEM] * 2, (h1, y1, h2, x2), cost_estimate=cost(0, 5e6), name="head_merge")
    other = ring.c(own)
    pieces_a = [(v, 2 * h + i) for h in range(2) for v in (own, other) for i in range(2)]
    seq.hold(other, c.parts[3])
    *h, own = pile(seq, b.both, ((0, 96),), True)
    b.xy_second(*h)
    b.own = ring.c(own)
    kept = [None, None]
    x = inputs
    seq.hold(b.y1, b.x2, b.own)
    rest = ring.c(c.xy_first(b.y1, b.x2))
    b.other = [(b.own, 0), (rest, 0), (b.own, 1), (rest, 1)]
    seq.hold(rest)
    h, parts_q, vecs, hids, pb = pile_last(seq, scal, c.both, ((0, 48), (48, 48)), q, ring.z_xor(q, 1))
    c.xy_second(*h[:2])
    d.xy_second(*h[2:])
    x1, a1, un, p, o, a2 = call_attn_fwd(seq, plan, scal, x, vecs[0], pb[0], pieces_a, 0, 0.01)
    got_q = [ring.z_xor(v, 2) for v in parts_q]
    x2, a3, sl, n4, a4 = call_ff_fwd(seq, plan, scal, x1, vecs[0], hids[0], b.pieces(), 0, 1, 0.01)
    kept[0] = (x, x1, a1, un, p, o, a2, a3, sl, n4, a4)
    x = x2
    seq.hold(d.y1, d.x2, got_q[0])
    c.core()
    d.core()
    x1, a1, un, p, o, a2 = call_attn_fwd(seq, plan, scal, x, vecs[1], pb[1], c.pieces(), 0)
    (a3, sl, n4, a4), grads = call_ff_mid(seq, plan, scal, x1, cotangent, vecs[1], hids[1], d.pieces(), 0)
    seq.carry(grads[1])
    q = zquad(seq, scal, *(v for pair in zip(parts_q, got_q) for v in pair))
    grads = grads[0], *seq.carried
    q_got = ring.c(q)
    pieces_c = [(v, 2 * h + i) for h in range(2) for v in (q, q_got) for i in range(2)]

    sc = Scatter(ring, grads)
    sc.core(*sc.send)
    sums = Sums(scal)
    sc.first(sums, sums.out(384), sums.out(384))
    u, v = sums.run(seq, "sums_0")
    sc.x1st, sc.y1st = ring.x(u), ring.y(v)

    pieces = d.pieces() + pieces_c
    (dx1, gva1, gh1), grads = call_ff_bwd(seq, plan, scal, cotangent, x1, a3, sl, n4, a4, vecs[1], hids[1], pieces, 0, 0, True, False)
    sb = Scatter(ring, grads)

    sums = Sums(scal)
    sc.second(sums, sums.out(192), sums.out(192))
    seq.carry(*sb.send)
    u, v = sums.run(seq, "sums_1")
    sb.core(*seq.carried)
    sc.x2nd, sc.y2nd = ring.x(u), ring.y(v)

    x1_last, a4_last = x1, a4
    (dy, gvb1), grads = call_attn_bwd(seq, plan, scal, dx1, x, a1, un, p, o, a2, vecs[1], c.pieces(), 0, ())
    sa = Scatter(ring, grads)

    sums = Sums(scal)
    third_pair(sums, sc)
    seq.carry(*sa.send)
    keep_c, send = sums.run(seq, "sums_2a")
    sa.core(*seq.carried)
    got_c = ring.z_xor(send, 2)

    sums = Sums(scal)
    outs = sums.out(784), sums.out(784)
    sb.first(sums, *outs)
    sa.first(sums, *outs, 384)
    u, v = sums.run(seq, "sums_2b")
    sb.x1st, sb.y1st = sa.x1st, sa.y1st = ring.x(u), ring.y(v)

    x, x1, a1, un, p, o, a2, a3, sl, n4, a4 = kept[0]
    s3 = Scatter(ring, call_down_grad(seq, plan, scal, dy, a4))
    s3.core(*s3.send)

    (dx1, gva0, gh0), grads = call_ff_bwd(seq, plan, scal, dy, x1, a3, sl, n4, a4, vecs[0], hids[0], b.pieces(), 0, 1, False, False, 0.01)
    s4 = Scatter(ring, grads)

    sums = Sums(scal)
    outs = sums.out(384), sums.out(384)
    sb.second(sums, *outs)
    sa.second(sums, *outs, 192)
    s3.first(sums, sums.out(384), sums.out(384))
    seq.hold(got_c)
    seq.carry(*s4.send)
    u, v, u3, v3 = sums.run(seq, "sums_3")
    s4.core(*seq.carried)
    sb.x2nd, sb.y2nd = sa.x2nd, sa.y2nd = ring.x(u), ring.y(v)
    s3.x1st, s3.y1st = ring.x(u3), ring.y(v3)

    others = (gva0, gva1, gvb1, gh0, gh1)
    (input_gradient, _), grads = call_attn_bwd(seq, plan, scal, dx1, x, a1, un, p, o, a2, vecs[0], pieces_a, 0, others, 0.01)
    s5 = Scatter(ring, grads)

    sums = Sums(scal)
    third_direct(sums, sb, sa)
    parts_ba = sums.run(seq, "sums_4a")
    parts_ba = [parts_ba[0]] + [ring.z(parts_ba[k], k) for k in (1, 2, 3)]

    sums = Sums(scal)
    outs = sums.out(576), sums.out(576)
    s3.second(sums, *outs)
    s4.first(sums, *outs, 192)
    seq.carry(*s5.send)
    u, v = sums.run(seq, "sums_4b")
    s5.core(*seq.carried)
    s4.x1st, s4.y1st = s3.x2nd, s3.y2nd = ring.x(u), ring.y(v)
    outputs = call_ff_out(seq, plan, scal, x1_last, a4_last, vecs[1], pieces, 0)

    sums = Sums(scal)
    s5.first(sums, sums.out(512), sums.out(512))
    u, v = sums.run(seq, "sums_4c")
    s5.x1st, s5.y1st = ring.x(u), ring.y(v)

    sums = Sums(scal)
    s4.second(sums, sums.out(192), sums.out(192))
    third_pair(sums, s3)
    seq.hold(*parts_ba[1:3])
    u, v, keep_c0, send = sums.run(seq, "sums_5")
    s4.x2nd, s4.y2nd = ring.x(u), ring.y(v)
    got_c0 = ring.z_xor(send, 2)

    sums = Sums(scal)
    s5.second(sums, sums.out(256), sums.out(256))
    third_direct(sums, s4)
    seq.hold(got_c0, parts_ba[3])
    u, v, *res = sums.run(seq, "sums_6")
    s5.x2nd, s5.y2nd = ring.x(u), ring.y(v)
    parts_b0 = [res[0]] + [ring.z(res[k], k) for k in (1, 2, 3)]

    sums = Sums(scal)
    third_direct(sums, s5)
    out = sums.out(192)
    fourth(sums, out, 0, keep_c, got_c)
    fourth(sums, out, 96, keep_c0, got_c0)
    seq.hold(*parts_b0[1:])
    *parts, last = sums.run(seq, "sums_7")
    parts = parts[:1] + [ring.z(parts[k], k) for k in (1, 2, 3)]
    last = ring.z_xor(last, 1)
    grads = finish(seq, scal, [keep_c, got_c, keep_c0, got_c0, last, *parts_ba, *parts_b0, *parts])
    down, *rows = grads[3:]
    return outputs, input_gradient, *grads[:3], down.transpose(0, 2, 1), *(v.transpose(1, 0, 2) for v in rows)


def whole_shards(inputs, lengths, in_projection, out_projection, up_weight, down_weight, norm_gains, biases, hidden_gains, hidden_biases, cotangent):
    plan = Plan(False)
    seq = Seq(False)
    scal = jnp.concatenate([lengths[0], jnp.zeros((6,), jnp.int32)])

    def full(w):
        return lax.all_gather(lax.all_gather(w, "fsdp", axis=1, tiled=True), "dp", axis=0, tiled=True)

    def rows(v, width):
        return jnp.pad(lax.all_gather(v, "dp", axis=1, tiled=True).astype(F32), ((0, VROWS - v.shape[0]), (0, 0)))

    vecs, hids, pieces = [], [], []
    for l in range(LAYERS):
        qkv = full(in_projection[l]).reshape(D, 4, 9 * HD)
        out = full(out_projection[l]).reshape(D, 4, 192)
        a = jnp.concatenate([qkv[:, :, :512].reshape(D, 2048), jnp.concatenate([qkv[:, :, 512:], out], axis=2).reshape(D, 1024)], axis=1)
        b = full(up_weight[l])
        c = full(down_weight[l]).reshape(4, D, D).transpose(0, 2, 1)
        shape = (4, 2, 2, 48, FF)
        got = [a.reshape(shape), b.reshape(shape), c.reshape(4, 4, 2, 2, 48, D)]
        pieces.append(got)
        vecs.append(rows(jnp.concatenate([norm_gains[l], biases[l]], axis=0), D))
        hid = rows(jnp.concatenate([hidden_gains[l], hidden_biases[l]], axis=0), FF)
        hids.append(jnp.roll(hid, HROW, axis=0))
    pb = [proj_bias(v) for v in vecs]
    x = inputs
    kept = []
    for l in range(LAYERS):
        x1, a1, un, p, o, a2 = call_attn_fwd(seq, plan, scal, x, vecs[l], pb[l], pieces[l], 0)
        x2, a3, sl, n4, a4 = call_ff_fwd(seq, plan, scal, x1, vecs[l], hids[l], pieces[l], 0, 0)
        kept.append((x, x1, a1, un, p, o, a2, a3, sl, n4, a4))
        x = x2
    places = jnp.arange(inputs.shape[0], dtype=jnp.int32)[:, None]
    outputs = x * (seg_of(scal, places) < SEQS).astype(F32)
    dy = cotangent
    layer_grads = [None] * LAYERS
    for l in reversed(range(LAYERS)):
        x, x1, a1, un, p, o, a2, a3, sl, n4, a4 = kept[l]
        last = l == LAYERS - 1
        (dx1, gva, gh), (gb, gc) = call_ff_bwd(seq, plan, scal, dy, x1, a3, sl, n4, a4, vecs[l], hids[l], pieces[l], 0, 0, last, True)
        (dy, gvb), (ga,) = call_attn_bwd(seq, plan, scal, dx1, x, a1, un, p, o, a2, vecs[l], pieces[l], 0, ())
        layer_grads[l] = (ga, gb, gc, gva + gvb, gh)

    def scatter(g):
        g = lax.psum_scatter(g.astype(BF), "dp", scatter_dimension=0, tiled=True)
        return lax.psum_scatter(g, "fsdp", scatter_dimension=1, tiled=True).astype(F32)

    def scatter_rows(v):
        v = lax.psum_scatter(v.astype(BF), "dp", scatter_dimension=1, tiled=True).astype(F32)
        return lax.psum(v, "fsdp")

    res = []
    for l in range(LAYERS):
        ga, gb, gc, gv, gh = layer_grads[l]
        ga = ga.reshape(4, D, D).transpose(1, 0, 2)
        gv = scatter_rows(gv[:10])
        gh = scatter_rows(gh[HROW : HROW + 3])
        res.append(
            (
                scatter(ga[:, :, :576].reshape(D, 3 * D)),
                scatter(ga[:, :, 576:].reshape(D, D)),
                scatter(gb.reshape(4, D, D).transpose(1, 0, 2).reshape(D, FF)),
                scatter(gc.reshape(4, D, D).transpose(0, 2, 1).reshape(FF, D)),
                gv[:3],
                gv[3:],
                gh[:1],
                gh[1:],
            )
        )
    return (outputs, dy, *(jnp.stack([r[i] for r in res]) for i in range(8)))


def solution(mesh):
    dp, fsdp = mesh.shape["dp"], mesh.shape["fsdp"]
    both = P(("dp", "fsdp"), None)
    mat = P(None, "dp", "fsdp")
    row = P(None, None, "dp")
    ring = Ring(dp, fsdp)
    shards = functools.partial(fast_shards, ring) if (dp, fsdp) == (8, 4) else whole_shards
    return jax.shard_map(
        shards,
        mesh=mesh,
        in_specs=(both, both, mat, mat, mat, mat, row, row, row, row, both),
        out_specs=(both, both, mat, mat, mat, mat, row, row, row, row),
        check_vma=False,
    )
```
